32 devices in a mesh: dp: 8 (over y, x, core), mp: 4 (over z).
Axes of the slice: x: 2, y: 2, z: 4, core: 2. Of those that a mesh axis runs over, the one named last changes fastest.
Arguments:
- hidden_in: bfloat16 [32768, 768], P(('dp', 'mp')), may hold values from -6 to 6
- cotangent: bfloat16 [32768, 768], P(('dp', 'mp')), may hold values from -6 to 6
- query_lengths: int32 [32, 32], P(('dp', 'mp')), may hold values from 1 to 128, 1024 in all within a row
- passage_index: int32 [1024, 32], P(('dp', 'mp')), may hold values from 0 to 1023
- passages: bfloat16 [1024, 768], replicated, may hold values from -1.1953125 to 1.1953125
- w_query: bfloat16 [768, 768], P(None, 'mp'), may hold values from -0.21875 to 0.21875
- w_key: bfloat16 [768, 768], P(None, 'mp'), may hold values from -0.21875 to 0.21875
- w_value: bfloat16 [768, 768], P(None, 'mp'), may hold values from -0.21875 to 0.21875
- w_output: bfloat16 [768, 768], P('mp'), may hold values from -0.875 to 0.875
- w_up: bfloat16 [768, 3072], P(None, 'mp'), may hold values from -0.21875 to 0.21875
- w_down: bfloat16 [3072, 768], P('mp'), may hold values from -0.109375 to 0.109375
- b_query: bfloat16 [768], P('mp'), may hold values from -1.5 to 1.5
- b_value: bfloat16 [768], P('mp'), may hold values from -1.5 to 1.5
- b_output: bfloat16 [768], replicated, may hold values from -1.5 to 1.5
- b_up: bfloat16 [3072], P('mp'), may hold values from -1.5 to 1.5
- b_down: bfloat16 [768], replicated, may hold values from -1.5 to 1.5
- first_gain: bfloat16 [768], replicated, may hold values from 0.099609375 to 1.8984375
- first_shift: bfloat16 [768], replicated, may hold values from -1.5 to 1.5
- second_gain: bfloat16 [768], replicated, may hold values from 0.099609375 to 1.8984375
- second_shift: bfloat16 [768], replicated, may hold values from -1.5 to 1.5
Outputs:
- output: bfloat16 [32768, 768], P(('dp', 'mp'))
- scores: float32 [1024, 32], P(('dp', 'mp'))
- input_grad: float32 [32768, 768], P(('dp', 'mp'))
- w_query_grad: float32 [768, 768], P(None, 'mp')
- w_key_grad: float32 [768, 768], P(None, 'mp')
- w_value_grad: float32 [768, 768], P(None, 'mp')
- w_output_grad: float32 [768, 768], P('mp')
- w_up_grad: float32 [768, 3072], P(None, 'mp')
- w_down_grad: float32 [3072, 768], P('mp')
- b_query_grad: float32 [768], P('mp')
- b_value_grad: float32 [768], P('mp')
- b_output_grad: float32 [768], replicated
- b_up_grad: float32 [3072], P('mp')
- b_down_grad: float32 [768], replicated
- first_gain_grad: float32 [768], replicated
- first_shift_grad: float32 [768], replicated
- second_gain_grad: float32 [768], replicated
- second_shift_grad: float32 [768], replicated
The draws below stay inside these ranges and needn't reach their ends.
Inputs may be any that keep to these rules, and one draw needn't show every extreme that they name: `query_lengths`: the 32 lengths of each row sum to 1024, and the longest query of every row has exactly 128 tokens.
All inputs are finite; a program needn't handle non-finite values.
Results may differ from the reference program's by a relative error of at most 0.015.
Values may be sent and summed in bfloat16 or wider, within the bound.
No kernel may reach another device: no remote copies, remote signals or barrier semaphores. Data moves between devices by JAX's collectives and lax.ppermute only.
A program may use at most 192 MiB of HBM per device.

```python
import math
import jax
import jax.numpy as jnp
import numpy as np
from jax import lax

D = 768
HEADS = 12
HEAD_DIM = 64
FF = 3072
ROW_LEN = 1024
QROW = 32
LMAX = 128
PASS = 1024
NPICK = 32
NROWS = 32
TOKENS = 32768
QUERIES = 1024
N_MP = 4


def touch_ends(entries, key, smallest, largest):
    longest = entries.shape.index(max(entries.shape))
    spots = []
    for shift in (0, 1):
        where = [jax.random.randint(jax.random.fold_in(key, axis), (), 0, length) for axis, length in enumerate(entries.shape)]
        where[longest] = (where[longest] + shift) % entries.shape[longest]
        spots.append(tuple(where))
    return entries.at[spots[0]].set(smallest).at[spots[1]].set(largest)


def block_scale(stream_key, extent, shards, smallest, high):
    level = 1.0
    for axis_at, blocks in shards:
        heights = jax.random.uniform(jax.random.fold_in(jax.random.fold_in(stream_key, 6), axis_at), (blocks,), jnp.float32, smallest / len(shards), high / len(shards))
        level = level * jnp.repeat(jnp.exp(heights), extent[axis_at] // blocks).reshape((-1,) + (1,) * (len(extent) - 1 - axis_at))
    return level


def profile(count, total, bound, skew):
    loads = [(1 << 20) // math.isqrt(grade ** skew) + 1 for grade in range(2, count + 1)]
    surplus, counts = total - bound - (count - 1), [1] * (count - 1)
    while surplus > 0:
        movable = [i for i in range(count - 1) if counts[i] < bound]
        mass, left = sum([loads[i] for i in movable]), surplus
        for i in movable:
            extra = min(bound - counts[i], max(1, left * loads[i] // mass), surplus)
            counts[i] = counts[i] + extra
            surplus = surplus - extra
    return np.array([bound] + counts)


def uneven_parts(key, amount, total, bound, skew):
    if amount == 2:
        one = jax.random.randint(key, (), max(1, total - bound), min(bound, total - 1) + 1)
        return jnp.stack([one, total - one])
    tallies = jnp.asarray(profile(amount, total, bound, skew), jnp.int32)
    twos = (amount - 1) // 2
    giver, sink = tallies[1:1 + 2 * twos:2], tallies[2:2 + 2 * twos:2]
    margin = jnp.minimum(giver - 1, bound - sink)
    shifted = jax.random.randint(jax.random.fold_in(key, 1), (twos,), 0, 1 << 20) % (margin + 1)
    tallies = tallies.at[1:1 + 2 * twos:2].set(giver - shifted).at[2:2 + 2 * twos:2].set(sink + shifted)
    return tallies[jax.random.permutation(jax.random.fold_in(key, 2), amount)]


def bell_draw(rng, shape, scale, reach, shards=(), held_as=jnp.bfloat16):
    loudness = block_scale(rng, shape, shards, -0.22, 0.18) if shards else 1.0
    entries = jax.random.normal(rng, shape, jnp.float32) * scale * loudness
    return jnp.minimum(jnp.maximum(entries, -reach), reach).astype(held_as)


def setup_inputs(seed: int = 0) -> dict:
    key_list = jax.random.split(jax.random.key(seed), 21)
    return {
        "hidden_in": bell_draw(key_list[0], (TOKENS, D), 1.0, 6.0, ((0, 32),)),
        "cotangent": bell_draw(key_list[1], (TOKENS, D), 1.0, 6.0, ((0, 32),)),
        "query_lengths": jax.vmap(lambda own: uneven_parts(own, QROW, ROW_LEN, LMAX, 2))(jax.random.split(key_list[2], NROWS)).reshape((NROWS, QROW)).astype(jnp.int32),
        "passage_index": touch_ends(jax.random.randint(key_list[3], (QUERIES, NPICK), 0, PASS), jax.random.fold_in(key_list[3], 1), 0, PASS - 1).astype(jnp.int32),
        "passages": bell_draw(key_list[4], (PASS, D), 0.2, 1.1953125),
        "w_query": bell_draw(key_list[5], (D, D), D ** -0.5, 0.21875, ((1, 4),)),
        "w_key": bell_draw(key_list[6], (D, D), D ** -0.5, 0.21875, ((1, 4),)),
        "w_value": bell_draw(key_list[7], (D, D), D ** -0.5, 0.21875, ((1, 4),)),
        "w_output": bell_draw(key_list[8], (D, D), (D // 16) ** -0.5, 0.875, ((0, 4),)),
        "w_up": bell_draw(key_list[9], (D, FF), D ** -0.5, 0.21875, ((1, 4),)),
        "w_down": bell_draw(key_list[10], (FF, D), FF ** -0.5, 0.109375, ((0, 4),)),
        "b_query": bell_draw(key_list[11], (D,), 0.3, 1.5, ((0, 4),)),
        "b_value": bell_draw(key_list[12], (D,), 0.3, 1.5, ((0, 4),)),
        "b_output": bell_draw(key_list[13], (D,), 0.3, 1.5),
        "b_up": bell_draw(key_list[14], (FF,), 0.3, 1.5, ((0, 4),)),
        "b_down": bell_draw(key_list[15], (D,), 0.3, 1.5),
        "first_gain": jnp.clip(1.0 + 0.18 * jax.random.normal(key_list[16], (D,), jnp.float32), 0.099609375, 1.8984375).astype(jnp.bfloat16),
        "first_shift": bell_draw(key_list[17], (D,), 0.3, 1.5),
        "second_gain": jnp.clip(1.0 + 0.18 * jax.random.normal(key_list[18], (D,), jnp.float32), 0.099609375, 1.8984375).astype(jnp.bfloat16),
        "second_shift": bell_draw(key_list[19], (D,), 0.3, 1.5),
    }


@jax.custom_vjp
def low(v):
    return lax.optimization_barrier(v.astype(jnp.bfloat16)).astype(jnp.float32)

@jax.custom_vjp
def low_back(v):
    return v

def low_keep(v):
    return (low(v), None)

def low_pass(kept, grad):
    return (grad,)

def back_keep(v):
    return (v, None)

def back_low(kept, grad):
    return (low(grad),)
low.defvjp(low_keep, low_pass)
low_back.defvjp(back_keep, back_low)
SCALE = 0.125
EPSILON = 1e-12
HIGH = lax.Precision.HIGHEST

def segment_ids(lengths, width):
    ends = jnp.cumsum(lengths, axis=-1, dtype=jnp.int32)
    places = lax.broadcasted_iota(jnp.int32, (lengths.shape[0], width, lengths.shape[1]), 1)
    return lax.optimization_barrier(jnp.sum((places >= ends[:, None, :]).astype(jnp.int32), axis=-1)).astype(jnp.int32)

def normalize(totals, gain, shift):
    mean_val = lax.optimization_barrier(jnp.mean(totals, axis=-1, keepdims=True))
    centred = totals - mean_val
    inv_std = lax.rsqrt(lax.optimization_barrier(jnp.mean(centred * centred, axis=-1, keepdims=True)) + EPSILON)
    return centred * inv_std * gain + shift

def one_row(packed):
    query_heads, key_heads, value_heads, seg_row = packed
    logits = jnp.einsum('ihd,jhd->hij', query_heads, key_heads, precision=HIGH) * SCALE
    logits = low_back(logits)
    allowed = (seg_row[:, None] == seg_row[None, :])[None]
    probs = jax.nn.softmax(jnp.where(allowed, logits, -1e+30), axis=-1)
    return jnp.einsum('hij,jhd->ihd', low(probs), value_heads, precision=HIGH)

def layer(x_in, weights, lengths):
    w_query, w_key, w_value, w_output, w_up, w_down, b_query, b_value, b_output, b_up, b_down, first_gain, first_shift, second_gain, second_shift = weights
    rows = lengths.shape[0]
    seg = segment_ids(lengths, ROW_LEN)
    query_all = low(low_back(jnp.dot(x_in, w_query, precision=HIGH) + b_query))
    key_all = low(low_back(jnp.dot(x_in, w_key, precision=HIGH)))
    value_all = low(low_back(jnp.dot(x_in, w_value, precision=HIGH) + b_value))
    shape_heads = (rows, ROW_LEN, HEADS, HEAD_DIM)
    context = lax.map(jax.checkpoint(one_row), (query_all.reshape(shape_heads), key_all.reshape(shape_heads), value_all.reshape(shape_heads), seg))
    context = low(low_back(context.reshape(rows * ROW_LEN, D)))
    attended = low_back(jnp.dot(context, w_output, precision=HIGH) + b_output)
    first_norm = normalize(x_in + attended, first_gain, first_shift)
    up_pre = low_back(jnp.dot(low(first_norm), w_up, precision=HIGH) + b_up)
    hidden_act = low(jax.nn.gelu(up_pre, approximate=False))
    down_out = low_back(jnp.dot(hidden_act, w_down, precision=HIGH) + b_down)
    return normalize(first_norm + down_out, second_gain, second_shift)

def score(out_block, lengths, picks, table):
    rows = lengths.shape[0]
    seg = segment_ids(lengths, ROW_LEN)
    labels = lax.broadcasted_iota(jnp.int32, (1, QROW, 1), 1)
    onehot = (seg[:, None, :] == labels).astype(jnp.float32)
    sums = jnp.einsum('rql,rld->rqd', onehot, out_block.reshape(rows, ROW_LEN, D), precision=HIGH)
    means = (sums / lengths[..., None].astype(jnp.float32)).reshape(rows * QROW, D)
    return jnp.einsum('qd,qpd->qp', means, table[picks], precision=HIGH)

def reference(hidden_in, cotangent, query_lengths, passage_index, passages, w_query, w_key, w_value, w_output, w_up, w_down, b_query, b_value, b_output, b_up, b_down, first_gain, first_shift, second_gain, second_shift):
    params = tuple((item.astype(jnp.float32) for item in (w_query, w_key, w_value, w_output, w_up, w_down, b_query, b_value, b_output, b_up, b_down, first_gain, first_shift, second_gain, second_shift)))
    groups = NROWS // N_MP
    inputs = hidden_in.astype(jnp.float32).reshape(groups, N_MP * ROW_LEN, D)
    cots = cotangent.astype(jnp.float32).reshape(groups, N_MP * ROW_LEN, D)
    lens = query_lengths.reshape(groups, N_MP, QROW)
    picks = passage_index.reshape(groups, N_MP * QROW, NPICK)
    table = passages.astype(jnp.float32)

    def step(totals, batch):
        x_block, cot_block, len_block, pick_block = batch

        def forward(x_in, weights):
            out_val = layer(x_in, weights, len_block)
            return (out_val, score(out_val, len_block, pick_block, table))
        out_block, back_fn, scored = jax.vjp(forward, x_block, params, has_aux=True)
        x_grad, weight_grads = back_fn(cot_block)
        totals = jax.tree.map(jnp.add, totals, weight_grads)
        return (totals, (out_block.astype(jnp.bfloat16), scored, x_grad))
    zeros = jax.tree.map(jnp.zeros_like, params)
    grads, (outs, scored, x_grads) = lax.scan(step, zeros, (inputs, cots, lens, picks))
    return (outs.reshape(TOKENS, D), scored.reshape(QUERIES, NPICK), x_grads.reshape(TOKENS, D), grads[0], grads[1], grads[2], grads[3], grads[4], grads[5], grads[6], grads[7], grads[8], grads[9], grads[10], grads[11], grads[12], grads[13], grads[14])
```

```python
import functools

import jax
import jax.numpy as jnp
from jax import lax
from jax.experimental import pallas as pl
from jax.experimental.pallas import tpu as pltpu
from jax.sharding import PartitionSpec as P

HEAD_DIM = 64
SCALE = 0.125
EPSILON = 1e-12
MASKED = -1e30
BLOCK = 128
WINDOW = 384
GROUP = 4 * HEAD_DIM
ROW_BLOCK = 256
GRAIN = 16
MEBI = 1024 * 1024
NT = (((1,), (1,)), ((), ()))
TN = (((0,), (0,)), ((), ()))
BF = jnp.bfloat16
F32 = jnp.float32

CORE, XBIT, YBIT = 1, 2, 4


def params(mebi=48):
    return pltpu.CompilerParams(vmem_limit_bytes=mebi * MEBI)


def cost(us):
    return pl.CostEstimate(flops=int(us * 1e9), bytes_accessed=int(us * 3e6), transcendentals=0)


def shape(dims, dtype):
    return jax.ShapeDtypeStruct(dims, dtype)


def scalar_spec():
    return pl.BlockSpec(memory_space=pltpu.SMEM)


def held_spec():
    return pl.BlockSpec(memory_space=pltpu.VMEM)


def whole_spec(dims):
    return pl.BlockSpec(dims, lambda i: (0,) * len(dims), pipeline_mode=pl.Buffered(1))


def fixed_spec(dims):
    return pl.BlockSpec(dims, lambda i: (0,) * len(dims))


def rows_spec(rows, width):
    return pl.BlockSpec((rows, width), lambda i: (i, 0))


def token_spec():
    return pl.BlockSpec(memory_space=pl.ANY)


def swap(block, axis, bit, size):
    return lax.ppermute(block, axis, [(i, i ^ bit) for i in range(size)])


def after(value, *others):
    return lax.optimization_barrier((value, *others))[0]


def piece_heads_kernel(place, wq, wk, wv, wo, piece):
    core, plane = place[0], place[1]
    heads = piece.shape[1]
    for side, pair in enumerate(((wq, wk), (wv, wo))):

        @pl.when(core == side)
        def _():
            for t, ref in enumerate(pair):
                for h in range(heads):
                    start = pl.multiple_of(h * HEAD_DIM + plane * GRAIN, GRAIN)
                    piece[t, h] = ref[pl.ds(start, GRAIN), :]


def piece_heads(place, *weights):
    local, width = weights[0].shape
    heads = local // HEAD_DIM
    return pl.pallas_call(
        piece_heads_kernel,
        in_specs=[scalar_spec()] + [held_spec()] * 4,
        out_specs=held_spec(),
        out_shape=shape((2, heads, GRAIN, width), BF),
        compiler_params=params(16),
        cost_estimate=cost(1),
        name="piece_heads",
    )(place, *weights).reshape(2 * heads * GRAIN, width)


def piece_feed_kernel(place, wu, wd, turned, piece_up, piece_down):
    core, plane = place[0], place[1]
    sub = piece_up.shape[0]
    turned[...] = wu[...].astype(F32).T.astype(BF)
    start = pl.multiple_of((core * 4 + plane) * sub, GRAIN)
    piece_up[...] = turned[pl.ds(start, sub), :]
    piece_down[...] = wd[pl.ds(start, sub), :]


def piece_feed(place, wu, wd):
    width, hidden = wu.shape
    sub = hidden // 8
    return pl.pallas_call(
        piece_feed_kernel,
        in_specs=[scalar_spec()] + [held_spec()] * 2,
        out_specs=[held_spec()] * 3,
        out_shape=[shape((hidden, width), BF), shape((sub, width), BF), shape((sub, width), BF)],
        compiler_params=params(16),
        cost_estimate=cost(3),
        name="piece_feed",
    )(place, wu, wd)


def finish_feed_kernel(turn, place, *refs):
    core, plane = place[0], place[1]
    out = refs[10]
    into = refs[11] if turn else out
    sub = refs[0].shape[0]
    half = sub // 2
    for c in range(2):
        a, x, y, first, second = refs[5 * c : 5 * c + 5]
        for g, ref in enumerate((a, x, y)):
            start = pl.multiple_of(((core ^ c) * 4 + (plane ^ g)) * sub, GRAIN)
            into[pl.ds(start, sub), :] = ref[...].astype(F32)
        start = pl.multiple_of(((core ^ c) * 4 + (plane ^ 3)) * sub, GRAIN)
        into[pl.ds(start, half), :] = first[...].astype(F32)
        start = pl.multiple_of(((core ^ c) * 4 + (plane ^ 3)) * sub + half, GRAIN)
        into[pl.ds(start, half), :] = second[...].astype(F32)
    if turn:
        out[...] = into[...].T


def finish_feed(place, pieces, turn):
    sub, width = pieces[0].shape
    out = (width, 8 * sub) if turn else (8 * sub, width)
    return pl.pallas_call(
        functools.partial(finish_feed_kernel, turn),
        in_specs=[scalar_spec()] + [held_spec()] * 10,
        out_specs=held_spec(),
        out_shape=shape(out, F32),
        scratch_shapes=[pltpu.VMEM((8 * sub, width), F32)] if turn else [],
        compiler_params=params(24),
        cost_estimate=cost(3),
        name="finish_up" if turn else "finish_down",
    )(place, *pieces)


def finish_heads_kernel(place, *refs):
    core, plane = place[0], place[1]
    pieces, outs = refs[:10], refs[10:]
    heads = outs[0].shape[0] // HEAD_DIM
    half = heads * GRAIN
    for side in range(2):

        @pl.when(core == side)
        def _():
            for c in range(2):
                a, x, y, first, second = pieces[5 * c : 5 * c + 5]
                for t in range(2):
                    out = outs[2 * (side ^ c) + t]
                    for g, ref in enumerate((a, x, y, (first, second)[t])):
                        base = 0 if g == 3 else t * half
                        for h in range(heads):
                            at = pl.multiple_of(h * HEAD_DIM + (plane ^ g) * GRAIN, GRAIN)
                            rows = slice(base + h * GRAIN, base + (h + 1) * GRAIN)
                            out[pl.ds(at, GRAIN), :] = ref[rows, :].astype(F32)


def finish_heads(place, pieces):
    rows, width = pieces[0].shape
    local = rows // (2 * GRAIN) * HEAD_DIM
    return pl.pallas_call(
        finish_heads_kernel,
        in_specs=[scalar_spec()] + [held_spec()] * 10,
        out_specs=[held_spec()] * 4,
        out_shape=[shape((local, width), F32)] * 4,
        compiler_params=params(24),
        cost_estimate=cost(2),
        name="finish_heads",
    )(place, *pieces)


def plane_step(piece, n_dp):
    by_x = swap(piece, "dp", XBIT, n_dp)
    by_y = swap(piece, "dp", YBIT, n_dp)
    return by_x, by_y


def corner_step(by_x, by_y, n_dp):
    half = by_x.shape[0] // 2
    return swap(by_x[:half], "dp", YBIT, n_dp), swap(by_y[half:], "dp", XBIT, n_dp)


def core_step(pieces, n_dp):
    return [swap(p, "dp", CORE, n_dp) for p in pieces]


def shard_step(piece, n_mp):
    return jnp.concatenate([swap(piece, "mp", r, n_mp) for r in range(1, n_mp)], axis=0)


def add(*terms):
    total = terms[0].astype(F32)
    for term in terms[1:]:
        total = total + term.astype(F32)
    return total.astype(BF)


def chip_sum(keep, send, n_dp):
    got = swap(send, "dp", CORE, n_dp)
    half = keep.shape[1] // 2
    first, second = slice(0, half), slice(half, None)
    return (
        add(keep[0::2, first], got[0::2, first]),
        add(keep[1::2, first], got[1::2, first]),
        add(keep[0:2, second], got[0:2, second]),
        add(keep[2:4, second], got[2:4, second]),
    )


def plane_sum(parts, n_dp):
    keep_x, send_x, keep_y, send_y = parts
    got_x = swap(send_x, "dp", XBIT, n_dp)
    got_y = swap(send_y, "dp", YBIT, n_dp)
    return (
        add(keep_x[0], got_x[0]),
        add(keep_x[1], got_x[1]),
        add(keep_y[0], got_y[0]),
        add(keep_y[1], got_y[1]),
    )


def corner_sum(parts, n_dp):
    keep_first, send_first, keep_second, send_second = parts
    got_first = swap(send_first, "dp", YBIT, n_dp)
    got_second = swap(send_second, "dp", XBIT, n_dp)
    half = keep_first.shape[0]
    return [add(keep_first[i], got_first[i]) for i in range(half)] + [
        add(keep_second[i], got_second[i]) for i in range(half)
    ]


def shard_sum(parts, n_dp, n_mp):
    total = parts[0].astype(F32)
    for r in range(1, n_mp):
        total = total + swap(parts[r], "mp", r, n_mp).astype(F32)
    bit = 8
    while bit < n_dp:
        total = total + swap(total, "dp", bit, n_dp)
        bit *= 2
    return total.astype(BF)


def gather_sum(total, n_dp):
    by_x, by_y = plane_step(total, n_dp)
    mine = [total, by_x, by_y, *corner_step(by_x, by_y, n_dp)]
    return mine + core_step(mine, n_dp)


def project_kernel(place, x, wq, wk, wv, wo, bq, bv, *refs):
    pieces, (q, k, v, full) = refs[:10], refs[10:]
    core, plane = place[0], place[1]
    heads = wq.shape[0] // HEAD_DIM
    shards = 1 + pieces[0].shape[0] // (2 * heads * GRAIN)

    @pl.when(pl.program_id(0) == 0)
    def _():
        for kind, ref in enumerate((wq, wk, wv, wo)):
            for h in range(heads):
                for g in range(4):
                    at = pl.multiple_of(h * HEAD_DIM + (plane ^ g) * GRAIN, GRAIN)
                    to = h * HEAD_DIM + g * GRAIN
                    full[kind, to : to + GRAIN, :] = ref[pl.ds(at, GRAIN), :]
        for c in range(2):
            a, x_, y_, first, second = pieces[5 * c : 5 * c + 5]
            half = first.shape[0]
            for r in range(1, shards):
                for t in range(2):
                    for h in range(heads):
                        at = ((r - 1) * 2 + t) * heads * GRAIN + h * GRAIN
                        to = (r * heads + h) * HEAD_DIM
                        for g, ref in enumerate((a, x_, y_, first if at < half else second)):
                            row = at - half if g == 3 and at >= half else at
                            full[
                                (core ^ c) * 2 + t, to + g * GRAIN : to + (g + 1) * GRAIN, :
                            ] = ref[row : row + GRAIN, :]

    block = x[...]
    for kind, (out, bias) in enumerate(((q, bq), (k, None), (v, bv))):
        value = lax.dot_general(block, full[kind], NT, preferred_element_type=F32)
        if bias is not None:
            value = value + bias[...]
        out[...] = value.astype(BF)


def project(place, x, weights, bq, bv, pieces):
    rows, width = x.shape
    block = rows_spec(ROW_BLOCK, width)
    return pl.pallas_call(
        project_kernel,
        grid=(rows // ROW_BLOCK,),
        in_specs=[scalar_spec(), block]
        + [whole_spec(a.shape) for a in (*weights, bq, bv, *pieces)],
        out_specs=[block, block, block, fixed_spec((4, width, width))],
        out_shape=[shape((rows, width), BF)] * 3 + [shape((4, width, width), BF)],
        compiler_params=params(),
        cost_estimate=cost(7),
        name="project",
    )(place, x, *weights, bq, bv, *pieces)


def spread_heads(block):
    lane = lax.broadcasted_iota(jnp.int32, block.shape, 1) // HEAD_DIM
    return jnp.concatenate(
        [jnp.where(lane == h, block, jnp.zeros_like(block)) for h in range(4)], axis=0
    )


def gather_heads(stacked):
    rows = stacked.shape[0] // 4
    lane = lax.broadcasted_iota(jnp.int32, (rows, GROUP), 1) // HEAD_DIM
    out = stacked[:rows]
    for h in range(1, 4):
        out = jnp.where(lane == h, stacked[h * rows : (h + 1) * rows], out)
    return out


def window_start(step, rows):
    return pl.multiple_of(jnp.clip(step - 1, 0, (rows - WINDOW) // BLOCK) * BLOCK, BLOCK)


def attend_kernel(
    q, k, v, segc, segr, x, wo, bo, gain, shift, ctx, saved, unit, low
):
    start = window_start(pl.program_id(0), k.shape[0])
    near = pl.ds(start, WINDOW)
    penalty = jnp.where(segc[...] == segr[:, near], 0.0, MASKED)
    lane = lax.broadcasted_iota(jnp.int32, (BLOCK, 128), 1)
    keep = jnp.zeros((BLOCK, 128), F32)
    for group in range(q.shape[1] // GROUP):
        cols = slice(group * GROUP, (group + 1) * GROUP)
        stacked = spread_heads(q[:, cols] * SCALE)
        logits = lax.dot_general(stacked, k[near, cols], NT, preferred_element_type=F32)
        logits = logits.reshape(4, BLOCK, WINDOW) + penalty[None]
        peak = jnp.max(logits, axis=-1, keepdims=True)
        raised = jnp.exp(logits - peak)
        sums = jnp.sum(raised, axis=-1, keepdims=True)
        probs = (raised * (1.0 / sums)).astype(BF).reshape(4 * BLOCK, WINDOW)
        context = jnp.dot(probs, v[near, cols], preferred_element_type=F32)
        ctx[:, cols] = gather_heads(context).astype(BF)
        log_total = peak + jnp.log(sums)
        for h in range(4):
            keep = jnp.where(lane == group * 4 + h, log_total[h], keep)
    attended = jnp.dot(ctx[...], wo[0], preferred_element_type=F32) + bo[...]
    total = x[...].astype(F32) + attended
    centred = total - jnp.mean(total, axis=-1, keepdims=True)
    inv_std = lax.rsqrt(jnp.mean(centred * centred, axis=-1, keepdims=True) + EPSILON)
    unit_val = centred * inv_std
    unit[...] = unit_val
    low[...] = (unit_val * gain[...] + shift[...]).astype(BF)
    saved[...] = jnp.where(lane == 127, inv_std, keep)


def attend(q, k, v, segc, segr, x, full, bo, gain, shift):
    rows, width = q.shape
    block = rows_spec(BLOCK, width)
    return pl.pallas_call(
        attend_kernel,
        grid=(rows // BLOCK,),
        in_specs=[
            block,
            whole_spec((rows, width)),
            whole_spec((rows, width)),
            rows_spec(BLOCK, 1),
            whole_spec((1, rows)),
            block,
            pl.BlockSpec((1, width, width), lambda i: (3, 0, 0), pipeline_mode=pl.Buffered(1)),
            whole_spec((1, width)),
            whole_spec((1, width)),
            whole_spec((1, width)),
        ],
        out_specs=[block, rows_spec(BLOCK, 128), block, block],
        out_shape=[
            shape((rows, width), BF),
            shape((rows, 128), F32),
            shape((rows, width), F32),
            shape((rows, width), BF),
        ],
        compiler_params=params(),
        cost_estimate=cost(18),
        name="attend",
    )(q, k, v, segc, segr, x, full, bo, gain, shift)


def attend_back_kernel(q, k, v, do, saved, segc, segr, *refs):
    dq, dk, dv, sums, dk_sum, dv_sum = refs[-6:]
    step = pl.program_id(0)

    @pl.when(step == 0)
    def _():
        dk_sum[...] = jnp.zeros_like(dk_sum)
        dv_sum[...] = jnp.zeros_like(dv_sum)
        sums[...] = jnp.zeros_like(sums)

    start = window_start(step, k.shape[0])
    near = pl.ds(start, WINDOW)
    penalty = jnp.where(segc[...] == segr[:, near], 0.0, MASKED)
    for group in range(q.shape[1] // GROUP):
        cols = slice(group * GROUP, (group + 1) * GROUP)
        q4 = spread_heads(q[:, cols] * SCALE)
        do4 = spread_heads(do[:, cols])
        k4 = k[near, cols]
        logits = lax.dot_general(q4, k4, NT, preferred_element_type=F32)
        logits = logits.reshape(4, BLOCK, WINDOW) + penalty[None]
        lse = jnp.stack([saved[:, group * 4 + h : group * 4 + h + 1] for h in range(4)])
        probs = jnp.exp(logits - lse)
        weight_grad = lax.dot_general(
            do4, v[near, cols], NT, preferred_element_type=F32
        ).reshape(4, BLOCK, WINDOW)
        inner = jnp.sum(weight_grad * probs, axis=-1, keepdims=True)
        logit_grad = (probs * (weight_grad - inner)).astype(BF).reshape(4 * BLOCK, WINDOW)
        probs_low = probs.astype(BF).reshape(4 * BLOCK, WINDOW)
        dq_low = (
            gather_heads(jnp.dot(logit_grad, k4, preferred_element_type=F32)) * SCALE
        ).astype(BF)
        dq[:, cols] = dq_low
        sums[0:1, cols] += jnp.sum(dq_low.astype(F32), axis=0, keepdims=True)
        dk_sum[near, cols] += lax.dot_general(logit_grad, q4, TN, preferred_element_type=F32)
        dv_sum[near, cols] += lax.dot_general(probs_low, do4, TN, preferred_element_type=F32)

    @pl.when(step == pl.num_programs(0) - 1)
    def _():
        dk[...] = dk_sum[...].astype(BF)
        dv_low = dv_sum[...].astype(BF)
        dv[...] = dv_low
        sums[1:2, :] = jnp.sum(dv_low.astype(F32), axis=0, keepdims=True)


def attend_back(q, k, v, do, saved, segc, segr, *tokens):
    rows, width = q.shape
    block = rows_spec(BLOCK, width)
    full = whole_spec((rows, width))
    return pl.pallas_call(
        attend_back_kernel,
        grid=(rows // BLOCK,),
        in_specs=[
            block,
            full,
            full,
            block,
            rows_spec(BLOCK, 128),
            rows_spec(BLOCK, 1),
            whole_spec((1, rows)),
        ]
        + [token_spec() for _ in tokens],
        out_specs=[block, fixed_spec((rows, width)), fixed_spec((rows, width)), fixed_spec((8, width))],
        out_shape=[shape((rows, width), BF)] * 3 + [shape((8, width), F32)],
        scratch_shapes=[pltpu.VMEM((rows, width), F32)] * 2,
        compiler_params=params(),
        cost_estimate=cost(30),
        name="attend_back",
    )(q, k, v, do, saved, segc, segr, *tokens)


def feed_kernel(place, x, unit, cot, turned, own, bu, vectors, *refs):
    pieces, outs = refs[:20], refs[20:]
    act, slope, layer, output, second, down_grad, sums, wu, wd = outs
    core, plane = place[0], place[1]
    sub = own.shape[0] // 8
    shards = 1 + pieces[0].shape[0] // sub

    @pl.when(pl.program_id(0) == 0)
    def _():
        sums[...] = jnp.zeros_like(sums)
        for source, into, parts in ((turned, wu, pieces[:10]), (own, wd, pieces[10:])):
            for c in range(2):
                a, x_, y_, first, second_ = parts[5 * c : 5 * c + 5]
                for g in range(4):
                    at = pl.multiple_of(((core ^ c) * 4 + (plane ^ g)) * sub, GRAIN)
                    to = (c * 4 + g) * shards * sub
                    into[to : to + sub, :] = source[pl.ds(at, sub), :]
                    to = to + sub
                    for ref in ((a,), (x_,), (y_,), (first, second_))[g]:
                        into[to : to + ref.shape[0], :] = ref[...]
                        to = to + ref.shape[0]

    block = x[...]
    hidden = wu.shape[0]
    for at in range(0, hidden, 256):
        span = slice(at, at + 256)
        pre = (
            lax.dot_general(block, wu[span, :], NT, preferred_element_type=F32) + bu[:, span]
        )
        below = 0.5 * (1.0 + lax.erf(pre * 0.7071067811865476))
        density = jnp.exp(-0.5 * pre * pre) * 0.3989422804014327
        act[:, span] = (pre * below).astype(BF)
        slope[:, span] = (below + pre * density).astype(BF)
    down = jnp.dot(act[...], wd[...], preferred_element_type=F32)
    b_down, first_gain, first_shift, second_gain, second_shift = (
        vectors[i : i + 1, :] for i in range(5)
    )
    total = unit[...] * first_gain + first_shift + down + b_down
    centred = total - jnp.mean(total, axis=-1, keepdims=True)
    inv_std = lax.rsqrt(jnp.mean(centred * centred, axis=-1, keepdims=True) + EPSILON)
    unit_val = centred * inv_std
    layer_out = unit_val * second_gain + second_shift
    layer[...] = layer_out
    output[...] = layer_out.astype(BF)
    grad = cot[...].astype(F32)
    scaled = grad * second_gain
    inner = (
        scaled
        - jnp.mean(scaled, axis=-1, keepdims=True)
        - unit_val * jnp.mean(scaled * unit_val, axis=-1, keepdims=True)
    )
    second_grad = inv_std * inner
    second[...] = second_grad
    grad_low = second_grad.astype(BF)
    down_grad[...] = grad_low
    sums[0:1, :] += jnp.sum(grad_low.astype(F32), axis=0, keepdims=True)
    sums[1:2, :] += jnp.sum(grad * unit_val, axis=0, keepdims=True)
    sums[2:3, :] += jnp.sum(grad, axis=0, keepdims=True)


def feed(place, x, unit, cot, turned, own, bu, vectors, pieces):
    rows, width = x.shape
    hidden = bu.shape[1]
    block = rows_spec(ROW_BLOCK, width)
    wide = rows_spec(ROW_BLOCK, hidden)
    weight = fixed_spec((hidden, width))
    return pl.pallas_call(
        feed_kernel,
        grid=(rows // ROW_BLOCK,),
        in_specs=[scalar_spec(), block, block, block]
        + [whole_spec(a.shape) for a in (turned, own, bu, vectors, *pieces)],
        out_specs=[wide, wide, block, block, block, block, fixed_spec((8, width)), weight, weight],
        out_shape=[
            shape((rows, hidden), BF),
            shape((rows, hidden), BF),
            shape((rows, width), F32),
            shape((rows, width), BF),
            shape((rows, width), F32),
            shape((rows, width), BF),
            shape((8, width), F32),
            shape((hidden, width), BF),
            shape((hidden, width), BF),
        ],
        compiler_params=params(56),
        cost_estimate=cost(24),
        name="feed",
    )(place, x, unit, cot, turned, own, bu, vectors, *pieces)


def down_weight_kernel(act, grad, *refs):
    refs[-1][...] = lax.dot_general(
        act[...], grad[...], TN, preferred_element_type=F32
    ).astype(BF)


def down_weight(act, grad, side, *tokens):
    rows, hidden = act.shape
    width = grad.shape[1]
    span = hidden // 4
    return pl.pallas_call(
        down_weight_kernel,
        grid=(2,),
        in_specs=[
            pl.BlockSpec((rows, span), lambda j: (0, 2 * side + j)),
            whole_spec((rows, width)),
        ]
        + [token_spec() for _ in tokens],
        out_specs=rows_spec(span, width),
        out_shape=shape((hidden // 2, width), BF),
        compiler_params=params(),
        cost_estimate=cost(5),
        name="down_weight",
    )(act, grad, *tokens)


def feed_back_kernel(more, grad, x, wu, wd, slope, *refs):
    weight, bias, out, held = refs[-4:]
    base = refs[0]

    @pl.when(pl.program_id(0) == 0)
    def _():
        out[...] = base[...] if more else jnp.zeros_like(out)

    total = None
    for at in range(0, x.shape[0], ROW_BLOCK):
        span = slice(at, at + ROW_BLOCK)
        act_grad = lax.dot_general(grad[span, :], wd[...], NT, preferred_element_type=F32)
        low = (act_grad * slope[span, :].astype(F32)).astype(BF)
        held[span, :] = low
        term = jnp.sum(low.astype(F32), axis=0, keepdims=True)
        total = term if total is None else total + term
    bias[...] = total
    out[...] += jnp.dot(held[...], wu[...], preferred_element_type=F32)
    weight[...] = lax.dot_general(
        held[...], x[...], TN, preferred_element_type=F32
    ).astype(BF)


def feed_back(grad, x, wu, wd, slope, side, base, *tokens):
    rows, width = x.shape
    hidden = wu.shape[0]
    span = hidden // 4
    full = whole_spec((rows, width))
    weight = pl.BlockSpec((span, width), lambda j: (2 * side + j, 0))
    return pl.pallas_call(
        functools.partial(feed_back_kernel, base is not None),
        grid=(2,),
        in_specs=[full, full, weight, weight, pl.BlockSpec((rows, span), lambda j: (0, 2 * side + j))]
        + ([full] if base is not None else [])
        + [token_spec() for _ in tokens],
        out_specs=[
            rows_spec(span, width),
            pl.BlockSpec((1, span), lambda j: (0, j)),
            fixed_spec((rows, width)),
        ],
        out_shape=[
            shape((hidden // 2, width), BF),
            shape((1, hidden // 2), F32),
            shape((rows, width), F32),
        ],
        scratch_shapes=[pltpu.VMEM((rows, span), BF)],
        compiler_params=params(),
        cost_estimate=cost(11),
        name="feed_back",
    )(grad, x, wu, wd, slope, *(() if base is None else (base,)), *tokens)


def middle_kernel(normed, second, unit, saved, ctx, wo, gain, *refs):
    first, context_grad, weight, sums, held = refs[-5:]
    step = pl.program_id(0)
    grad = normed[...] + second[...]
    unit_val = unit[...]
    scaled = grad * gain[...]
    inner = (
        scaled
        - jnp.mean(scaled, axis=-1, keepdims=True)
        - unit_val * jnp.mean(scaled * unit_val, axis=-1, keepdims=True)
    )
    first_grad = saved[:, 127:128] * inner
    first[...] = first_grad
    low = first_grad.astype(BF)
    context_grad[...] = lax.dot_general(
        low, wo[0], NT, preferred_element_type=F32
    ).astype(BF)
    term = lax.dot_general(ctx[...], low, TN, preferred_element_type=F32)

    @pl.when(step == 0)
    def _():
        sums[...] = jnp.zeros_like(sums)
        held[...] = jnp.zeros_like(held)

    held[...] += term
    sums[0:1, :] += jnp.sum(low.astype(F32), axis=0, keepdims=True)
    sums[1:2, :] += jnp.sum(grad * unit_val, axis=0, keepdims=True)
    sums[2:3, :] += jnp.sum(grad, axis=0, keepdims=True)

    @pl.when(step == pl.num_programs(0) - 1)
    def _():
        weight[...] = held[...].astype(BF)


def middle(normed, second, unit, saved, ctx, full, gain, *tokens):
    rows, width = normed.shape
    block = rows_spec(ROW_BLOCK, width)
    return pl.pallas_call(
        middle_kernel,
        grid=(rows // ROW_BLOCK,),
        in_specs=[
            block,
            block,
            block,
            rows_spec(ROW_BLOCK, 128),
            block,
            pl.BlockSpec((1, width, width), lambda i: (3, 0, 0), pipeline_mode=pl.Buffered(1)),
            whole_spec((1, width)),
        ]
        + [token_spec() for _ in tokens],
        out_specs=[block, block, fixed_spec((width, width)), fixed_spec((8, width))],
        out_shape=[
            shape((rows, width), F32),
            shape((rows, width), BF),
            shape((width, width), BF),
            shape((8, width), F32),
        ],
        scratch_shapes=[pltpu.VMEM((width, width), F32)],
        compiler_params=params(),
        cost_estimate=cost(8),
        name="middle",
    )(normed, second, unit, saved, ctx, full, gain, *tokens)


def head_weights_kernel(place, dq, dk, dv, x, wo, *refs):
    keep, send, held = refs[-3:]
    core = place[0]
    shards, heads = keep.shape[1], keep.shape[3]
    for kind in range(4):
        if kind < 3:
            held[...] = lax.dot_general(
                (dq, dk, dv)[kind][...], x[...], TN, preferred_element_type=F32
            ).astype(BF)
        source = held if kind < 3 else wo
        for side in range(2):

            @pl.when(core == side)
            def _():
                out = keep if side == kind // 2 else send
                for r in range(shards):
                    for h in range(heads):
                        for g in range(4):
                            at = (r * heads + h) * HEAD_DIM + g * GRAIN
                            out[g, r, kind % 2, h] = source[at : at + GRAIN, :]


def head_weights(place, dq, dk, dv, x, wo, n_mp, *tokens):
    rows, width = x.shape
    heads = width // HEAD_DIM // n_mp
    dims = (4, n_mp, 2, heads, GRAIN, width)
    keep, send = pl.pallas_call(
        head_weights_kernel,
        in_specs=[scalar_spec()] + [held_spec()] * 5 + [token_spec() for _ in tokens],
        out_specs=[held_spec()] * 2,
        out_shape=[shape(dims, BF)] * 2,
        scratch_shapes=[pltpu.VMEM((width, width), BF)],
        compiler_params=params(),
        cost_estimate=cost(8),
        name="head_weights",
    )(place, dq, dk, dv, x, wo, *tokens)
    dims = (4, n_mp, 2 * heads * GRAIN, width)
    return keep.reshape(dims), send.reshape(dims)


def input_kernel(dq, dk, dv, full, first, *refs):
    out = refs[-1]
    total = first[...]
    for kind, ref in enumerate((dq, dk, dv)):
        total = total + jnp.dot(ref[...], full[kind], preferred_element_type=F32)
    out[...] = total


def input_gradient(dq, dk, dv, full, first, *tokens):
    rows, width = dq.shape
    block = rows_spec(ROW_BLOCK, width)
    return pl.pallas_call(
        input_kernel,
        grid=(rows // ROW_BLOCK,),
        in_specs=[
            block,
            block,
            block,
            pl.BlockSpec((3, width, width), lambda i: (0, 0, 0), pipeline_mode=pl.Buffered(1)),
            block,
        ]
        + [token_spec() for _ in tokens],
        out_specs=block,
        out_shape=shape((rows, width), F32),
        compiler_params=params(),
        cost_estimate=cost(6),
        name="input_gradient",
    )(dq, dk, dv, full, first, *tokens)


def score_kernel(out_ref, segr_ref, len_ref, table_ref, pick_ref, *refs):
    score_ref = refs[-1]
    queries = pick_ref.shape[0]
    rows = out_ref.shape[0]
    label = lax.broadcasted_iota(jnp.int32, (queries, rows), 0)
    onehot = (label == segr_ref[...]).astype(F32)
    sums = jnp.dot(
        onehot, out_ref[...], precision=lax.Precision.HIGHEST, preferred_element_type=F32
    )
    means = sums / len_ref[...].astype(F32)
    every = lax.dot_general(
        means,
        table_ref[...].astype(F32),
        NT,
        precision=lax.Precision.HIGHEST,
        preferred_element_type=F32,
    )
    at = lax.broadcasted_iota(jnp.int32, every.shape, 1)
    column = lax.broadcasted_iota(jnp.int32, pick_ref.shape, 1)
    result = jnp.zeros(pick_ref.shape, F32)
    for p in range(pick_ref.shape[1]):
        chosen = jnp.sum(
            jnp.where(at == pick_ref[:, p : p + 1], every, 0.0), axis=1, keepdims=True
        )
        result = jnp.where(column == p, chosen, result)
    score_ref[...] = result


def score(layer_out, segr, lengths, table, picks, *tokens):
    return pl.pallas_call(
        score_kernel,
        in_specs=[held_spec()] * 5 + [token_spec() for _ in tokens],
        out_specs=held_spec(),
        out_shape=shape(picks.shape, F32),
        compiler_params=params(),
        cost_estimate=cost(8),
        name="score",
    )(layer_out, segr, lengths, table, picks, *tokens)


def per_device(
    n_dp,
    n_mp,
    hidden_in,
    cotangent,
    query_lengths,
    passage_index,
    passages,
    w_query,
    w_key,
    w_value,
    w_output,
    w_up,
    w_down,
    b_query,
    b_value,
    b_output,
    b_up,
    b_down,
    first_gain,
    first_shift,
    second_gain,
    second_shift,
):
    rows, width = hidden_in.shape
    heads = w_query.shape[1] // HEAD_DIM
    sub = w_up.shape[1] // 8
    at_dp = lax.axis_index("dp")
    core, plane = at_dp & 1, (at_dp >> 1) & 3
    place = jnp.stack([core, plane]).astype(jnp.int32)
    own_heads = (w_query.T, w_key.T, w_value.T, w_output)

    heads_piece = piece_heads(place, *own_heads)
    turned, up_piece, down_piece = piece_feed(place, w_up, w_down)

    heads_shards = shard_step(heads_piece, n_mp)
    up_shards = shard_step(after(up_piece, heads_shards), n_mp)
    heads_plane = plane_step(heads_shards, n_dp)
    heads_corner = corner_step(*heads_plane, n_dp)
    heads_mine = [heads_shards, *heads_plane, *heads_corner]
    heads_pieces = heads_mine + core_step(heads_mine, n_dp)
    down_shards = shard_step(after(down_piece, up_shards, heads_plane[0]), n_mp)
    up_plane = plane_step(after(up_shards, *heads_corner), n_dp)
    up_corner = corner_step(*up_plane, n_dp)
    up_mine = [up_shards, *up_plane, *up_corner]
    up_pieces = up_mine + core_step(up_mine, n_dp)
    down_plane = plane_step(after(down_shards, *up_corner), n_dp)
    down_corner = corner_step(*down_plane, n_dp)
    down_mine = [down_shards, *down_plane, *down_corner]
    down_pieces = down_mine + core_step(down_mine, n_dp)

    order4 = (lax.broadcasted_iota(jnp.int32, (4, 4), 0) ^ plane) == lax.broadcasted_iota(
        jnp.int32, (4, 4), 1
    )
    order8 = (
        lax.broadcasted_iota(jnp.int32, (8, 8), 0) ^ (core * 4 + plane)
    ) == lax.broadcasted_iota(jnp.int32, (8, 8), 1)
    order4, order8 = order4.astype(F32), order8.astype(F32)
    exact = functools.partial(
        jnp.einsum, precision=lax.Precision.HIGHEST, preferred_element_type=F32
    )

    def turn_heads(vector):
        return exact("gk,thki->thgi", order4, vector.reshape(-1, heads, 4, GRAIN))

    def turn_hidden(vector):
        return exact("sk,ki->si", order8, vector.reshape(8, sub))

    local_bias = jnp.concatenate(
        [
            turn_heads(jnp.concatenate([b_query, b_value]).astype(F32)).reshape(-1),
            turn_hidden(b_up.astype(F32)).reshape(-1),
        ]
    )
    all_bias = jnp.stack(
        [local_bias] + [swap(local_bias, "mp", r, n_mp) for r in range(1, n_mp)]
    )
    cut = heads * HEAD_DIM
    query_bias = all_bias[:, :cut].reshape(1, -1)
    value_bias = all_bias[:, cut : 2 * cut].reshape(1, -1)
    up_bias = all_bias[:, 2 * cut :].reshape(n_mp, 8, sub).transpose(1, 0, 2).reshape(1, -1)

    ends = jnp.cumsum(query_lengths, axis=-1, dtype=jnp.int32)
    places = lax.broadcasted_iota(jnp.int32, (rows, query_lengths.shape[1]), 0)
    seg = jnp.sum((places >= ends).astype(jnp.int32), axis=-1)
    segc, segr = seg.reshape(rows, 1), seg.reshape(1, rows)
    vectors = jnp.stack(
        [b_down, first_gain, first_shift, second_gain, second_shift, b_output, b_output, b_output]
    ).astype(F32)

    query, key, value, full = project(
        place, hidden_in, own_heads, query_bias, value_bias, heads_pieces
    )
    context, saved, unit, low = attend(
        query, key, value, segc, segr, hidden_in, full, vectors[5:6], vectors[1:2], vectors[2:3]
    )
    act, slope, layer_out, output, second_grad, down_grad, second_sums, wu, wd = feed(
        place, low, unit, cotangent, turned, w_down, up_bias, vectors, up_pieces + down_pieces
    )

    dims = (4, n_mp, sub, width)
    down_send = down_weight(act, down_grad, 1)
    down_keep = down_weight(act, down_grad, 0)
    down_parts = chip_sum(down_keep.reshape(dims), down_send.reshape(dims), n_dp)
    up_send, bias_send, normed = feed_back(down_grad, low, wu, wd, slope, 1, None, down_keep)
    down_parts2 = plane_sum(down_parts, n_dp)
    up_keep, bias_keep, normed = feed_back(
        down_grad, low, wu, wd, slope, 0, normed, *down_parts
    )
    up_parts = chip_sum(up_keep.reshape(dims), up_send.reshape(dims), n_dp)
    first_grad, context_grad, wo_grad, first_sums = middle(
        normed, second_grad, unit, saved, context, full, vectors[1:2], *down_parts2
    )
    down_parts3 = corner_sum(down_parts2, n_dp)
    up_parts2 = plane_sum(up_parts, n_dp)
    dq, dk, dv, head_sums = attend_back(
        query, key, value, context_grad, saved, segc, segr, *down_parts3, *up_parts
    )
    down_total = shard_sum(down_parts3, n_dp, n_mp)
    up_parts3 = corner_sum(up_parts2, n_dp)
    heads_keep, heads_send = head_weights(
        place, dq, dk, dv, hidden_in, wo_grad, n_mp, down_total, *up_parts2
    )
    heads_parts = chip_sum(heads_keep, heads_send, n_dp)
    up_total = shard_sum(up_parts3, n_dp, n_mp)
    down_all = gather_sum(down_total, n_dp)
    input_grad = input_gradient(dq, dk, dv, full, first_grad, *up_parts3, heads_keep)
    heads_parts2 = plane_sum(heads_parts, n_dp)
    up_all = gather_sum(up_total, n_dp)
    scores = score(
        layer_out, segr, query_lengths.reshape(-1, 1), passages, passage_index, input_grad
    )
    heads_parts3 = corner_sum(heads_parts2, n_dp)
    heads_total = shard_sum(heads_parts3, n_dp, n_mp)
    heads_all = gather_sum(heads_total, n_dp)
    w_down_grad = finish_feed(place, down_all, False)
    w_up_grad = finish_feed(place, up_all, True)
    query_t, key_t, value_t, w_output_grad = finish_heads(place, heads_all)

    bias_grad = jnp.concatenate(
        [
            head_sums[0].reshape(n_mp, cut),
            head_sums[1].reshape(n_mp, cut),
            jnp.concatenate([bias_keep, bias_send], axis=1)
            .reshape(8, n_mp, sub)
            .transpose(1, 0, 2)
            .reshape(n_mp, -1),
        ],
        axis=1,
    )
    own_bias = bias_grad[0]
    for r in range(1, n_mp):
        own_bias = own_bias + swap(bias_grad[r], "mp", r, n_mp)
    own_bias = jnp.concatenate(
        [turn_heads(own_bias[: 2 * cut]).reshape(-1), turn_hidden(own_bias[2 * cut :]).reshape(-1)]
    )
    shared = jnp.concatenate([first_sums[:3], second_sums[:3]])
    bit = 1
    while bit < n_mp:
        shared = shared + swap(shared, "mp", bit, n_mp)
        bit *= 2
    every = jnp.concatenate([shared.reshape(-1), own_bias])
    bit = 1
    while bit < n_dp:
        every = every + swap(every, "dp", bit, n_dp)
        bit *= 2
    shared = every[: 6 * width].reshape(6, width)
    own_bias = every[6 * width :]
    return (
        output,
        scores,
        input_grad,
        query_t.T,
        key_t.T,
        value_t.T,
        w_output_grad,
        w_up_grad,
        w_down_grad,
        own_bias[:cut],
        own_bias[cut : 2 * cut],
        shared[0],
        own_bias[2 * cut :],
        shared[3],
        shared[1],
        shared[2],
        shared[4],
        shared[5],
    )


def solution(mesh):
    both, split = P(("dp", "mp"), None), P(None, "mp")
    return jax.shard_map(
        functools.partial(per_device, mesh.shape["dp"], mesh.shape["mp"]),
        mesh=mesh,
        in_specs=(both, both, both, both, P())
        + (split, split, split, P("mp", None), split, P("mp", None))
        + (P("mp"), P("mp"), P(), P("mp"), P(), P(), P(), P(), P()),
        out_specs=(both, both, both)
        + (split, split, split, P("mp", None), split, P("mp", None))
        + (P("mp"), P("mp"), P(), P("mp"), P(), P(), P(), P(), P()),
        check_vma=False,
    )
```

```python
import functools

import jax
import jax.numpy as jnp
from jax import lax
from jax.experimental import pallas as pl
from jax.experimental.pallas import tpu as pltpu
from jax.sharding import PartitionSpec as P

HEAD_DIM = 64
SCALE = 0.125
EPSILON = 1e-12
MASKED = -1e30
BLOCK = 128
WINDOW = 384
GROUP = 4 * HEAD_DIM
ROW_BLOCK = 256
GRAIN = 16
MEBI = 1024 * 1024
NT = (((1,), (1,)), ((), ()))
TN = (((0,), (0,)), ((), ()))
BF = jnp.bfloat16
F32 = jnp.float32

CORE, XBIT, YBIT = 1, 2, 4


def params(mebi=60):
    return pltpu.CompilerParams(vmem_limit_bytes=mebi * MEBI)


def cost(us):
    return pl.CostEstimate(flops=int(us * 5e9), bytes_accessed=int(us * 15e6), transcendentals=0)


def shape(dims, dtype):
    return jax.ShapeDtypeStruct(dims, dtype)


def scalar_spec():
    return pl.BlockSpec(memory_space=pltpu.SMEM)


def held_spec():
    return pl.BlockSpec(memory_space=pltpu.VMEM)


def whole_spec(dims):
    return pl.BlockSpec(dims, lambda i: (0,) * len(dims), pipeline_mode=pl.Buffered(1))


def fixed_spec(dims):
    return pl.BlockSpec(dims, lambda i: (0,) * len(dims))


def rows_spec(rows, width):
    return pl.BlockSpec((rows, width), lambda i: (i, 0))


def token_spec():
    return pl.BlockSpec(memory_space=pl.ANY)


def swap(block, axis, bit, size):
    return lax.ppermute(block, axis, [(i, i ^ bit) for i in range(size)])


def after(value, *others):
    return lax.optimization_barrier((value, *others))[0]


def neighbour(core, g):
    if g in (0, 3):
        return g
    return g ^ (3 * core)


def piece_heads_kernel(place, wq, wk, wv, wo, piece, sems):
    core, plane = place[0], place[1]
    heads = piece.shape[1]
    for side, pair in enumerate(((wq, wk), (wv, wo))):

        @pl.when(core == side)
        def _():
            copies = []
            for t, ref in enumerate(pair):
                for h in range(heads):
                    start = pl.multiple_of(h * HEAD_DIM + plane * GRAIN, GRAIN)
                    copies.append(
                        pltpu.make_async_copy(
                            ref.at[pl.ds(start, GRAIN), :], piece.at[t, h], sems.at[t * heads + h]
                        )
                    )
            for copy in copies:
                copy.start()
            for copy in copies:
                copy.wait()


def piece_heads(place, *weights):
    local, width = weights[0].shape
    heads = local // HEAD_DIM
    return pl.pallas_call(
        piece_heads_kernel,
        in_specs=[scalar_spec()] + [token_spec()] * 4,
        out_specs=held_spec(),
        out_shape=shape((2, heads, GRAIN, width), BF),
        scratch_shapes=[pltpu.SemaphoreType.DMA((2 * heads,))],
        compiler_params=params(),
        cost_estimate=cost(1),
        name="piece_heads",
    )(place, *weights).reshape(2 * heads * GRAIN, width)


def piece_feed_kernel(place, wu, wd, turned, piece_up, piece_down):
    core, plane = place[0], place[1]
    sub = piece_up.shape[0]
    turned[...] = wu[...].astype(F32).T.astype(BF)
    start = pl.multiple_of((core * 4 + plane) * sub, GRAIN)
    piece_up[...] = turned[pl.ds(start, sub), :]
    piece_down[...] = wd[pl.ds(start, sub), :]


def piece_feed(place, wu, wd):
    width, hidden = wu.shape
    sub = hidden // 8
    return pl.pallas_call(
        piece_feed_kernel,
        in_specs=[scalar_spec()] + [held_spec()] * 2,
        out_specs=[held_spec()] * 3,
        out_shape=[shape((hidden, width), BF), shape((sub, width), BF), shape((sub, width), BF)],
        compiler_params=params(),
        cost_estimate=cost(3),
        name="piece_feed",
    )(place, wu, wd)


def finish_feed_kernel(place, mine, other, up, down, held):
    core = place[0]
    sub = mine.shape[1] // 2
    for c, ref in enumerate((mine, other)):
        for g in range(4):
            start = pl.multiple_of(((core ^ c) * 4 + g) * sub, GRAIN)
            held[pl.ds(start, sub), :] = ref[g, :sub, :].astype(F32)
            down[pl.ds(start, sub), :] = ref[g, sub:, :].astype(F32)
    up[...] = held[...].T


def finish_feed(place, pieces, *tokens):
    _, rows, width = pieces[0].shape
    return pl.pallas_call(
        finish_feed_drop,
        in_specs=[scalar_spec()] + [held_spec()] * 2 + [token_spec() for _ in tokens],
        out_specs=[held_spec()] * 2,
        out_shape=[shape((width, 4 * rows), F32), shape((4 * rows, width), F32)],
        scratch_shapes=[pltpu.VMEM((4 * rows, width), F32)],
        compiler_params=params(),
        cost_estimate=cost(6),
        name="finish_feed",
    )(place, *pieces, *tokens)


def finish_feed_drop(place, mine, other, *refs):
    finish_feed_kernel(place, mine, other, *refs[-3:])


def finish_heads_kernel(place, mine, other, *outs):
    core = place[0]
    heads = outs[0].shape[0] // HEAD_DIM
    for side in range(2):

        @pl.when(core == side)
        def _():
            for c, ref in enumerate((mine, other)):
                for t in range(2):
                    out = outs[2 * (side ^ c) + t]
                    for g in range(4):
                        for h in range(heads):
                            at = h * HEAD_DIM + g * GRAIN
                            row = (t * heads + h) * GRAIN
                            out[at : at + GRAIN, :] = ref[g, row : row + GRAIN, :].astype(F32)


def finish_heads(place, pieces):
    _, rows, width = pieces[0].shape
    local = rows // (2 * GRAIN) * HEAD_DIM
    return pl.pallas_call(
        finish_heads_kernel,
        in_specs=[scalar_spec()] + [held_spec()] * 2,
        out_specs=[held_spec()] * 4,
        out_shape=[shape((local, width), F32)] * 4,
        compiler_params=params(),
        cost_estimate=cost(2),
        name="finish_heads",
    )(place, *pieces)


def shard_step(piece, n_mp):
    return [swap(piece, "mp", r, n_mp) for r in range(1, n_mp)]


def turn_swap(block, bits, n_dp):
    return lax.ppermute(block, "dp", [(i, i ^ bits[i & 1]) for i in range(n_dp)])


def first_swap(block, n_dp):
    return turn_swap(block, (XBIT, YBIT), n_dp)


def second_swap(block, n_dp):
    return turn_swap(block, (YBIT, XBIT), n_dp)


def core_swap(block, n_dp):
    return swap(block, "dp", CORE, n_dp)


def exchange(block, axis, groups=None):
    return lax.all_to_all(block, axis, 0, 0, axis_index_groups=groups, tiled=True)


def spread(block, n):
    return jnp.broadcast_to(block[None], (n, *block.shape))


def plane_groups(n_dp):
    return [[8 * e + 2 * g + c for g in range(4)] for e in range(n_dp // 8) for c in range(2)]


def add(*terms):
    total = terms[0].astype(F32)
    for term in terms[1:]:
        total = total + term.astype(F32)
    return total.astype(BF)


def chip_sum(keep, got):
    return add(keep[0::2], got[0::2]), add(keep[1::2], got[1::2])


def side_sum(stay, got):
    return add(stay[0], got[0]), add(stay[1], got[1])


def shard_swap(parts, n_mp):
    shard = lax.axis_index("mp")
    return [
        swap(lax.dynamic_index_in_dim(parts, shard ^ r, 0, keepdims=False), "mp", r, n_mp)
        for r in range(1, n_mp)
    ]


def shard_sum(own, got, n_dp):
    total = own.astype(F32)
    for part in got:
        total = total + part.astype(F32)
    bit = 8
    while bit < n_dp:
        total = total + swap(total, "dp", bit, n_dp)
        bit *= 2
    return total.astype(BF)


def plane_gather(four, n_dp):
    return exchange(four, "dp", plane_groups(n_dp))


def project_kernel(place, x, wq, wk, wv, wo, bq, bv, *refs):
    pieces, (q, k, v, full, sems) = refs[:8], refs[-5:]
    core, plane, shard = place[0], place[1], place[2]
    heads = wq.shape[0] // HEAD_DIM
    shards = 1 + pieces[0].shape[0] // (2 * heads * GRAIN)

    @pl.when(pl.program_id(0) == 0)
    def _():
        copies = []
        base = pl.multiple_of(shard * heads * HEAD_DIM, HEAD_DIM)
        for kind, ref in enumerate((wq, wk, wv, wo)):
            for h in range(heads):
                for g in range(4):
                    source = plane ^ neighbour(kind // 2, g)
                    at = pl.multiple_of(h * HEAD_DIM + source * GRAIN, GRAIN)
                    to = pl.multiple_of(base + h * HEAD_DIM + g * GRAIN, GRAIN)
                    copies.append(
                        pltpu.make_async_copy(
                            ref.at[pl.ds(at, GRAIN), :],
                            full.at[kind, pl.ds(to, GRAIN), :],
                            sems.at[len(copies)],
                        )
                    )
        for copy in copies:
            copy.start()
        for c in range(2):
            for g, ref in enumerate(pieces[4 * c : 4 * c + 4]):
                for r in range(1, shards):
                    base = pl.multiple_of((shard ^ r) * heads * HEAD_DIM, HEAD_DIM)
                    for t in range(2):
                        for h in range(heads):
                            row = (((r - 1) * 2 + t) * heads + h) * GRAIN
                            to = pl.multiple_of(base + h * HEAD_DIM + g * GRAIN, GRAIN)
                            full[(core ^ c) * 2 + t, pl.ds(to, GRAIN), :] = ref[
                                row : row + GRAIN, :
                            ]
        for copy in copies:
            copy.wait()

    block = x[...]
    for kind, (out, bias) in enumerate(((q, bq), (k, None), (v, bv))):
        value = lax.dot_general(block, full[kind], NT, preferred_element_type=F32)
        if bias is not None:
            value = value + bias[...]
        out[...] = value.astype(BF)


def project(place, x, weights, bq, bv, pieces, *tokens):
    rows, width = x.shape
    block = rows_spec(ROW_BLOCK, width)
    return pl.pallas_call(
        project_kernel,
        grid=(rows // ROW_BLOCK,),
        in_specs=[scalar_spec(), block]
        + [token_spec()] * 4
        + [whole_spec(a.shape) for a in (bq, bv, *pieces)]
        + [token_spec() for _ in tokens],
        out_specs=[block, block, block, fixed_spec((4, width, width))],
        out_shape=[shape((rows, width), BF)] * 3 + [shape((4, width, width), BF)],
        scratch_shapes=[pltpu.SemaphoreType.DMA((weights[0].shape[0] // GRAIN * 4,))],
        compiler_params=params(),
        cost_estimate=cost(10),
        name="project",
    )(place, x, *weights, bq, bv, *pieces, *tokens)


def spread_heads(block):
    lane = lax.broadcasted_iota(jnp.int32, block.shape, 1) // HEAD_DIM
    return jnp.concatenate(
        [jnp.where(lane == h, block, jnp.zeros_like(block)) for h in range(4)], axis=0
    )


def gather_heads(stacked):
    rows = stacked.shape[0] // 4
    lane = lax.broadcasted_iota(jnp.int32, (rows, GROUP), 1) // HEAD_DIM
    out = stacked[:rows]
    for h in range(1, 4):
        out = jnp.where(lane == h, stacked[h * rows : (h + 1) * rows], out)
    return out


def window_start(step, rows):
    return pl.multiple_of(jnp.clip(step - 1, 0, (rows - WINDOW) // BLOCK) * BLOCK, BLOCK)


def attend_kernel(part, q, k, v, segc, segr, x, wo, bo, gain, shift, *refs):
    ctx, saved, unit, low = refs[-4:]
    start = window_start(part * pl.num_programs(0) + pl.program_id(0), k.shape[0])
    near = pl.ds(start, WINDOW)
    penalty = jnp.where(segc[...] == segr[:, near], 0.0, MASKED)
    lane = lax.broadcasted_iota(jnp.int32, (BLOCK, 128), 1)
    groups = q.shape[1] // GROUP

    def score_group(group):
        cols = slice(group * GROUP, (group + 1) * GROUP)
        return lax.dot_general(
            spread_heads(q[:, cols] * SCALE), k[near, cols], NT, preferred_element_type=F32
        )

    keep = jnp.zeros((BLOCK, 128), F32)
    ahead = score_group(0)
    for group in range(groups):
        cols = slice(group * GROUP, (group + 1) * GROUP)
        logits = ahead.reshape(4, BLOCK, WINDOW) + penalty[None]
        if group + 1 < groups:
            ahead = score_group(group + 1)
        peak = jnp.max(logits, axis=-1, keepdims=True)
        raised = jnp.exp(logits - peak)
        sums = jnp.sum(raised, axis=-1, keepdims=True)
        context = jnp.dot(
            raised.astype(BF).reshape(4 * BLOCK, WINDOW), v[near, cols], preferred_element_type=F32
        )
        context = (context.reshape(4, BLOCK, GROUP) * (1.0 / sums)).reshape(4 * BLOCK, GROUP)
        ctx[:, cols] = gather_heads(context).astype(BF)
        log_total = peak + jnp.log(sums)
        for h in range(4):
            keep = jnp.where(lane == group * 4 + h, log_total[h], keep)
    attended = jnp.dot(ctx[...], wo[0], preferred_element_type=F32) + bo[...]
    total = x[...].astype(F32) + attended
    centred = total - jnp.mean(total, axis=-1, keepdims=True)
    inv_std = lax.rsqrt(jnp.mean(centred * centred, axis=-1, keepdims=True) + EPSILON)
    unit_val = centred * inv_std
    unit[...] = unit_val
    low[...] = (unit_val * gain[...] + shift[...]).astype(BF)
    saved[...] = jnp.where(lane == 127, inv_std, keep)


def attend(part, parts, q, k, v, segc, segr, x, full, bo, gain, shift, held, *tokens):
    rows, width = q.shape
    steps = rows // BLOCK // parts

    def block(wide):
        return pl.BlockSpec((BLOCK, wide), lambda i: (part * steps + i, 0))

    return pl.pallas_call(
        functools.partial(attend_kernel, part),
        grid=(steps,),
        in_specs=[
            block(width),
            whole_spec((rows, width)),
            whole_spec((rows, width)),
            block(1),
            whole_spec((1, rows)),
            block(width),
            pl.BlockSpec((1, width, width), lambda i: (3, 0, 0), pipeline_mode=pl.Buffered(1)),
            whole_spec((1, width)),
            whole_spec((1, width)),
            whole_spec((1, width)),
        ]
        + [token_spec() for _ in (*held, *tokens)],
        out_specs=[block(width), block(128), block(width), block(width)],
        out_shape=[
            shape((rows, width), BF),
            shape((rows, 128), F32),
            shape((rows, width), F32),
            shape((rows, width), BF),
        ],
        input_output_aliases={10 + i: i for i in range(len(held))},
        compiler_params=params(),
        cost_estimate=cost(16 / parts),
        name="attend",
    )(q, k, v, segc, segr, x, full, bo, gain, shift, *held, *tokens)


def attend_back_kernel(q, k, v, do, saved, inner, segc, segr, *refs):
    dq, dk, dv, sums, dk_sum, dv_sum = refs[-6:]
    step = pl.program_id(0)

    @pl.when(step == 0)
    def _():
        dk_sum[...] = jnp.zeros_like(dk_sum)
        dv_sum[...] = jnp.zeros_like(dv_sum)
        sums[...] = jnp.zeros_like(sums)

    start = window_start(step, k.shape[0])
    near = pl.ds(start, WINDOW)
    penalty = jnp.where(segc[...] == segr[:, near], 0.0, MASKED)
    for group in range(q.shape[1] // GROUP):
        cols = slice(group * GROUP, (group + 1) * GROUP)
        q4 = spread_heads(q[:, cols] * SCALE)
        do4 = spread_heads(do[:, cols])
        k4 = k[near, cols]
        logits = lax.dot_general(q4, k4, NT, preferred_element_type=F32)
        logits = logits.reshape(4, BLOCK, WINDOW) + penalty[None]
        lse = jnp.stack([saved[:, group * 4 + h : group * 4 + h + 1] for h in range(4)])
        mean_grad = jnp.stack([inner[:, group * 4 + h : group * 4 + h + 1] for h in range(4)])
        probs = jnp.exp(logits - lse)
        weight_grad = lax.dot_general(
            do4, v[near, cols], NT, preferred_element_type=F32
        ).reshape(4, BLOCK, WINDOW)
        logit_grad = (probs * (weight_grad - mean_grad)).astype(BF).reshape(4 * BLOCK, WINDOW)
        probs_low = probs.astype(BF).reshape(4 * BLOCK, WINDOW)
        dq_low = (
            gather_heads(jnp.dot(logit_grad, k4, preferred_element_type=F32)) * SCALE
        ).astype(BF)
        dq[:, cols] = dq_low
        sums[0:1, cols] += jnp.sum(dq_low.astype(F32), axis=0, keepdims=True)
        dk_sum[near, cols] += lax.dot_general(logit_grad, q4, TN, preferred_element_type=F32)
        dv_sum[near, cols] += lax.dot_general(probs_low, do4, TN, preferred_element_type=F32)

    @pl.when(step == pl.num_programs(0) - 1)
    def _():
        dk[...] = dk_sum[...].astype(BF)
        dv_low = dv_sum[...].astype(BF)
        dv[...] = dv_low
        sums[1:2, :] = jnp.sum(dv_low.astype(F32), axis=0, keepdims=True)


def attend_back(q, k, v, do, saved, inner, segc, segr, *tokens):
    rows, width = q.shape
    block = rows_spec(BLOCK, width)
    full = whole_spec((rows, width))
    return pl.pallas_call(
        attend_back_kernel,
        grid=(rows // BLOCK,),
        in_specs=[
            block,
            full,
            full,
            block,
            rows_spec(BLOCK, 128),
            rows_spec(BLOCK, 128),
            rows_spec(BLOCK, 1),
            whole_spec((1, rows)),
        ]
        + [token_spec() for _ in tokens],
        out_specs=[block, fixed_spec((rows, width)), fixed_spec((rows, width)), fixed_spec((8, width))],
        out_shape=[shape((rows, width), BF)] * 3 + [shape((8, width), F32)],
        scratch_shapes=[pltpu.VMEM((rows, width), F32)] * 2,
        compiler_params=params(),
        cost_estimate=cost(22),
        name="attend_back",
    )(q, k, v, do, saved, inner, segc, segr, *tokens)


def assemble(place, own, pieces, into):
    core, plane, shard = place[0], place[1], place[2]
    sub = own.shape[0] // 8
    shards = 1 + pieces[0].shape[0] // sub

    def rows(c, g, r):
        return pl.ds(pl.multiple_of(((c * 4 + g) * shards + (shard ^ r)) * sub, GRAIN), sub)

    for c in range(2):
        for g, ref in enumerate(pieces[4 * c : 4 * c + 4]):
            at = pl.multiple_of(((core ^ c) * 4 + (plane ^ neighbour(core ^ c, g))) * sub, GRAIN)
            into[rows(c, g, 0), :] = own[pl.ds(at, sub), :]
            for r in range(1, shards):
                into[rows(c, g, r), :] = ref[(r - 1) * sub : r * sub, :]


def feed_up_kernel(place, x, own, bu, *refs):
    pieces, (act, slope, wu) = refs[:8], refs[-3:]

    @pl.when(pl.program_id(0) == 0)
    def _():
        assemble(place, own, pieces, wu)

    block = x[...]
    for at in range(0, wu.shape[0], 256):
        span = slice(at, at + 256)
        pre = (
            lax.dot_general(block, wu[span, :], NT, preferred_element_type=F32) + bu[:, span]
        )
        below = 0.5 * (1.0 + lax.erf(pre * 0.7071067811865476))
        density = jnp.exp(-0.5 * pre * pre) * 0.3989422804014327
        act[:, span] = (pre * below).astype(BF)
        slope[:, span] = (below + pre * density).astype(BF)


def feed_up(place, x, own, bu, pieces, *tokens):
    rows, width = x.shape
    hidden = bu.shape[1]
    wide = rows_spec(ROW_BLOCK, hidden)
    return pl.pallas_call(
        feed_up_kernel,
        grid=(rows // ROW_BLOCK,),
        in_specs=[scalar_spec(), rows_spec(ROW_BLOCK, width)]
        + [whole_spec(a.shape) for a in (own, bu, *pieces)]
        + [token_spec() for _ in tokens],
        out_specs=[wide, wide, fixed_spec((hidden, width))],
        out_shape=[shape((rows, hidden), BF)] * 2 + [shape((hidden, width), BF)],
        compiler_params=params(),
        cost_estimate=cost(12),
        name="feed_up",
    )(place, x, own, bu, *pieces, *tokens)


def feed_down_kernel(place, act, unit, cot, own, vectors, *refs):
    pieces, outs = refs[:8], refs[-6:]
    layer, output, second, down_grad, sums, wd = outs

    @pl.when(pl.program_id(0) == 0)
    def _():
        sums[...] = jnp.zeros_like(sums)
        assemble(place, own, pieces, wd)

    down = jnp.dot(act[...], wd[...], preferred_element_type=F32)
    b_down, first_gain, first_shift, second_gain, second_shift = (
        vectors[i : i + 1, :] for i in range(5)
    )
    total = unit[...] * first_gain + first_shift + down + b_down
    centred = total - jnp.mean(total, axis=-1, keepdims=True)
    inv_std = lax.rsqrt(jnp.mean(centred * centred, axis=-1, keepdims=True) + EPSILON)
    unit_val = centred * inv_std
    layer_out = unit_val * second_gain + second_shift
    layer[...] = layer_out
    output[...] = layer_out.astype(BF)
    grad = cot[...].astype(F32)
    scaled = grad * second_gain
    inner = (
        scaled
        - jnp.mean(scaled, axis=-1, keepdims=True)
        - unit_val * jnp.mean(scaled * unit_val, axis=-1, keepdims=True)
    )
    second_grad = inv_std * inner
    second[...] = second_grad
    grad_low = second_grad.astype(BF)
    down_grad[...] = grad_low
    sums[0:1, :] += jnp.sum(grad_low.astype(F32), axis=0, keepdims=True)
    sums[1:2, :] += jnp.sum(grad * unit_val, axis=0, keepdims=True)
    sums[2:3, :] += jnp.sum(grad, axis=0, keepdims=True)


def feed_down(place, act, unit, cot, own, vectors, pieces):
    rows, hidden = act.shape
    width = unit.shape[1]
    block = rows_spec(ROW_BLOCK, width)
    return pl.pallas_call(
        feed_down_kernel,
        grid=(rows // ROW_BLOCK,),
        in_specs=[scalar_spec(), rows_spec(ROW_BLOCK, hidden), block, block]
        + [whole_spec(a.shape) for a in (own, vectors, *pieces)],
        out_specs=[block, block, block, block, fixed_spec((8, width)), fixed_spec((hidden, width))],
        out_shape=[
            shape((rows, width), F32),
            shape((rows, width), BF),
            shape((rows, width), F32),
            shape((rows, width), BF),
            shape((8, width), F32),
            shape((hidden, width), BF),
        ],
        compiler_params=params(),
        cost_estimate=cost(13),
        name="feed_down",
    )(place, act, unit, cot, own, vectors, *pieces)


def feed_back_kernel(grad, x, wu, wd, slope, act, keep, send, bias, out, held):
    step = pl.program_id(0)
    half = pl.num_programs(0) // 2
    chips, shards, _, sub, width = keep.shape

    @pl.when(step == 0)
    def _():
        out[...] = jnp.zeros_like(out)

    total = None
    for at in range(0, x.shape[0], ROW_BLOCK):
        span = slice(at, at + ROW_BLOCK)
        act_grad = lax.dot_general(grad[span, :], wd[...], NT, preferred_element_type=F32)
        low = (act_grad * slope[span, :].astype(F32)).astype(BF)
        held[span, :] = low
        term = jnp.sum(low.astype(F32), axis=0, keepdims=True)
        total = term if total is None else total + term
    bias[...] = jnp.broadcast_to(total, bias.shape[1:])[None]
    out[...] += jnp.dot(held[...], wu[...], preferred_element_type=F32)
    dims = (chips, shards, sub, width)
    up = lax.dot_general(held[...], x[...], TN, preferred_element_type=F32).astype(BF)
    down = lax.dot_general(act[...], grad[...], TN, preferred_element_type=F32).astype(BF)

    @pl.when(step < half)
    def _():
        send[:, :, 0] = up.reshape(dims)
        send[:, :, 1] = down.reshape(dims)

    @pl.when(step >= half)
    def _():
        keep[:, :, 0] = up.reshape(dims)
        keep[:, :, 1] = down.reshape(dims)


def feed_back(grad, x, wu, wd, slope, act, n_mp):
    rows, width = x.shape
    hidden = wu.shape[0]
    span = hidden // 4
    full = whole_spec((rows, width))
    weight = pl.BlockSpec((span, width), lambda j: ((j + 2) % 4, 0))
    wide = pl.BlockSpec((rows, span), lambda j: (0, (j + 2) % 4))
    dims = (4, n_mp, 2, hidden // 8 // n_mp, width)
    block = (2, *dims[1:])
    return pl.pallas_call(
        feed_back_kernel,
        grid=(4,),
        in_specs=[full, full, weight, weight, wide, wide],
        out_specs=[
            pl.BlockSpec(block, lambda j: (jnp.maximum(j - 2, 0), 0, 0, 0, 0)),
            pl.BlockSpec(block, lambda j: (jnp.minimum(j, 1), 0, 0, 0, 0)),
            pl.BlockSpec((1, 8, span), lambda j: ((j + 2) % 4, 0, 0)),
            fixed_spec((rows, width)),
        ],
        out_shape=[
            shape(dims, BF),
            shape(dims, BF),
            shape((4, 8, span), F32),
            shape((rows, width), F32),
        ],
        scratch_shapes=[pltpu.VMEM((rows, span), BF)],
        compiler_params=params(),
        cost_estimate=cost(27),
        name="feed_back",
    )(grad, x, wu, wd, slope, act)


def middle_kernel(normed, second, unit, saved, ctx, wo, gain, *refs):
    first, context_grad, inner_sum, weight, sums, held = refs[-6:]
    step = pl.program_id(0)
    grad = normed[...] + second[...]
    unit_val = unit[...]
    scaled = grad * gain[...]
    inner = (
        scaled
        - jnp.mean(scaled, axis=-1, keepdims=True)
        - unit_val * jnp.mean(scaled * unit_val, axis=-1, keepdims=True)
    )
    first_grad = saved[:, 127:128] * inner
    first[...] = first_grad
    low = first_grad.astype(BF)
    context_low = lax.dot_general(low, wo[0], NT, preferred_element_type=F32).astype(BF)
    context_grad[...] = context_low
    product = context_low.astype(F32) * ctx[...].astype(F32)
    high = product.astype(BF)
    rest = (product - high.astype(F32)).astype(BF)
    width = product.shape[1]
    head = lax.broadcasted_iota(jnp.int32, (width, 128), 0) // HEAD_DIM
    head = (head == lax.broadcasted_iota(jnp.int32, (width, 128), 1)).astype(BF)
    inner_sum[...] = jnp.dot(high, head, preferred_element_type=F32) + jnp.dot(
        rest, head, preferred_element_type=F32
    )
    term = lax.dot_general(ctx[...], low, TN, preferred_element_type=F32)

    @pl.when(step == 0)
    def _():
        sums[...] = jnp.zeros_like(sums)
        held[...] = jnp.zeros_like(held)

    held[...] += term
    sums[0:1, :] += jnp.sum(low.astype(F32), axis=0, keepdims=True)
    sums[1:2, :] += jnp.sum(grad * unit_val, axis=0, keepdims=True)
    sums[2:3, :] += jnp.sum(grad, axis=0, keepdims=True)

    @pl.when(step == pl.num_programs(0) - 1)
    def _():
        weight[...] = held[...].astype(BF)


def middle(normed, second, unit, saved, ctx, full, gain, *tokens):
    rows, width = normed.shape
    block = rows_spec(ROW_BLOCK, width)
    return pl.pallas_call(
        middle_kernel,
        grid=(rows // ROW_BLOCK,),
        in_specs=[
            block,
            block,
            block,
            rows_spec(ROW_BLOCK, 128),
            block,
            pl.BlockSpec((1, width, width), lambda i: (3, 0, 0), pipeline_mode=pl.Buffered(1)),
            whole_spec((1, width)),
        ]
        + [token_spec() for _ in tokens],
        out_specs=[block, block, rows_spec(ROW_BLOCK, 128), fixed_spec((width, width)), fixed_spec((8, width))],
        out_shape=[
            shape((rows, width), F32),
            shape((rows, width), BF),
            shape((rows, 128), F32),
            shape((width, width), BF),
            shape((8, width), F32),
        ],
        scratch_shapes=[pltpu.VMEM((width, width), F32)],
        compiler_params=params(),
        cost_estimate=cost(8),
        name="middle",
    )(normed, second, unit, saved, ctx, full, gain, *tokens)


def head_weights_kernel(place, dq, dk, dv, x, wo, *refs):
    keep, send, held = refs[-3:]
    core = place[0]
    shards, heads = keep.shape[1], keep.shape[3]
    for kind in range(4):
        if kind < 3:
            held[...] = lax.dot_general(
                (dq, dk, dv)[kind][...], x[...], TN, preferred_element_type=F32
            ).astype(BF)
        source = held if kind < 3 else wo
        for side in range(2):

            @pl.when(core == side)
            def _():
                out = keep if side == kind // 2 else send
                for r in range(shards):
                    for h in range(heads):
                        for g in range(4):
                            at = (r * heads + h) * HEAD_DIM + g * GRAIN
                            out[g, r, kind % 2, h] = source[at : at + GRAIN, :]


def head_weights(place, dq, dk, dv, x, wo, n_mp, *tokens):
    rows, width = x.shape
    heads = width // HEAD_DIM // n_mp
    dims = (4, n_mp, 2, heads, GRAIN, width)
    keep, send = pl.pallas_call(
        head_weights_kernel,
        in_specs=[scalar_spec()] + [held_spec()] * 5 + [token_spec() for _ in tokens],
        out_specs=[held_spec()] * 2,
        out_shape=[shape(dims, BF)] * 2,
        scratch_shapes=[pltpu.VMEM((width, width), BF)],
        compiler_params=params(),
        cost_estimate=cost(8),
        name="head_weights",
    )(place, dq, dk, dv, x, wo, *tokens)
    dims = (4, n_mp, 2 * heads * GRAIN, width)
    return keep.reshape(dims), send.reshape(dims)


def input_kernel(dq, dk, dv, full, first, *refs):
    out = refs[-1]
    total = first[...]
    for kind, ref in enumerate((dq, dk, dv)):
        total = total + jnp.dot(ref[...], full[kind], preferred_element_type=F32)
    out[...] = total


def input_gradient(dq, dk, dv, full, first, *tokens):
    rows, width = dq.shape
    block = rows_spec(ROW_BLOCK, width)
    return pl.pallas_call(
        input_kernel,
        grid=(rows // ROW_BLOCK,),
        in_specs=[
            block,
            block,
            block,
            pl.BlockSpec((3, width, width), lambda i: (0, 0, 0), pipeline_mode=pl.Buffered(1)),
            block,
        ]
        + [token_spec() for _ in tokens],
        out_specs=block,
        out_shape=shape((rows, width), F32),
        compiler_params=params(),
        cost_estimate=cost(6),
        name="input_gradient",
    )(dq, dk, dv, full, first, *tokens)


def score_kernel(out_ref, segr_ref, len_ref, table_ref, pick_ref, *refs):
    score_ref = refs[-1]
    queries = pick_ref.shape[0]
    rows = out_ref.shape[0]
    label = lax.broadcasted_iota(jnp.int32, (queries, rows), 0)
    onehot = (label == segr_ref[...]).astype(F32)
    sums = jnp.dot(
        onehot, out_ref[...], precision=lax.Precision.HIGHEST, preferred_element_type=F32
    )
    means = sums / len_ref[...].astype(F32)
    every = lax.dot_general(
        means,
        table_ref[...].astype(F32),
        NT,
        precision=lax.Precision.HIGHEST,
        preferred_element_type=F32,
    )
    at = lax.broadcasted_iota(jnp.int32, every.shape, 1)
    column = lax.broadcasted_iota(jnp.int32, pick_ref.shape, 1)
    result = jnp.zeros(pick_ref.shape, F32)
    for p in range(pick_ref.shape[1]):
        chosen = jnp.sum(
            jnp.where(at == pick_ref[:, p : p + 1], every, 0.0), axis=1, keepdims=True
        )
        result = jnp.where(column == p, chosen, result)
    score_ref[...] = result


def score(layer_out, segr, lengths, table, picks, *tokens):
    return pl.pallas_call(
        score_kernel,
        in_specs=[held_spec()] * 5 + [token_spec() for _ in tokens],
        out_specs=held_spec(),
        out_shape=shape(picks.shape, F32),
        compiler_params=params(),
        cost_estimate=cost(8),
        name="score",
    )(layer_out, segr, lengths, table, picks, *tokens)


def per_device(
    n_dp,
    n_mp,
    hidden_in,
    cotangent,
    query_lengths,
    passage_index,
    passages,
    w_query,
    w_key,
    w_value,
    w_output,
    w_up,
    w_down,
    b_query,
    b_value,
    b_output,
    b_up,
    b_down,
    first_gain,
    first_shift,
    second_gain,
    second_shift,
):
    rows, width = hidden_in.shape
    heads = w_query.shape[1] // HEAD_DIM
    sub = w_up.shape[1] // 8
    at_dp = lax.axis_index("dp")
    core, plane = at_dp & 1, (at_dp >> 1) & 3
    shard = lax.axis_index("mp")
    place = jnp.stack([core, plane, shard]).astype(jnp.int32)
    own_heads = (w_query.T, w_key.T, w_value.T, w_output)

    heads_piece = piece_heads(place, *own_heads)
    heads_parts = shard_step(heads_piece, n_mp)
    turned, up_piece, down_piece = piece_feed(place, w_up, w_down)
    heads_shards = jnp.concatenate(heads_parts)
    up_got = exchange(spread(after(up_piece, heads_shards), n_mp), "mp")
    heads_first = first_swap(heads_shards, n_dp)
    heads_second = second_swap(heads_shards, n_dp)
    heads_corner = second_swap(heads_first, n_dp)
    heads_mine = [heads_shards, heads_first, heads_second, heads_corner]
    heads_pieces = heads_mine + [core_swap(p, n_dp) for p in heads_mine]

    def others(got):
        return jnp.concatenate(
            [
                lax.dynamic_index_in_dim(got, shard ^ r, 0, keepdims=False)
                for r in range(1, n_mp)
            ]
        )

    ranks = lax.broadcasted_iota(jnp.int32, (4, 4), 0)
    places4 = lax.broadcasted_iota(jnp.int32, (4, 4), 1)
    turned_ranks = jnp.where((ranks == 1) | (ranks == 2), ranks ^ 3, ranks)
    order_q = ((plane ^ ranks) == places4).astype(F32)
    order_v = ((plane ^ turned_ranks) == places4).astype(F32)
    owner = (core ^ jnp.arange(2, dtype=jnp.int32)).reshape(2, 1, 1, 1)
    is_owner = (owner == jnp.arange(2, dtype=jnp.int32).reshape(1, 1, 2, 1)).astype(F32)
    order_up = jnp.where(owner == 0, order_q[None, :, None], order_v[None, :, None])
    order_up = (order_up * is_owner).reshape(8, 8)
    exact = functools.partial(
        jnp.einsum, precision=lax.Precision.HIGHEST, preferred_element_type=F32
    )
    cut = heads * HEAD_DIM

    def turn(vector, there="gk"):
        query = vector[:cut].reshape(-1, 4, GRAIN)
        value = vector[cut : 2 * cut].reshape(-1, 4, GRAIN)
        hidden = vector[2 * cut :].reshape(8, sub)
        to = "g" if there == "gk" else "k"
        frm = "k" if there == "gk" else "g"
        return jnp.concatenate(
            [
                exact(f"gk,t{frm}i->t{to}i", order_q, query).reshape(-1),
                exact(f"gk,t{frm}i->t{to}i", order_v, value).reshape(-1),
                exact(f"gk,{frm}i->{to}i", order_up, hidden).reshape(-1),
            ]
        )

    local_bias = turn(
        jnp.concatenate(after((b_query, b_value, b_up), heads_shards)).astype(F32)
    )
    all_bias = exchange(spread(after(local_bias, up_got), n_mp), "mp")
    query_bias = all_bias[:, :cut].reshape(1, -1)
    value_bias = all_bias[:, cut : 2 * cut].reshape(1, -1)
    up_bias = all_bias[:, 2 * cut :].reshape(n_mp, 8, sub).transpose(1, 0, 2).reshape(1, -1)

    up_shards = others(lax.optimization_barrier((up_got, *heads_pieces))[0])
    up_first = first_swap(up_shards, n_dp)
    up_second = second_swap(up_shards, n_dp)
    down_got = exchange(spread(after(down_piece, all_bias), n_mp), "mp")

    ends = jnp.cumsum(query_lengths, axis=-1, dtype=jnp.int32)
    places = lax.broadcasted_iota(jnp.int32, (rows, query_lengths.shape[1]), 0)
    seg = jnp.sum((places >= ends).astype(jnp.int32), axis=-1)
    segc, segr = seg.reshape(rows, 1), seg.reshape(1, rows)
    vectors = jnp.stack(
        [b_down, first_gain, first_shift, second_gain, second_shift, b_output, b_output, b_output]
    ).astype(F32)

    query, key, value, full = project(
        place, hidden_in, own_heads, query_bias, value_bias, heads_pieces, up_shards
    )
    up_first, up_second, down_got, query = lax.optimization_barrier(
        (up_first, up_second, down_got, query)
    )
    up_corner = second_swap(up_first, n_dp)
    up_mine = [up_shards, up_first, up_second]
    up_other = [core_swap(p, n_dp) for p in up_mine]
    down_shards = others(down_got)
    down_first = first_swap(down_shards, n_dp)
    down_second = second_swap(down_shards, n_dp)
    held = attend(
        0, 2, query, key, value, segc, segr, hidden_in, full,
        vectors[5:6], vectors[1:2], vectors[2:3], (), down_shards,
    )
    up_corner, down_first, down_second, *held = lax.optimization_barrier(
        (up_corner, down_first, down_second, *held)
    )
    up_pieces = up_mine + [up_corner] + up_other + [core_swap(up_corner, n_dp)]
    down_corner = second_swap(down_first, n_dp)
    down_mine = [down_shards, down_first, down_second]
    down_other = [core_swap(p, n_dp) for p in down_mine]
    context, saved, unit, low = attend(
        1, 2, query, key, value, segc, segr, hidden_in, full,
        vectors[5:6], vectors[1:2], vectors[2:3], held,
    )
    down_corner, low = lax.optimization_barrier((down_corner, low))
    down_pieces = down_mine + [down_corner] + down_other + [core_swap(down_corner, n_dp)]
    act, slope, wu = feed_up(place, low, turned, up_bias, up_pieces)
    layer_out, output, second_grad, down_grad, second_sums, wd = feed_down(
        place, act, unit, cotangent, w_down, vectors, down_pieces
    )

    feed_keep, feed_send, up_sums, normed = feed_back(
        down_grad, low, wu, wd, slope, act, n_mp
    )
    dims = (4, n_mp, 2 * sub, width)
    feed_keep = feed_keep.reshape(dims)
    got = core_swap(feed_send.reshape(dims), n_dp)
    first_grad, context_grad, inner, wo_grad, first_sums = middle(
        normed, second_grad, unit, saved, context, full, vectors[1:2]
    )
    got, context_grad = lax.optimization_barrier((got, context_grad))
    feed_stay, feed_go = chip_sum(feed_keep, got)
    got = first_swap(feed_go, n_dp)
    dq, dk, dv, head_sums = attend_back(
        query, key, value, context_grad, saved, inner, segc, segr, feed_go
    )
    every = jnp.concatenate(
        [second_sums, first_sums, head_sums, up_sums.reshape(-1, width)]
    )
    vector_got = swap(every, "mp", 1, n_mp)
    heads_keep, heads_send = head_weights(
        place, dq, dk, dv, hidden_in, wo_grad, n_mp, every
    )
    got, vector_got, heads_keep = lax.optimization_barrier((got, vector_got, heads_keep))
    feed_own, feed_go = side_sum(feed_stay, got)
    every = every + vector_got
    got = second_swap(feed_go, n_dp)
    vector_got = swap(every, "mp", 2, n_mp)
    heads_got = core_swap(heads_send, n_dp)
    input_grad = input_gradient(dq, dk, dv, full, first_grad, heads_keep, feed_go, every)
    got, vector_got, heads_got, input_grad = lax.optimization_barrier(
        (got, vector_got, heads_got, input_grad)
    )
    heads_stay, heads_go = chip_sum(heads_keep, heads_got)
    heads_got = first_swap(heads_go, n_dp)
    feed_parts = add(feed_own, got)
    feed_got = exchange(feed_parts, "mp")
    every = every + vector_got
    up_sums = every[24:].reshape(2, 2, 8, 2, n_mp, sub)[:, :, 0]
    own_bias = jnp.concatenate(
        [
            lax.dynamic_slice_in_dim(every[16:18], shard * cut, cut, axis=1).reshape(-1),
            lax.dynamic_index_in_dim(up_sums, shard, 3, keepdims=False).reshape(-1),
        ]
    )
    every = jnp.concatenate(
        [every[0:3].reshape(-1), every[8:11].reshape(-1), turn(own_bias, "kg")]
    )
    vector_got = core_swap(every, n_dp)
    scores = score(
        layer_out, segr, query_lengths.reshape(-1, 1), passages, passage_index,
        every, feed_parts, heads_go,
    )
    heads_got, vector_got, scores = lax.optimization_barrier((heads_got, vector_got, scores))
    heads_own, heads_go = side_sum(heads_stay, heads_got)
    heads_got = second_swap(heads_go, n_dp)
    every = every + vector_got
    vector_got = swap(every, "dp", XBIT, n_dp)
    feed_got, heads_got, vector_got = lax.optimization_barrier(
        (feed_got, heads_got, vector_got)
    )
    heads_parts = add(heads_own, heads_got)
    heads_got = shard_swap(heads_parts, n_mp)
    heads_own = lax.dynamic_index_in_dim(heads_parts, shard, 0, keepdims=False)
    feed_total = shard_sum(feed_got[0], [feed_got[r] for r in range(1, n_mp)], n_dp)
    feed_mine = plane_gather(spread(feed_total, 4), n_dp)
    every = every + vector_got
    vector_got = swap(every, "dp", YBIT, n_dp)
    feed_mine, vector_got, *heads_got = lax.optimization_barrier(
        (feed_mine, vector_got, *heads_got)
    )
    heads_total = shard_sum(heads_own, heads_got, n_dp)
    heads_mine = plane_gather(spread(heads_total, 4), n_dp)
    feed_other = core_swap(feed_mine, n_dp)
    every = every + vector_got
    bit = 8
    while bit < n_dp:
        every = every + swap(every, "dp", bit, n_dp)
        bit *= 2
    w_up_grad, w_down_grad = finish_feed(place, (feed_mine, feed_other), heads_total)
    heads_other = core_swap(after(heads_mine, w_up_grad), n_dp)
    query_t, key_t, value_t, w_output_grad = finish_heads(place, (heads_mine, heads_other))
    second_sums, first_sums = every[: 3 * width].reshape(3, width), every[3 * width : 6 * width].reshape(3, width)
    shared = [first_sums[0], second_sums[0], first_sums[1], first_sums[2], second_sums[1], second_sums[2]]
    own_bias = every[6 * width :]
    return (
        output,
        scores,
        input_grad,
        query_t.T,
        key_t.T,
        value_t.T,
        w_output_grad,
        w_up_grad,
        w_down_grad,
        own_bias[:cut],
        own_bias[cut : 2 * cut],
        shared[0],
        own_bias[2 * cut :],
        shared[1],
        shared[2],
        shared[3],
        shared[4],
        shared[5],
    )


def solution(mesh):
    both, split = P(("dp", "mp"), None), P(None, "mp")
    return jax.shard_map(
        functools.partial(per_device, mesh.shape["dp"], mesh.shape["mp"]),
        mesh=mesh,
        in_specs=(both, both, both, both, P())
        + (split, split, split, P("mp", None), split, P("mp", None))
        + (P("mp"), P("mp"), P(), P("mp"), P(), P(), P(), P(), P()),
        out_specs=(both, both, both)
        + (split, split, split, P("mp", None), split, P("mp", None))
        + (P("mp"), P("mp"), P(), P("mp"), P(), P(), P(), P(), P()),
        check_vma=False,
    )
```

```python
import functools

import jax
import jax.numpy as jnp
from jax import lax
from jax.experimental import pallas as pl
from jax.experimental.pallas import tpu as pltpu
from jax.sharding import PartitionSpec as P

HEAD_DIM = 64
SCALE = 0.125
EPSILON = 1e-12
MASKED = -1e30
BLOCK = 128
WINDOW = 384
GROUP = 4 * HEAD_DIM
ROW_BLOCK = 256
GRAIN = 16
MEBI = 1024 * 1024
NT = (((1,), (1,)), ((), ()))
TN = (((0,), (0,)), ((), ()))
BF = jnp.bfloat16
F32 = jnp.float32

CORE, XBIT, YBIT = 1, 2, 4


def params(mebi=60):
    return pltpu.CompilerParams(vmem_limit_bytes=mebi * MEBI)


def cost(us):
    return pl.CostEstimate(flops=int(us * 5e9), bytes_accessed=int(us * 15e6), transcendentals=0)


def shape(dims, dtype):
    return jax.ShapeDtypeStruct(dims, dtype)


def scalar_spec():
    return pl.BlockSpec(memory_space=pltpu.SMEM)


def held_spec():
    return pl.BlockSpec(memory_space=pltpu.VMEM)


def whole_spec(dims):
    return pl.BlockSpec(dims, lambda i: (0,) * len(dims), pipeline_mode=pl.Buffered(1))


def fixed_spec(dims):
    return pl.BlockSpec(dims, lambda i: (0,) * len(dims))


def rows_spec(rows, width):
    return pl.BlockSpec((rows, width), lambda i: (i, 0))


def token_spec():
    return pl.BlockSpec(memory_space=pl.ANY)


def swap(block, axis, bit, size):
    return lax.ppermute(block, axis, [(i, i ^ bit) for i in range(size)])


def after(value, *others):
    return lax.optimization_barrier((value, *others))[0]


def neighbour(core, g):
    if g in (0, 3):
        return g
    return g ^ (3 * core)


def piece_heads_kernel(place, wq, wk, wv, wo, piece, sems):
    core, plane = place[0], place[1]
    heads = piece.shape[0] // (2 * GRAIN)
    for side, pair in enumerate(((wq, wk), (wv, wo))):

        @pl.when(core == side)
        def _():
            copies = []
            for t, ref in enumerate(pair):
                for h in range(heads):
                    start = pl.multiple_of(h * HEAD_DIM + plane * GRAIN, GRAIN)
                    to = (t * heads + h) * GRAIN
                    copies.append(
                        pltpu.make_async_copy(
                            ref.at[pl.ds(start, GRAIN), :],
                            piece.at[to : to + GRAIN, :],
                            sems.at[t * heads + h],
                        )
                    )
            for copy in copies:
                copy.start()
            for copy in copies:
                copy.wait()


def piece_heads(place, *weights):
    local, width = weights[0].shape
    heads = local // HEAD_DIM
    return pl.pallas_call(
        piece_heads_kernel,
        in_specs=[scalar_spec()] + [token_spec()] * 4,
        out_specs=held_spec(),
        out_shape=shape((2 * heads * GRAIN, width), BF),
        scratch_shapes=[pltpu.SemaphoreType.DMA((2 * heads,))],
        compiler_params=params(),
        cost_estimate=cost(1),
        name="piece_heads",
    )(place, *weights)


def piece_feed_kernel(place, wu, wd, rest, turned, piece_up, piece_down):
    core, plane = place[0], place[1]
    sub = piece_down.shape[1]
    turned[...] = wu[...].astype(F32).T.astype(BF)
    start = pl.multiple_of((core * 4 + plane) * sub, GRAIN)
    for r in range(piece_up.shape[0]):
        piece_up[r, :sub, :] = turned[pl.ds(start, sub), :]
        piece_up[r, sub:, :] = rest[...]
        piece_down[r] = wd[pl.ds(start, sub), :]


def piece_feed(place, wu, wd, rest, n_mp):
    width, hidden = wu.shape
    sub = hidden // 8
    return pl.pallas_call(
        piece_feed_kernel,
        in_specs=[scalar_spec()] + [held_spec()] * 3,
        out_specs=[held_spec()] * 3,
        out_shape=[
            shape((hidden, width), BF),
            shape((n_mp, sub + GRAIN, width), BF),
            shape((n_mp, sub, width), BF),
        ],
        compiler_params=params(),
        cost_estimate=cost(3),
        name="piece_feed",
    )(place, wu, wd, rest)


def finish_feed_kernel(place, mine, other, up, down, held):
    core = place[0]
    sub = mine.shape[1] // 2
    for c, ref in enumerate((mine, other)):
        for g in range(4):
            start = pl.multiple_of(((core ^ c) * 4 + g) * sub, GRAIN)
            held[pl.ds(start, sub), :] = ref[g, :sub, :].astype(F32)
            down[pl.ds(start, sub), :] = ref[g, sub:, :].astype(F32)
    up[...] = held[...].T


def finish_feed(place, pieces, *tokens):
    _, rows, width = pieces[0].shape
    return pl.pallas_call(
        finish_feed_drop,
        in_specs=[scalar_spec()] + [held_spec()] * 2 + [token_spec() for _ in tokens],
        out_specs=[held_spec()] * 2,
        out_shape=[shape((width, 4 * rows), F32), shape((4 * rows, width), F32)],
        scratch_shapes=[pltpu.VMEM((4 * rows, width), F32)],
        compiler_params=params(),
        cost_estimate=cost(6),
        name="finish_feed",
    )(place, *pieces, *tokens)


def finish_feed_drop(place, mine, other, *refs):
    finish_feed_kernel(place, mine, other, *refs[-3:])


def finish_heads_kernel(place, mine, other, *outs):
    core = place[0]
    heads = outs[0].shape[0] // HEAD_DIM
    for side in range(2):

        @pl.when(core == side)
        def _():
            for c, ref in enumerate((mine, other)):
                for t in range(2):
                    out = outs[2 * (side ^ c) + t]
                    for g in range(4):
                        for h in range(heads):
                            at = h * HEAD_DIM + g * GRAIN
                            row = (t * heads + h) * GRAIN
                            out[at : at + GRAIN, :] = ref[g, row : row + GRAIN, :].astype(F32)


def finish_heads(place, pieces):
    _, rows, width = pieces[0].shape
    local = rows // (2 * GRAIN) * HEAD_DIM
    return pl.pallas_call(
        finish_heads_kernel,
        in_specs=[scalar_spec()] + [held_spec()] * 2,
        out_specs=[held_spec()] * 4,
        out_shape=[shape((local, width), F32)] * 4,
        compiler_params=params(),
        cost_estimate=cost(2),
        name="finish_heads",
    )(place, *pieces)


def turn_swap(block, bits, n_dp):
    return lax.ppermute(block, "dp", [(i, i ^ bits[i & 1]) for i in range(n_dp)])


def first_swap(block, n_dp):
    return turn_swap(block, (XBIT, YBIT), n_dp)


def second_swap(block, n_dp):
    return turn_swap(block, (YBIT, XBIT), n_dp)


def core_swap(block, n_dp):
    return swap(block, "dp", CORE, n_dp)


def exchange(block, axis, groups=None):
    return lax.all_to_all(block, axis, 0, 0, axis_index_groups=groups, tiled=True)


def spread(block, n):
    return jnp.broadcast_to(block[None], (n, *block.shape))


def plane_groups(n_dp):
    return [[8 * e + 2 * g + c for g in range(4)] for e in range(n_dp // 8) for c in range(2)]


def add(*terms):
    total = terms[0].astype(F32)
    for term in terms[1:]:
        total = total + term.astype(F32)
    return total.astype(BF)


def chip_sum(keep, got):
    return add(keep[0::2], got[0::2]), add(keep[1::2], got[1::2])


def side_sum(stay, got):
    return add(stay[0], got[0]), add(stay[1], got[1])


def shard_swap(parts, n_mp):
    shard = lax.axis_index("mp")
    return [
        swap(lax.dynamic_index_in_dim(parts, shard ^ r, 0, keepdims=False), "mp", r, n_mp)
        for r in range(1, n_mp)
    ]


def shard_sum(own, got, n_dp):
    total = own.astype(F32)
    for part in got:
        total = total + part.astype(F32)
    bit = 8
    while bit < n_dp:
        total = total + swap(total, "dp", bit, n_dp)
        bit *= 2
    return total.astype(BF)


def plane_gather(four, n_dp):
    return exchange(four, "dp", plane_groups(n_dp))


def project_kernel(place, x, wq, wk, wv, wo, bq, bv, *refs):
    pieces, (q, k, v, out, full, sems, sem) = refs[:8], refs[-7:]
    last = pltpu.make_async_copy(full, out, sem)
    core, plane, shard = place[0], place[1], place[2]
    heads = wq.shape[0] // HEAD_DIM
    shards = 1 + pieces[0].shape[0] // (2 * heads * GRAIN)

    @pl.when(pl.program_id(0) == 0)
    def _():
        copies = []
        base = pl.multiple_of(shard * heads * HEAD_DIM, HEAD_DIM)
        for kind, ref in enumerate((wq, wk, wv, wo)):
            for h in range(heads):
                for g in range(4):
                    source = plane ^ neighbour(kind // 2, g)
                    at = pl.multiple_of(h * HEAD_DIM + source * GRAIN, GRAIN)
                    to = pl.multiple_of(base + h * HEAD_DIM + g * GRAIN, GRAIN)
                    copies.append(
                        pltpu.make_async_copy(
                            ref.at[pl.ds(at, GRAIN), :],
                            full.at[kind, pl.ds(to, GRAIN), :],
                            sems.at[len(copies)],
                        )
                    )
        for copy in copies:
            copy.start()
        for c in range(2):
            for g, ref in enumerate(pieces[4 * c : 4 * c + 4]):
                for r in range(1, shards):
                    base = pl.multiple_of((shard ^ r) * heads * HEAD_DIM, HEAD_DIM)
                    for t in range(2):
                        for h in range(heads):
                            row = (((r - 1) * 2 + t) * heads + h) * GRAIN
                            to = pl.multiple_of(base + h * HEAD_DIM + g * GRAIN, GRAIN)
                            full[(core ^ c) * 2 + t, pl.ds(to, GRAIN), :] = ref[
                                row : row + GRAIN, :
                            ]
        for copy in copies:
            copy.wait()
        last.start()

    block = x[...]
    for kind, (into, bias) in enumerate(((q, bq), (k, None), (v, bv))):
        value = lax.dot_general(block, full[kind], NT, preferred_element_type=F32)
        if bias is not None:
            value = value + bias[...]
        into[...] = value.astype(BF)

    @pl.when(pl.program_id(0) == pl.num_programs(0) - 1)
    def _():
        last.wait()


def project(place, x, weights, bq, bv, pieces, *tokens):
    rows, width = x.shape
    block = rows_spec(ROW_BLOCK, width)
    return pl.pallas_call(
        project_kernel,
        grid=(rows // ROW_BLOCK,),
        in_specs=[scalar_spec(), block]
        + [token_spec()] * 4
        + [whole_spec(a.shape) for a in (bq, bv, *pieces)]
        + [token_spec() for _ in tokens],
        out_specs=[block, block, block, token_spec()],
        out_shape=[shape((rows, width), BF)] * 3 + [shape((4, width, width), BF)],
        scratch_shapes=[
            pltpu.VMEM((4, width, width), BF),
            pltpu.SemaphoreType.DMA((weights[0].shape[0] // GRAIN * 4,)),
            pltpu.SemaphoreType.DMA,
        ],
        compiler_params=params(),
        cost_estimate=cost(10),
        name="project",
    )(place, x, *weights, bq, bv, *pieces, *tokens)


def spread_heads(block):
    lane = lax.broadcasted_iota(jnp.int32, block.shape, 1) // HEAD_DIM
    return jnp.concatenate(
        [jnp.where(lane == h, block, jnp.zeros_like(block)) for h in range(4)], axis=0
    )


def gather_heads(stacked):
    rows = stacked.shape[0] // 4
    lane = lax.broadcasted_iota(jnp.int32, (rows, GROUP), 1) // HEAD_DIM
    out = stacked[:rows]
    for h in range(1, 4):
        out = jnp.where(lane == h, stacked[h * rows : (h + 1) * rows], out)
    return out


def window_start(step, rows):
    return pl.multiple_of(jnp.clip(step - 1, 0, (rows - WINDOW) // BLOCK) * BLOCK, BLOCK)


def attend_kernel(part, q, k, v, segc, segr, x, wo, bo, gain, shift, *refs):
    ctx, saved, unit, low = refs[-4:]
    start = window_start(part * pl.num_programs(0) + pl.program_id(0), k.shape[0])
    near = pl.ds(start, WINDOW)
    penalty = jnp.where(segc[...] == segr[:, near], 0.0, MASKED)
    lane = lax.broadcasted_iota(jnp.int32, (BLOCK, 128), 1)
    groups = q.shape[1] // GROUP

    def score_group(group):
        cols = slice(group * GROUP, (group + 1) * GROUP)
        return lax.dot_general(
            spread_heads(q[:, cols] * SCALE), k[near, cols], NT, preferred_element_type=F32
        )

    keep = jnp.zeros((BLOCK, 128), F32)
    ahead = score_group(0)
    for group in range(groups):
        cols = slice(group * GROUP, (group + 1) * GROUP)
        logits = ahead.reshape(4, BLOCK, WINDOW) + penalty[None]
        if group + 1 < groups:
            ahead = score_group(group + 1)
        peak = jnp.max(logits, axis=-1, keepdims=True)
        raised = jnp.exp(logits - peak)
        sums = jnp.sum(raised, axis=-1, keepdims=True)
        context = jnp.dot(
            raised.astype(BF).reshape(4 * BLOCK, WINDOW), v[near, cols], preferred_element_type=F32
        )
        context = (context.reshape(4, BLOCK, GROUP) * (1.0 / sums)).reshape(4 * BLOCK, GROUP)
        ctx[:, cols] = gather_heads(context).astype(BF)
        log_total = peak + jnp.log(sums)
        for h in range(4):
            keep = jnp.where(lane == group * 4 + h, log_total[h], keep)
    attended = jnp.dot(ctx[...], wo[0], preferred_element_type=F32) + bo[...]
    total = x[...].astype(F32) + attended
    centred = total - jnp.mean(total, axis=-1, keepdims=True)
    inv_std = lax.rsqrt(jnp.mean(centred * centred, axis=-1, keepdims=True) + EPSILON)
    unit_val = centred * inv_std
    unit[...] = unit_val
    low[...] = (unit_val * gain[...] + shift[...]).astype(BF)
    saved[...] = jnp.where(lane == 127, inv_std, keep)


def attend(part, parts, q, k, v, segc, segr, x, full, bo, gain, shift, held, *tokens):
    rows, width = q.shape
    steps = rows // BLOCK // parts

    def block(wide):
        return pl.BlockSpec((BLOCK, wide), lambda i: (part * steps + i, 0))

    return pl.pallas_call(
        functools.partial(attend_kernel, part),
        grid=(steps,),
        in_specs=[
            block(width),
            whole_spec((rows, width)),
            whole_spec((rows, width)),
            block(1),
            whole_spec((1, rows)),
            block(width),
            pl.BlockSpec((1, width, width), lambda i: (3, 0, 0), pipeline_mode=pl.Buffered(1)),
            whole_spec((1, width)),
            whole_spec((1, width)),
            whole_spec((1, width)),
        ]
        + [token_spec() for _ in (*held, *tokens)],
        out_specs=[block(width), block(128), block(width), block(width)],
        out_shape=[
            shape((rows, width), BF),
            shape((rows, 128), F32),
            shape((rows, width), F32),
            shape((rows, width), BF),
        ],
        input_output_aliases={10 + i: i for i in range(len(held))},
        compiler_params=params(),
        cost_estimate=cost(16 / parts),
        name="attend",
    )(q, k, v, segc, segr, x, full, bo, gain, shift, *held, *tokens)


def whole_order(rows, plane):
    width = rows.shape[1]
    rank = (lax.broadcasted_iota(jnp.int32, rows.shape, 1) // GRAIN) % 4
    row = lax.broadcasted_iota(jnp.int32, rows.shape, 0)

    def shifted(block, by):
        return pltpu.roll(block, by % width, 1)

    middle = jnp.where(rank == 1, shifted(rows, -GRAIN), shifted(rows, GRAIN))
    swapped = (row == 7) & ((rank == 1) | (rank == 2))
    rows = jnp.where(swapped, middle, rows)
    for bit in (1, 2):
        by = bit * GRAIN
        other = jnp.where((rank & bit) == 0, shifted(rows, -by), shifted(rows, by))
        rows = jnp.where((plane & bit) == 0, rows, other)
    return rows


def attend_back_kernel(place, q, k, v, do, saved, inner, segc, segr, *refs):
    dq, dk, dv, sums, dk_sum, dv_sum = refs[-6:]
    step = pl.program_id(0)

    @pl.when(step == 0)
    def _():
        dk_sum[...] = jnp.zeros_like(dk_sum)
        dv_sum[...] = jnp.zeros_like(dv_sum)
        sums[...] = jnp.zeros_like(sums)

    start = window_start(step, k.shape[0])
    near = pl.ds(start, WINDOW)
    penalty = jnp.where(segc[...] == segr[:, near], 0.0, MASKED)
    for group in range(q.shape[1] // GROUP):
        cols = slice(group * GROUP, (group + 1) * GROUP)
        q4 = spread_heads(q[:, cols] * SCALE)
        do4 = spread_heads(do[:, cols])
        k4 = k[near, cols]
        logits = lax.dot_general(q4, k4, NT, preferred_element_type=F32)
        logits = logits.reshape(4, BLOCK, WINDOW) + penalty[None]
        lse = jnp.stack([saved[:, group * 4 + h : group * 4 + h + 1] for h in range(4)])
        mean_grad = jnp.stack([inner[:, group * 4 + h : group * 4 + h + 1] for h in range(4)])
        probs = jnp.exp(logits - lse)
        weight_grad = lax.dot_general(
            do4, v[near, cols], NT, preferred_element_type=F32
        ).reshape(4, BLOCK, WINDOW)
        logit_grad = (probs * (weight_grad - mean_grad)).astype(BF).reshape(4 * BLOCK, WINDOW)
        probs_low = probs.astype(BF).reshape(4 * BLOCK, WINDOW)
        dq_low = (
            gather_heads(jnp.dot(logit_grad, k4, preferred_element_type=F32)) * SCALE
        ).astype(BF)
        dq[:, cols] = dq_low
        sums[6:7, cols] += jnp.sum(dq_low.astype(F32), axis=0, keepdims=True)
        dk_sum[near, cols] += lax.dot_general(logit_grad, q4, TN, preferred_element_type=F32)
        dv_sum[near, cols] += lax.dot_general(probs_low, do4, TN, preferred_element_type=F32)

    @pl.when(step == pl.num_programs(0) - 1)
    def _():
        dk[...] = dk_sum[...].astype(BF)
        dv_low = dv_sum[...].astype(BF)
        dv[...] = dv_low
        sums[7:8, :] = jnp.sum(dv_low.astype(F32), axis=0, keepdims=True)
        sums[...] = whole_order(sums[...], place[1])


def attend_back(place, q, k, v, do, saved, inner, segc, segr, *tokens):
    rows, width = q.shape
    block = rows_spec(BLOCK, width)
    full = whole_spec((rows, width))
    return pl.pallas_call(
        attend_back_kernel,
        grid=(rows // BLOCK,),
        in_specs=[
            scalar_spec(),
            block,
            full,
            full,
            block,
            rows_spec(BLOCK, 128),
            rows_spec(BLOCK, 128),
            rows_spec(BLOCK, 1),
            whole_spec((1, rows)),
        ]
        + [token_spec() for _ in tokens],
        out_specs=[block, fixed_spec((rows, width)), fixed_spec((rows, width)), fixed_spec((8, width))],
        out_shape=[shape((rows, width), BF)] * 3 + [shape((8, width), F32)],
        scratch_shapes=[pltpu.VMEM((rows, width), F32)] * 2,
        compiler_params=params(),
        cost_estimate=cost(22),
        name="attend_back",
    )(place, q, k, v, do, saved, inner, segc, segr, *tokens)


def assemble(place, own, pieces, into):
    core, plane, shard = place[0], place[1], place[2]
    sub = own.shape[0] // 8
    shards = 1 + pieces[0].shape[0] // sub

    def rows(c, g, r):
        return pl.ds(pl.multiple_of(((c * 4 + g) * shards + (shard ^ r)) * sub, GRAIN), sub)

    for c in range(2):
        for g, ref in enumerate(pieces[4 * c : 4 * c + 4]):
            at = pl.multiple_of(((core ^ c) * 4 + (plane ^ neighbour(core ^ c, g))) * sub, GRAIN)
            into[rows(c, g, 0), :] = own[pl.ds(at, sub), :]
            for r in range(1, shards):
                into[rows(c, g, r), :] = ref[(r - 1) * sub : r * sub, :]


def feed_up_kernel(place, x, own, bu, *refs):
    pieces, (act, slope, out, wu, sem) = refs[:8], refs[-5:]
    copy = pltpu.make_async_copy(wu, out, sem)

    @pl.when(pl.program_id(0) == 0)
    def _():
        assemble(place, own, pieces, wu)
        copy.start()

    block = x[...]
    for at in range(0, wu.shape[0], 256):
        span = slice(at, at + 256)
        pre = (
            lax.dot_general(block, wu[span, :], NT, preferred_element_type=F32) + bu[:, span]
        )
        below = 0.5 * (1.0 + lax.erf(pre * 0.7071067811865476))
        density = jnp.exp(-0.5 * pre * pre) * 0.3989422804014327
        act[:, span] = (pre * below).astype(BF)
        slope[:, span] = (below + pre * density).astype(BF)

    @pl.when(pl.program_id(0) == pl.num_programs(0) - 1)
    def _():
        copy.wait()


def feed_up(place, x, own, bu, pieces, *tokens):
    rows, width = x.shape
    hidden = bu.shape[1]
    wide = rows_spec(ROW_BLOCK, hidden)
    return pl.pallas_call(
        feed_up_kernel,
        grid=(rows // ROW_BLOCK,),
        in_specs=[scalar_spec(), rows_spec(ROW_BLOCK, width)]
        + [whole_spec(a.shape) for a in (own, bu, *pieces)]
        + [token_spec() for _ in tokens],
        out_specs=[wide, wide, token_spec()],
        out_shape=[shape((rows, hidden), BF)] * 2 + [shape((hidden, width), BF)],
        scratch_shapes=[pltpu.VMEM((hidden, width), BF), pltpu.SemaphoreType.DMA],
        compiler_params=params(),
        cost_estimate=cost(12),
        name="feed_up",
    )(place, x, own, bu, *pieces, *tokens)


def feed_down_kernel(place, act, unit, cot, own, vectors, *refs):
    pieces, outs = refs[:8], refs[-8:]
    layer, output, second, down_grad, sums, out, wd, sem = outs
    copy = pltpu.make_async_copy(wd, out, sem)

    @pl.when(pl.program_id(0) == 0)
    def _():
        sums[...] = jnp.zeros_like(sums)
        assemble(place, own, pieces, wd)
        copy.start()

    down = jnp.dot(act[...], wd[...], preferred_element_type=F32)
    b_down, first_gain, first_shift, second_gain, second_shift = (
        vectors[i : i + 1, :] for i in range(5)
    )
    total = unit[...] * first_gain + first_shift + down + b_down
    centred = total - jnp.mean(total, axis=-1, keepdims=True)
    inv_std = lax.rsqrt(jnp.mean(centred * centred, axis=-1, keepdims=True) + EPSILON)
    unit_val = centred * inv_std
    layer_out = unit_val * second_gain + second_shift
    layer[...] = layer_out
    output[...] = layer_out.astype(BF)
    grad = cot[...].astype(F32)
    scaled = grad * second_gain
    inner = (
        scaled
        - jnp.mean(scaled, axis=-1, keepdims=True)
        - unit_val * jnp.mean(scaled * unit_val, axis=-1, keepdims=True)
    )
    second_grad = inv_std * inner
    second[...] = second_grad
    grad_low = second_grad.astype(BF)
    down_grad[...] = grad_low
    sums[3:4, :] += jnp.sum(grad_low.astype(F32), axis=0, keepdims=True)
    sums[4:5, :] += jnp.sum(grad * unit_val, axis=0, keepdims=True)
    sums[5:6, :] += jnp.sum(grad, axis=0, keepdims=True)

    @pl.when(pl.program_id(0) == pl.num_programs(0) - 1)
    def _():
        copy.wait()


def feed_down(place, act, unit, cot, own, vectors, pieces):
    rows, hidden = act.shape
    width = unit.shape[1]
    block = rows_spec(ROW_BLOCK, width)
    return pl.pallas_call(
        feed_down_kernel,
        grid=(rows // ROW_BLOCK,),
        in_specs=[scalar_spec(), rows_spec(ROW_BLOCK, hidden), block, block]
        + [whole_spec(a.shape) for a in (own, vectors, *pieces)],
        out_specs=[block, block, block, block, fixed_spec((8, width)), token_spec()],
        out_shape=[
            shape((rows, width), F32),
            shape((rows, width), BF),
            shape((rows, width), F32),
            shape((rows, width), BF),
            shape((8, width), F32),
            shape((hidden, width), BF),
        ],
        scratch_shapes=[pltpu.VMEM((hidden, width), BF), pltpu.SemaphoreType.DMA],
        compiler_params=params(),
        cost_estimate=cost(13),
        name="feed_down",
    )(place, act, unit, cot, own, vectors, *pieces)


def feed_back_kernel(grad, x, wu, wd, slope, act, keep, send, bias, out, held):
    step = pl.program_id(0)
    half = pl.num_programs(0) // 2
    chips, shards, _, sub, width = keep.shape

    @pl.when(step == 0)
    def _():
        out[...] = jnp.zeros_like(out)
        bias[...] = jnp.zeros_like(bias)

    total = None
    for at in range(0, x.shape[0], ROW_BLOCK):
        span = slice(at, at + ROW_BLOCK)
        act_grad = lax.dot_general(grad[span, :], wd[...], NT, preferred_element_type=F32)
        low = (act_grad * slope[span, :].astype(F32)).astype(BF)
        held[span, :] = low
        term = jnp.sum(low.astype(F32), axis=0, keepdims=True)
        total = term if total is None else total + term
    for block in range(4):

        @pl.when(step == (block + 2) % 4)
        def _():
            for g in range(chips):
                for r in range(shards):
                    at = (g * shards + r) * sub
                    row = block * chips + g
                    bias[row : row + 1, r * 128 : r * 128 + sub] = total[:, at : at + sub]

    out[...] += jnp.dot(held[...], wu[...], preferred_element_type=F32)
    dims = (chips, shards, sub, width)
    up = lax.dot_general(held[...], x[...], TN, preferred_element_type=F32).astype(BF)
    down = lax.dot_general(act[...], grad[...], TN, preferred_element_type=F32).astype(BF)

    @pl.when(step < half)
    def _():
        send[:, :, 0] = up.reshape(dims)
        send[:, :, 1] = down.reshape(dims)

    @pl.when(step >= half)
    def _():
        keep[:, :, 0] = up.reshape(dims)
        keep[:, :, 1] = down.reshape(dims)


def feed_back(grad, x, wu, wd, slope, act, n_mp):
    rows, width = x.shape
    hidden = wu.shape[0]
    span = hidden // 4
    full = whole_spec((rows, width))
    weight = pl.BlockSpec((span, width), lambda j: ((j + 2) % 4, 0))
    wide = pl.BlockSpec((rows, span), lambda j: (0, (j + 2) % 4))
    dims = (4, n_mp, 2, hidden // 8 // n_mp, width)
    block = (2, *dims[1:])
    return pl.pallas_call(
        feed_back_kernel,
        grid=(4,),
        in_specs=[full, full, weight, weight, wide, wide],
        out_specs=[
            pl.BlockSpec(block, lambda j: (jnp.maximum(j - 2, 0), 0, 0, 0, 0)),
            pl.BlockSpec(block, lambda j: (jnp.minimum(j, 1), 0, 0, 0, 0)),
            fixed_spec((8, 128 * n_mp)),
            fixed_spec((rows, width)),
        ],
        out_shape=[
            shape(dims, BF),
            shape(dims, BF),
            shape((8, 128 * n_mp), F32),
            shape((rows, width), F32),
        ],
        scratch_shapes=[pltpu.VMEM((rows, span), BF)],
        compiler_params=params(),
        cost_estimate=cost(27),
        name="feed_back",
    )(grad, x, wu, wd, slope, act)


def middle_kernel(normed, second, unit, saved, ctx, wo, gain, *refs):
    first, context_grad, inner_sum, weight, sums, held = refs[-6:]
    step = pl.program_id(0)
    grad = normed[...] + second[...]
    unit_val = unit[...]
    scaled = grad * gain[...]
    inner = (
        scaled
        - jnp.mean(scaled, axis=-1, keepdims=True)
        - unit_val * jnp.mean(scaled * unit_val, axis=-1, keepdims=True)
    )
    first_grad = saved[:, 127:128] * inner
    first[...] = first_grad
    low = first_grad.astype(BF)
    context_low = lax.dot_general(low, wo[0], NT, preferred_element_type=F32).astype(BF)
    context_grad[...] = context_low
    product = context_low.astype(F32) * ctx[...].astype(F32)
    high = product.astype(BF)
    rest = (product - high.astype(F32)).astype(BF)
    width = product.shape[1]
    head = lax.broadcasted_iota(jnp.int32, (width, 128), 0) // HEAD_DIM
    head = (head == lax.broadcasted_iota(jnp.int32, (width, 128), 1)).astype(BF)
    inner_sum[...] = jnp.dot(high, head, preferred_element_type=F32) + jnp.dot(
        rest, head, preferred_element_type=F32
    )
    term = lax.dot_general(ctx[...], low, TN, preferred_element_type=F32)

    @pl.when(step == 0)
    def _():
        sums[...] = jnp.zeros_like(sums)
        held[...] = jnp.zeros_like(held)

    held[...] += term
    sums[0:1, :] += jnp.sum(low.astype(F32), axis=0, keepdims=True)
    sums[1:2, :] += jnp.sum(grad * unit_val, axis=0, keepdims=True)
    sums[2:3, :] += jnp.sum(grad, axis=0, keepdims=True)

    @pl.when(step == pl.num_programs(0) - 1)
    def _():
        weight[...] = held[...].astype(BF)


def middle(normed, second, unit, saved, ctx, full, gain, *tokens):
    rows, width = normed.shape
    block = rows_spec(ROW_BLOCK, width)
    return pl.pallas_call(
        middle_kernel,
        grid=(rows // ROW_BLOCK,),
        in_specs=[
            block,
            block,
            block,
            rows_spec(ROW_BLOCK, 128),
            block,
            pl.BlockSpec((1, width, width), lambda i: (3, 0, 0), pipeline_mode=pl.Buffered(1)),
            whole_spec((1, width)),
        ]
        + [token_spec() for _ in tokens],
        out_specs=[block, block, rows_spec(ROW_BLOCK, 128), fixed_spec((width, width)), fixed_spec((8, width))],
        out_shape=[
            shape((rows, width), F32),
            shape((rows, width), BF),
            shape((rows, 128), F32),
            shape((width, width), BF),
            shape((8, width), F32),
        ],
        scratch_shapes=[pltpu.VMEM((width, width), F32)],
        compiler_params=params(),
        cost_estimate=cost(8),
        name="middle",
    )(normed, second, unit, saved, ctx, full, gain, *tokens)


def head_weights_kernel(place, dq, dk, dv, x, wo, *refs):
    keep, send, held = refs[-3:]
    core = place[0]
    shards, heads = keep.shape[1], keep.shape[3]
    for kind in range(4):
        if kind < 3:
            held[...] = lax.dot_general(
                (dq, dk, dv)[kind][...], x[...], TN, preferred_element_type=F32
            ).astype(BF)
        source = held if kind < 3 else wo
        for side in range(2):

            @pl.when(core == side)
            def _():
                out = keep if side == kind // 2 else send
                for r in range(shards):
                    for h in range(heads):
                        for g in range(4):
                            at = (r * heads + h) * HEAD_DIM + g * GRAIN
                            out[g, r, kind % 2, h] = source[at : at + GRAIN, :]


def head_weights(place, dq, dk, dv, x, wo, n_mp, *tokens):
    rows, width = x.shape
    heads = width // HEAD_DIM // n_mp
    dims = (4, n_mp, 2, heads, GRAIN, width)
    keep, send = pl.pallas_call(
        head_weights_kernel,
        in_specs=[scalar_spec()] + [held_spec()] * 5 + [token_spec() for _ in tokens],
        out_specs=[held_spec()] * 2,
        out_shape=[shape(dims, BF)] * 2,
        scratch_shapes=[pltpu.VMEM((width, width), BF)],
        compiler_params=params(),
        cost_estimate=cost(8),
        name="head_weights",
    )(place, dq, dk, dv, x, wo, *tokens)
    dims = (4, n_mp, 2 * heads * GRAIN, width)
    return keep.reshape(dims), send.reshape(dims)


def input_kernel(dq, dk, dv, full, first, *refs):
    out = refs[-1]
    total = first[...]
    for kind, ref in enumerate((dq, dk, dv)):
        total = total + jnp.dot(ref[...], full[kind], preferred_element_type=F32)
    out[...] = total


def input_gradient(dq, dk, dv, full, first, *tokens):
    rows, width = dq.shape
    block = rows_spec(ROW_BLOCK, width)
    return pl.pallas_call(
        input_kernel,
        grid=(rows // ROW_BLOCK,),
        in_specs=[
            block,
            block,
            block,
            pl.BlockSpec((3, width, width), lambda i: (0, 0, 0), pipeline_mode=pl.Buffered(1)),
            block,
        ]
        + [token_spec() for _ in tokens],
        out_specs=block,
        out_shape=shape((rows, width), F32),
        compiler_params=params(),
        cost_estimate=cost(6),
        name="input_gradient",
    )(dq, dk, dv, full, first, *tokens)


def score_kernel(out_ref, segr_ref, len_ref, table_ref, pick_ref, *refs):
    score_ref = refs[-1]
    queries = pick_ref.shape[0]
    rows = out_ref.shape[0]
    label = lax.broadcasted_iota(jnp.int32, (queries, rows), 0)
    onehot = (label == segr_ref[...]).astype(F32)
    sums = jnp.dot(
        onehot, out_ref[...], precision=lax.Precision.HIGHEST, preferred_element_type=F32
    )
    means = sums / len_ref[...].astype(F32)
    every = lax.dot_general(
        means,
        table_ref[...].astype(F32),
        NT,
        precision=lax.Precision.HIGHEST,
        preferred_element_type=F32,
    )
    at = lax.broadcasted_iota(jnp.int32, every.shape, 1)
    column = lax.broadcasted_iota(jnp.int32, pick_ref.shape, 1)
    result = jnp.zeros(pick_ref.shape, F32)
    for p in range(pick_ref.shape[1]):
        chosen = jnp.sum(
            jnp.where(at == pick_ref[:, p : p + 1], every, 0.0), axis=1, keepdims=True
        )
        result = jnp.where(column == p, chosen, result)
    score_ref[...] = result


def score(layer_out, segr, lengths, table, picks, *tokens):
    return pl.pallas_call(
        score_kernel,
        in_specs=[held_spec()] * 5 + [token_spec() for _ in tokens],
        out_specs=held_spec(),
        out_shape=shape(picks.shape, F32),
        compiler_params=params(),
        cost_estimate=cost(8),
        name="score",
    )(layer_out, segr, lengths, table, picks, *tokens)


def per_device(
    n_dp,
    n_mp,
    hidden_in,
    cotangent,
    query_lengths,
    passage_index,
    passages,
    w_query,
    w_key,
    w_value,
    w_output,
    w_up,
    w_down,
    b_query,
    b_value,
    b_output,
    b_up,
    b_down,
    first_gain,
    first_shift,
    second_gain,
    second_shift,
):
    rows, width = hidden_in.shape
    heads = w_query.shape[1] // HEAD_DIM
    sub = w_up.shape[1] // 8
    at_dp = lax.axis_index("dp")
    core, plane = at_dp & 1, (at_dp >> 1) & 3
    shard = lax.axis_index("mp")
    place = jnp.stack([core, plane, shard]).astype(jnp.int32)
    own_heads = (w_query.T, w_key.T, w_value.T, w_output)

    cut = heads * HEAD_DIM
    heads_piece = piece_heads(place, *own_heads)
    bias_rows = jnp.stack(
        [jnp.pad(b_query, (0, width - cut)), jnp.pad(b_value, (0, width - cut)), b_up]
    )
    turned, up_piece, down_piece = piece_feed(
        place, w_up, w_down, after(jnp.pad(bias_rows, ((0, GRAIN - 3), (0, 0))), heads_piece), n_mp
    )
    heads_parts = [swap(after(heads_piece, down_piece), "mp", 1, n_mp)] + [
        swap(heads_piece, "mp", r, n_mp) for r in range(2, n_mp)
    ]
    up_got = exchange(up_piece, "mp")
    heads_shards = jnp.concatenate(heads_parts)
    heads_first = first_swap(heads_shards, n_dp)
    heads_second = second_swap(heads_shards, n_dp)
    heads_corner = second_swap(after(heads_first, heads_second), n_dp)
    heads_other = [core_swap(p, n_dp) for p in (heads_shards, heads_first, heads_second)]
    heads_corner, up_got = lax.optimization_barrier((heads_corner, up_got))
    heads_mine = [heads_shards, heads_first, heads_second, heads_corner]
    heads_other = heads_other + [core_swap(heads_corner, n_dp)]

    def others(got):
        return jnp.concatenate(
            [
                lax.dynamic_index_in_dim(got, shard ^ r, 0, keepdims=False)[:sub]
                for r in range(1, n_mp)
            ]
        )

    up_shards = others(after(up_got, *heads_mine, *heads_other))
    up_first = first_swap(up_shards, n_dp)
    up_second = second_swap(up_shards, n_dp)
    down_got = exchange(after(down_piece, up_got), "mp")

    ranks = lax.broadcasted_iota(jnp.int32, (4, 4), 0)
    places4 = lax.broadcasted_iota(jnp.int32, (4, 4), 1)
    turned_ranks = jnp.where((ranks == 1) | (ranks == 2), ranks ^ 3, ranks)
    order_q = ((plane ^ ranks) == places4).astype(F32)
    order_v = ((plane ^ turned_ranks) == places4).astype(F32)
    owner = (core ^ jnp.arange(2, dtype=jnp.int32)).reshape(2, 1, 1, 1)
    is_owner = (owner == jnp.arange(2, dtype=jnp.int32).reshape(1, 1, 2, 1)).astype(F32)
    order_up = jnp.where(owner == 0, order_q[None, :, None], order_v[None, :, None])
    order_up = (order_up * is_owner).reshape(8, 8)
    exact = functools.partial(
        jnp.einsum, precision=lax.Precision.HIGHEST, preferred_element_type=F32
    )
    all_bias = up_got[:, sub : sub + 3].astype(F32)
    by_head = (n_mp, heads, 4, GRAIN)
    query_bias = exact("gk,zhki->zhgi", order_q, all_bias[:, 0, :cut].reshape(by_head))
    value_bias = exact("gk,zhki->zhgi", order_v, all_bias[:, 1, :cut].reshape(by_head))
    up_bias = exact("gk,zki->gzi", order_up, all_bias[:, 2].reshape(n_mp, 8, sub))
    query_bias, value_bias, up_bias = (
        b.reshape(1, -1) for b in (query_bias, value_bias, up_bias)
    )

    ends = jnp.cumsum(query_lengths, axis=-1, dtype=jnp.int32)
    places = lax.broadcasted_iota(jnp.int32, (rows, query_lengths.shape[1]), 0)
    seg = jnp.sum((places >= ends).astype(jnp.int32), axis=-1)
    segc, segr = seg.reshape(rows, 1), seg.reshape(1, rows)
    vectors = jnp.stack(
        [b_down, first_gain, first_shift, second_gain, second_shift, b_output, b_output, b_output]
    ).astype(F32)

    query, key, value, full = project(
        place, hidden_in, own_heads, query_bias, value_bias, heads_mine + heads_other
    )
    up_first, up_second, down_got, query = lax.optimization_barrier(
        (up_first, up_second, down_got, query)
    )
    up_corner = second_swap(up_first, n_dp)
    up_mine = [up_shards, up_first, up_second]
    up_other = [core_swap(p, n_dp) for p in up_mine]
    down_shards = others(down_got)
    down_first = first_swap(down_shards, n_dp)
    down_second = second_swap(down_shards, n_dp)
    held = attend(
        0, 2, query, key, value, segc, segr, hidden_in, full,
        vectors[5:6], vectors[1:2], vectors[2:3], (), down_shards,
    )
    up_corner, down_first, down_second, *held = lax.optimization_barrier(
        (up_corner, down_first, down_second, *held)
    )
    up_pieces = up_mine + [up_corner] + up_other + [core_swap(up_corner, n_dp)]
    down_corner = second_swap(down_first, n_dp)
    down_mine = [down_shards, down_first, down_second]
    context, saved, unit, low = attend(
        1, 2, query, key, value, segc, segr, hidden_in, full,
        vectors[5:6], vectors[1:2], vectors[2:3], held,
    )
    down_corner, low = lax.optimization_barrier((down_corner, low))
    down_mine = down_mine + [down_corner]
    down_pieces = down_mine + [core_swap(p, n_dp) for p in down_mine]
    act, slope, wu = feed_up(place, low, turned, up_bias, up_pieces, down_corner)
    layer_out, output, second_grad, down_grad, second_sums, wd = feed_down(
        place, act, unit, cotangent, w_down, vectors, down_pieces
    )

    feed_keep, feed_send, up_sums, normed = feed_back(
        down_grad, low, wu, wd, slope, act, n_mp
    )
    dims = (4, n_mp, 2 * sub, width)
    feed_keep = feed_keep.reshape(dims)
    got = core_swap(feed_send.reshape(dims), n_dp)
    first_grad, context_grad, inner, wo_grad, first_sums = middle(
        normed, second_grad, unit, saved, context, full, vectors[1:2]
    )
    got, context_grad = lax.optimization_barrier((got, context_grad))
    feed_stay, feed_go = chip_sum(feed_keep, got)
    got = first_swap(feed_go, n_dp)
    dq, dk, dv, head_sums = attend_back(
        place, query, key, value, context_grad, saved, inner, segc, segr, feed_go
    )
    got, head_sums = lax.optimization_barrier((got, head_sums))
    feed_own, feed_go = side_sum(feed_stay, got)
    got = second_swap(feed_go, n_dp)
    every = jnp.concatenate(
        [second_sums + first_sums + head_sums, exact("sk,si->ki", order_up, up_sums)], axis=1
    )
    vector_got = swap(every, "mp", 1, n_mp)
    heads_keep, heads_send = head_weights(
        place, dq, dk, dv, hidden_in, wo_grad, n_mp, every, feed_go
    )
    got, heads_keep = lax.optimization_barrier((got, heads_keep))
    feed_parts = add(feed_own, got)
    heads_got = core_swap(after(heads_send, feed_parts), n_dp)
    feed_got = exchange(feed_parts, "mp")
    heads_stay, heads_go = chip_sum(heads_keep, heads_got)
    heads_got = first_swap(heads_go, n_dp)
    every = every + after(vector_got, heads_go)
    vector_got = core_swap(every, n_dp)
    input_grad = input_gradient(dq, dk, dv, full, first_grad, heads_go, every)
    heads_got, vector_got, input_grad = lax.optimization_barrier(
        (heads_got, vector_got, input_grad)
    )
    heads_own, heads_go = side_sum(heads_stay, heads_got)
    heads_got = second_swap(heads_go, n_dp)
    every = every + after(vector_got, heads_go)
    bit = 2
    while bit < n_mp:
        vector_got = swap(every, "mp", bit, n_mp)
        bit *= 2
    feed_got, heads_go = lax.optimization_barrier((feed_got, heads_go))
    feed_total = shard_sum(feed_got[0], [feed_got[r] for r in range(1, n_mp)], n_dp)
    feed_four = spread(feed_total, 4)
    feed_mine = plane_gather(feed_four, n_dp)
    heads_got, vector_got, feed_four = lax.optimization_barrier(
        (heads_got, vector_got, feed_four)
    )
    heads_parts = add(heads_own, heads_got)
    heads_got = shard_swap(heads_parts, n_mp)
    heads_own = lax.dynamic_index_in_dim(heads_parts, shard, 0, keepdims=False)
    every = every + after(vector_got, heads_parts)
    vector_got = swap(every, "dp", XBIT, n_dp)
    scores = score(
        layer_out, segr, query_lengths.reshape(-1, 1), passages, passage_index,
        heads_parts, every,
    )
    vector_got, scores = lax.optimization_barrier((vector_got, scores))
    every = every + vector_got
    vector_got = swap(every, "dp", YBIT, n_dp)
    feed_mine, *heads_got = lax.optimization_barrier((feed_mine, *heads_got, scores))[:n_mp]
    heads_total = shard_sum(heads_own, heads_got, n_dp)
    heads_mine = plane_gather(spread(heads_total, 4), n_dp)
    feed_other = core_swap(feed_mine, n_dp)
    every = every + after(vector_got, heads_total)
    bit = 8
    while bit < n_dp:
        every = every + swap(every, "dp", bit, n_dp)
        bit *= 2
    w_up_grad, w_down_grad = finish_feed(place, (feed_mine, feed_other), heads_total, every)
    heads_mine, w_up_grad = lax.optimization_barrier((heads_mine, w_up_grad))
    heads_other = core_swap(heads_mine, n_dp)
    query_t, key_t, value_t, w_output_grad = finish_heads(place, (heads_mine, heads_other))
    shared = every[:6, :width]
    query_sums, value_sums = (
        lax.dynamic_slice_in_dim(every[row, :width], shard * cut, cut) for row in (6, 7)
    )
    up_sums = lax.dynamic_slice_in_dim(every[:, width:], shard * 128, 128, axis=1)
    up_sums = up_sums[:, :sub].reshape(-1)
    return (
        output,
        scores,
        input_grad,
        query_t.T,
        key_t.T,
        value_t.T,
        w_output_grad,
        w_up_grad,
        w_down_grad,
        query_sums,
        value_sums,
        shared[0],
        up_sums,
        shared[3],
        shared[1],
        shared[2],
        shared[4],
        shared[5],
    )


def solution(mesh):
    both, split = P(("dp", "mp"), None), P(None, "mp")
    return jax.shard_map(
        functools.partial(per_device, mesh.shape["dp"], mesh.shape["mp"]),
        mesh=mesh,
        in_specs=(both, both, both, both, P())
        + (split, split, split, P("mp", None), split, P("mp", None))
        + (P("mp"), P("mp"), P(), P("mp"), P(), P(), P(), P(), P()),
        out_specs=(both, both, both)
        + (split, split, split, P("mp", None), split, P("mp", None))
        + (P("mp"), P("mp"), P(), P("mp"), P(), P(), P(), P(), P()),
        check_vma=False,
    )
```

```python
import functools

import jax
import jax.numpy as jnp
from jax import lax
from jax.experimental import pallas as pl
from jax.experimental.pallas import tpu as pltpu
from jax.sharding import PartitionSpec as P

HEAD_DIM = 64
SCALE = 0.125
EPSILON = 1e-12
MASKED = -1e30
BLOCK = 128
WINDOW = 384
GROUP = 4 * HEAD_DIM
ROW_BLOCK = 256
GRAIN = 16
MEBI = 1024 * 1024
NT = (((1,), (1,)), ((), ()))
TN = (((0,), (0,)), ((), ()))
BF = jnp.bfloat16
F32 = jnp.float32

CORE, XBIT, YBIT = 1, 2, 4


def params(mebi=60.5):
    return pltpu.CompilerParams(vmem_limit_bytes=int(mebi * MEBI))


def cost(us):
    return pl.CostEstimate(flops=int(us * 5e9), bytes_accessed=int(us * 15e6), transcendentals=0)


def shape(dims, dtype):
    return jax.ShapeDtypeStruct(dims, dtype)


def scalar_spec():
    return pl.BlockSpec(memory_space=pltpu.SMEM)


def held_spec():
    return pl.BlockSpec(memory_space=pltpu.VMEM)


def whole_spec(dims):
    return pl.BlockSpec(dims, lambda i: (0,) * len(dims), pipeline_mode=pl.Buffered(1))


def fixed_spec(dims):
    return pl.BlockSpec(dims, lambda i: (0,) * len(dims))


def rows_spec(rows, width):
    return pl.BlockSpec((rows, width), lambda i: (i, 0))


def token_spec():
    return pl.BlockSpec(memory_space=pl.ANY)


def swap(block, axis, bit, size):
    return lax.ppermute(block, axis, [(i, i ^ bit) for i in range(size)])


def after(value, *others):
    return lax.optimization_barrier((value, *others))[0]


def neighbour(core, g):
    if g in (0, 3):
        return g
    return g ^ (3 * core)


def piece_heads_kernel(place, wq, wk, wv, wo, piece, sems):
    core, plane = place[0], place[1]
    heads = piece.shape[0] // (2 * GRAIN)
    for side, pair in enumerate(((wq, wk), (wv, wo))):

        @pl.when(core == side)
        def _():
            copies = []
            for t, ref in enumerate(pair):
                for h in range(heads):
                    start = pl.multiple_of(h * HEAD_DIM + plane * GRAIN, GRAIN)
                    to = (t * heads + h) * GRAIN
                    copies.append(
                        pltpu.make_async_copy(
                            ref.at[pl.ds(start, GRAIN), :],
                            piece.at[to : to + GRAIN, :],
                            sems.at[t * heads + h],
                        )
                    )
            for copy in copies:
                copy.start()
            for copy in copies:
                copy.wait()


def piece_heads(place, *weights):
    local, width = weights[0].shape
    heads = local // HEAD_DIM
    return pl.pallas_call(
        piece_heads_kernel,
        in_specs=[scalar_spec()] + [token_spec()] * 4,
        out_specs=held_spec(),
        out_shape=shape((2 * heads * GRAIN, width), BF),
        scratch_shapes=[pltpu.SemaphoreType.DMA((2 * heads,))],
        compiler_params=params(),
        cost_estimate=cost(1),
        name="piece_heads",
    )(place, *weights)


def piece_feed_kernel(place, wu, wd, rest, turned, piece_up, piece_down):
    core, plane = place[0], place[1]
    sub = piece_down.shape[1]
    turned[...] = wu[...].astype(F32).T.astype(BF)
    start = pl.multiple_of((core * 4 + plane) * sub, GRAIN)
    for r in range(piece_up.shape[0]):
        piece_up[r, :sub, :] = turned[pl.ds(start, sub), :]
        piece_up[r, sub:, :] = rest[...]
        piece_down[r] = wd[pl.ds(start, sub), :]


def piece_feed(place, wu, wd, rest, n_mp):
    width, hidden = wu.shape
    sub = hidden // 8
    return pl.pallas_call(
        piece_feed_kernel,
        in_specs=[scalar_spec()] + [held_spec()] * 3,
        out_specs=[held_spec()] * 3,
        out_shape=[
            shape((hidden, width), BF),
            shape((n_mp, sub + GRAIN, width), BF),
            shape((n_mp, sub, width), BF),
        ],
        compiler_params=params(),
        cost_estimate=cost(3),
        name="piece_feed",
    )(place, wu, wd, rest)


def finish_feed_kernel(place, *refs):
    pieces, (up, down, held) = refs[:8], refs[-3:]
    core, plane = place[0], place[1]
    sub = pieces[0].shape[0] // 2
    for c in range(2):
        for g, ref in enumerate(pieces[4 * c : 4 * c + 4]):
            chip = plane ^ neighbour(core ^ c, g)
            start = pl.multiple_of(((core ^ c) * 4 + chip) * sub, GRAIN)
            held[pl.ds(start, sub), :] = ref[:sub, :].astype(F32)
            down[pl.ds(start, sub), :] = ref[sub:, :].astype(F32)
    up[...] = held[...].T


def finish_feed(place, pieces, *tokens):
    rows, width = pieces[0].shape
    return pl.pallas_call(
        finish_feed_kernel,
        in_specs=[scalar_spec()] + [held_spec()] * 8 + [token_spec() for _ in tokens],
        out_specs=[held_spec()] * 2,
        out_shape=[shape((width, 4 * rows), F32), shape((4 * rows, width), F32)],
        scratch_shapes=[pltpu.VMEM((4 * rows, width), F32)],
        compiler_params=params(),
        cost_estimate=cost(6),
        name="finish_feed",
    )(place, *pieces, *tokens)


def finish_heads_kernel(place, mine, other, *outs):
    core = place[0]
    heads = outs[0].shape[0] // HEAD_DIM
    for side in range(2):

        @pl.when(core == side)
        def _():
            for c, ref in enumerate((mine, other)):
                for t in range(2):
                    out = outs[2 * (side ^ c) + t]
                    for g in range(4):
                        for h in range(heads):
                            at = h * HEAD_DIM + g * GRAIN
                            row = (t * heads + h) * GRAIN
                            out[at : at + GRAIN, :] = ref[g, row : row + GRAIN, :].astype(F32)


def finish_heads(place, pieces):
    _, rows, width = pieces[0].shape
    local = rows // (2 * GRAIN) * HEAD_DIM
    return pl.pallas_call(
        finish_heads_kernel,
        in_specs=[scalar_spec()] + [held_spec()] * 2,
        out_specs=[held_spec()] * 4,
        out_shape=[shape((local, width), F32)] * 4,
        compiler_params=params(),
        cost_estimate=cost(2),
        name="finish_heads",
    )(place, *pieces)


def turn_swap(block, bits, n_dp):
    return lax.ppermute(block, "dp", [(i, i ^ bits[i & 1]) for i in range(n_dp)])


def first_swap(block, n_dp):
    return turn_swap(block, (XBIT, YBIT), n_dp)


def second_swap(block, n_dp):
    return turn_swap(block, (YBIT, XBIT), n_dp)


def core_swap(block, n_dp):
    return swap(block, "dp", CORE, n_dp)


def exchange(block, axis, groups=None):
    return lax.all_to_all(block, axis, 0, 0, axis_index_groups=groups, tiled=True)


def spread(block, n):
    return jnp.broadcast_to(block[None], (n, *block.shape))


def plane_groups(n_dp):
    return [[8 * e + 2 * g + c for g in range(4)] for e in range(n_dp // 8) for c in range(2)]


def add(*terms):
    total = terms[0].astype(F32)
    for term in terms[1:]:
        total = total + term.astype(F32)
    return total.astype(BF)


def chip_sum(keep, got):
    return add(keep[0::2], got[0::2]), add(keep[1::2], got[1::2])


def side_sum(stay, got):
    return add(stay[0], got[0]), add(stay[1], got[1])


def shard_sum(own, got, n_dp):
    total = own.astype(F32)
    for part in got:
        total = total + part.astype(F32)
    bit = 8
    while bit < n_dp:
        total = total + swap(total, "dp", bit, n_dp)
        bit *= 2
    return total.astype(BF)


def plane_gather(four, n_dp):
    return exchange(four, "dp", plane_groups(n_dp))


def project_kernel(place, x, wq, wk, wv, wo, bq, bv, *refs):
    pieces, (q, k, v, out, full, sems, sem) = refs[:8], refs[-7:]
    last = pltpu.make_async_copy(full, out, sem)
    core, plane, shard = place[0], place[1], place[2]
    heads = wq.shape[0] // HEAD_DIM
    shards = 1 + pieces[0].shape[0] // (2 * heads * GRAIN)

    @pl.when(pl.program_id(0) == 0)
    def _():
        copies = []
        base = pl.multiple_of(shard * heads * HEAD_DIM, HEAD_DIM)
        for kind, ref in enumerate((wq, wk, wv, wo)):
            for h in range(heads):
                for g in range(4):
                    source = plane ^ neighbour(kind // 2, g)
                    at = pl.multiple_of(h * HEAD_DIM + source * GRAIN, GRAIN)
                    to = pl.multiple_of(base + h * HEAD_DIM + g * GRAIN, GRAIN)
                    copies.append(
                        pltpu.make_async_copy(
                            ref.at[pl.ds(at, GRAIN), :],
                            full.at[kind, pl.ds(to, GRAIN), :],
                            sems.at[len(copies)],
                        )
                    )
        for copy in copies:
            copy.start()
        for c in range(2):
            for g, ref in enumerate(pieces[4 * c : 4 * c + 4]):
                for r in range(1, shards):
                    base = pl.multiple_of((shard ^ r) * heads * HEAD_DIM, HEAD_DIM)
                    for t in range(2):
                        for h in range(heads):
                            row = (((r - 1) * 2 + t) * heads + h) * GRAIN
                            to = pl.multiple_of(base + h * HEAD_DIM + g * GRAIN, GRAIN)
                            full[(core ^ c) * 2 + t, pl.ds(to, GRAIN), :] = ref[
                                row : row + GRAIN, :
                            ]
        for copy in copies:
            copy.wait()
        last.start()

    block = x[...]
    for kind, (into, bias) in enumerate(((q, bq), (k, None), (v, bv))):
        value = lax.dot_general(block, full[kind], NT, preferred_element_type=F32)
        if bias is not None:
            value = value + bias[...]
        into[...] = value.astype(BF)

    @pl.when(pl.program_id(0) == pl.num_programs(0) - 1)
    def _():
        last.wait()


def project(place, x, weights, bq, bv, pieces, *tokens):
    rows, width = x.shape
    block = rows_spec(ROW_BLOCK, width)
    return pl.pallas_call(
        project_kernel,
        grid=(rows // ROW_BLOCK,),
        in_specs=[scalar_spec(), block]
        + [token_spec()] * 4
        + [whole_spec(a.shape) for a in (bq, bv, *pieces)]
        + [token_spec() for _ in tokens],
        out_specs=[block, block, block, token_spec()],
        out_shape=[shape((rows, width), BF)] * 3 + [shape((4, width, width), BF)],
        scratch_shapes=[
            pltpu.VMEM((4, width, width), BF),
            pltpu.SemaphoreType.DMA((weights[0].shape[0] // GRAIN * 4,)),
            pltpu.SemaphoreType.DMA,
        ],
        compiler_params=params(),
        cost_estimate=cost(10),
        name="project",
    )(place, x, *weights, bq, bv, *pieces, *tokens)


def spread_heads(block):
    lane = lax.broadcasted_iota(jnp.int32, block.shape, 1) // HEAD_DIM
    return jnp.concatenate(
        [jnp.where(lane == h, block, jnp.zeros_like(block)) for h in range(4)], axis=0
    )


def gather_heads(stacked):
    rows = stacked.shape[0] // 4
    lane = lax.broadcasted_iota(jnp.int32, (rows, GROUP), 1) // HEAD_DIM
    out = stacked[:rows]
    for h in range(1, 4):
        out = jnp.where(lane == h, stacked[h * rows : (h + 1) * rows], out)
    return out


def window_start(step, rows):
    return pl.multiple_of(jnp.clip(step - 1, 0, (rows - WINDOW) // BLOCK) * BLOCK, BLOCK)


def attend_kernel(part, q, k, v, segc, segr, x, wo, bo, gain, shift, *refs):
    ctx, saved, unit, low = refs[-4:]
    start = window_start(part * pl.num_programs(0) + pl.program_id(0), k.shape[0])
    near = pl.ds(start, WINDOW)
    penalty = jnp.where(segc[...] == segr[:, near], 0.0, MASKED)
    lane = lax.broadcasted_iota(jnp.int32, (BLOCK, 128), 1)
    groups = q.shape[1] // GROUP

    def score_group(group):
        cols = slice(group * GROUP, (group + 1) * GROUP)
        return lax.dot_general(
            spread_heads(q[:, cols] * SCALE), k[near, cols], NT, preferred_element_type=F32
        )

    keep = jnp.zeros((BLOCK, 128), F32)
    ahead = score_group(0)
    for group in range(groups):
        cols = slice(group * GROUP, (group + 1) * GROUP)
        logits = ahead.reshape(4, BLOCK, WINDOW) + penalty[None]
        if group + 1 < groups:
            ahead = score_group(group + 1)
        peak = jnp.max(logits, axis=-1, keepdims=True)
        raised = jnp.exp(logits - peak)
        sums = jnp.sum(raised, axis=-1, keepdims=True)
        context = jnp.dot(
            raised.astype(BF).reshape(4 * BLOCK, WINDOW), v[near, cols], preferred_element_type=F32
        )
        context = (context.reshape(4, BLOCK, GROUP) * (1.0 / sums)).reshape(4 * BLOCK, GROUP)
        ctx[:, cols] = gather_heads(context).astype(BF)
        log_total = peak + jnp.log(sums)
        for h in range(4):
            keep = jnp.where(lane == group * 4 + h, log_total[h], keep)
    attended = jnp.dot(ctx[...], wo[0], preferred_element_type=F32) + bo[...]
    total = x[...].astype(F32) + attended
    centred = total - jnp.mean(total, axis=-1, keepdims=True)
    inv_std = lax.rsqrt(jnp.mean(centred * centred, axis=-1, keepdims=True) + EPSILON)
    unit_val = centred * inv_std
    unit[...] = unit_val
    low[...] = (unit_val * gain[...] + shift[...]).astype(BF)
    saved[...] = jnp.where(lane == 127, inv_std, keep)


def attend(part, parts, q, k, v, segc, segr, x, full, bo, gain, shift, held, *tokens):
    rows, width = q.shape
    steps = rows // BLOCK // parts

    def block(wide):
        return pl.BlockSpec((BLOCK, wide), lambda i: (part * steps + i, 0))

    return pl.pallas_call(
        functools.partial(attend_kernel, part),
        grid=(steps,),
        in_specs=[
            block(width),
            whole_spec((rows, width)),
            whole_spec((rows, width)),
            block(1),
            whole_spec((1, rows)),
            block(width),
            pl.BlockSpec((1, width, width), lambda i: (3, 0, 0), pipeline_mode=pl.Buffered(1)),
            whole_spec((1, width)),
            whole_spec((1, width)),
            whole_spec((1, width)),
        ]
        + [token_spec() for _ in (*held, *tokens)],
        out_specs=[block(width), block(128), block(width), block(width)],
        out_shape=[
            shape((rows, width), BF),
            shape((rows, 128), F32),
            shape((rows, width), F32),
            shape((rows, width), BF),
        ],
        input_output_aliases={10 + i: i for i in range(len(held))},
        compiler_params=params(),
        cost_estimate=cost(16 / parts),
        name="attend",
    )(q, k, v, segc, segr, x, full, bo, gain, shift, *held, *tokens)


def whole_order(rows, plane):
    width = rows.shape[1]
    rank = (lax.broadcasted_iota(jnp.int32, rows.shape, 1) // GRAIN) % 4
    row = lax.broadcasted_iota(jnp.int32, rows.shape, 0)

    def shifted(block, by):
        return pltpu.roll(block, by % width, 1)

    middle = jnp.where(rank == 1, shifted(rows, -GRAIN), shifted(rows, GRAIN))
    swapped = (row == 7) & ((rank == 1) | (rank == 2))
    rows = jnp.where(swapped, middle, rows)
    for bit in (1, 2):
        by = bit * GRAIN
        other = jnp.where((rank & bit) == 0, shifted(rows, -by), shifted(rows, by))
        rows = jnp.where((plane & bit) == 0, rows, other)
    return rows


def attend_back_kernel(place, q, k, v, do, saved, inner, segc, segr, *refs):
    dq, dk, dv, sums, dk_sum, dv_sum = refs[-6:]
    step = pl.program_id(0)

    @pl.when(step == 0)
    def _():
        dk_sum[...] = jnp.zeros_like(dk_sum)
        dv_sum[...] = jnp.zeros_like(dv_sum)
        sums[...] = jnp.zeros_like(sums)

    start = window_start(step, k.shape[0])
    near = pl.ds(start, WINDOW)
    penalty = jnp.where(segc[...] == segr[:, near], 0.0, MASKED)
    for group in range(q.shape[1] // GROUP):
        cols = slice(group * GROUP, (group + 1) * GROUP)
        q4 = spread_heads(q[:, cols] * SCALE)
        do4 = spread_heads(do[:, cols])
        k4 = k[near, cols]
        logits = lax.dot_general(q4, k4, NT, preferred_element_type=F32)
        logits = logits.reshape(4, BLOCK, WINDOW) + penalty[None]
        lse = jnp.stack([saved[:, group * 4 + h : group * 4 + h + 1] for h in range(4)])
        mean_grad = jnp.stack([inner[:, group * 4 + h : group * 4 + h + 1] for h in range(4)])
        probs = jnp.exp(logits - lse)
        weight_grad = lax.dot_general(
            do4, v[near, cols], NT, preferred_element_type=F32
        ).reshape(4, BLOCK, WINDOW)
        logit_grad = (probs * (weight_grad - mean_grad)).astype(BF).reshape(4 * BLOCK, WINDOW)
        probs_low = probs.astype(BF).reshape(4 * BLOCK, WINDOW)
        dq_low = (
            gather_heads(jnp.dot(logit_grad, k4, preferred_element_type=F32)) * SCALE
        ).astype(BF)
        dq[:, cols] = dq_low
        sums[6:7, cols] += jnp.sum(dq_low.astype(F32), axis=0, keepdims=True)
        dk_sum[near, cols] += lax.dot_general(logit_grad, q4, TN, preferred_element_type=F32)
        dv_sum[near, cols] += lax.dot_general(probs_low, do4, TN, preferred_element_type=F32)

    @pl.when(step == pl.num_programs(0) - 1)
    def _():
        dk[...] = dk_sum[...].astype(BF)
        dv_low = dv_sum[...].astype(BF)
        dv[...] = dv_low
        sums[7:8, :] = jnp.sum(dv_low.astype(F32), axis=0, keepdims=True)
        sums[...] = whole_order(sums[...], place[1])


def attend_back(place, q, k, v, do, saved, inner, segc, segr, *tokens):
    rows, width = q.shape
    block = rows_spec(BLOCK, width)
    full = whole_spec((rows, width))
    return pl.pallas_call(
        attend_back_kernel,
        grid=(rows // BLOCK,),
        in_specs=[
            scalar_spec(),
            block,
            full,
            full,
            block,
            rows_spec(BLOCK, 128),
            rows_spec(BLOCK, 128),
            rows_spec(BLOCK, 1),
            whole_spec((1, rows)),
        ]
        + [token_spec() for _ in tokens],
        out_specs=[block, fixed_spec((rows, width)), fixed_spec((rows, width)), fixed_spec((8, width))],
        out_shape=[shape((rows, width), BF)] * 3 + [shape((8, width), F32)],
        scratch_shapes=[pltpu.VMEM((rows, width), F32)] * 2,
        compiler_params=params(),
        cost_estimate=cost(22),
        name="attend_back",
    )(place, q, k, v, do, saved, inner, segc, segr, *tokens)


def assemble(place, own, pieces, into):
    core, plane, shard = place[0], place[1], place[2]
    sub = own.shape[0] // 8
    shards = 1 + pieces[0].shape[0] // sub

    def rows(c, g, r):
        return pl.ds(pl.multiple_of(((c * 4 + g) * shards + (shard ^ r)) * sub, GRAIN), sub)

    for c in range(2):
        for g, ref in enumerate(pieces[4 * c : 4 * c + 4]):
            at = pl.multiple_of(((core ^ c) * 4 + (plane ^ neighbour(core ^ c, g))) * sub, GRAIN)
            into[rows(c, g, 0), :] = own[pl.ds(at, sub), :]
            for r in range(1, shards):
                into[rows(c, g, r), :] = ref[(r - 1) * sub : r * sub, :]


def feed_up_kernel(place, x, own, bu, *refs):
    pieces, (act, slope, out, wu, sem) = refs[:8], refs[-5:]
    copy = pltpu.make_async_copy(wu, out, sem)

    @pl.when(pl.program_id(0) == 0)
    def _():
        assemble(place, own, pieces, wu)
        copy.start()

    block = x[...]
    for at in range(0, wu.shape[0], 256):
        span = slice(at, at + 256)
        pre = (
            lax.dot_general(block, wu[span, :], NT, preferred_element_type=F32) + bu[:, span]
        )
        below = 0.5 * (1.0 + lax.erf(pre * 0.7071067811865476))
        density = jnp.exp(-0.5 * pre * pre) * 0.3989422804014327
        act[:, span] = (pre * below).astype(BF)
        slope[:, span] = (below + pre * density).astype(BF)

    @pl.when(pl.program_id(0) == pl.num_programs(0) - 1)
    def _():
        copy.wait()


def feed_up(place, x, own, bu, pieces, *tokens):
    rows, width = x.shape
    hidden = bu.shape[1]
    wide = rows_spec(ROW_BLOCK, hidden)
    return pl.pallas_call(
        feed_up_kernel,
        grid=(rows // ROW_BLOCK,),
        in_specs=[scalar_spec(), rows_spec(ROW_BLOCK, width)]
        + [whole_spec(a.shape) for a in (own, bu, *pieces)]
        + [token_spec() for _ in tokens],
        out_specs=[wide, wide, token_spec()],
        out_shape=[shape((rows, hidden), BF)] * 2 + [shape((hidden, width), BF)],
        scratch_shapes=[pltpu.VMEM((hidden, width), BF), pltpu.SemaphoreType.DMA],
        compiler_params=params(),
        cost_estimate=cost(12),
        name="feed_up",
    )(place, x, own, bu, *pieces, *tokens)


def feed_down_kernel(place, act, unit, cot, own, vectors, *refs):
    pieces, outs = refs[:8], refs[-8:]
    layer, output, second, down_grad, sums, out, wd, sem = outs
    copy = pltpu.make_async_copy(wd, out, sem)

    @pl.when(pl.program_id(0) == 0)
    def _():
        sums[...] = jnp.zeros_like(sums)
        assemble(place, own, pieces, wd)
        copy.start()

    down = jnp.dot(act[...], wd[...], preferred_element_type=F32)
    b_down, first_gain, first_shift, second_gain, second_shift = (
        vectors[i : i + 1, :] for i in range(5)
    )
    total = unit[...] * first_gain + first_shift + down + b_down
    centred = total - jnp.mean(total, axis=-1, keepdims=True)
    inv_std = lax.rsqrt(jnp.mean(centred * centred, axis=-1, keepdims=True) + EPSILON)
    unit_val = centred * inv_std
    layer_out = unit_val * second_gain + second_shift
    layer[...] = layer_out
    output[...] = layer_out.astype(BF)
    grad = cot[...].astype(F32)
    scaled = grad * second_gain
    inner = (
        scaled
        - jnp.mean(scaled, axis=-1, keepdims=True)
        - unit_val * jnp.mean(scaled * unit_val, axis=-1, keepdims=True)
    )
    second_grad = inv_std * inner
    second[...] = second_grad
    grad_low = second_grad.astype(BF)
    down_grad[...] = grad_low
    sums[3:4, :] += jnp.sum(grad_low.astype(F32), axis=0, keepdims=True)
    sums[4:5, :] += jnp.sum(grad * unit_val, axis=0, keepdims=True)
    sums[5:6, :] += jnp.sum(grad, axis=0, keepdims=True)

    @pl.when(pl.program_id(0) == pl.num_programs(0) - 1)
    def _():
        copy.wait()


def feed_down(place, act, unit, cot, own, vectors, pieces):
    rows, hidden = act.shape
    width = unit.shape[1]
    block = rows_spec(ROW_BLOCK, width)
    return pl.pallas_call(
        feed_down_kernel,
        grid=(rows // ROW_BLOCK,),
        in_specs=[scalar_spec(), rows_spec(ROW_BLOCK, hidden), block, block]
        + [whole_spec(a.shape) for a in (own, vectors, *pieces)],
        out_specs=[block, block, block, block, fixed_spec((8, width)), token_spec()],
        out_shape=[
            shape((rows, width), F32),
            shape((rows, width), BF),
            shape((rows, width), F32),
            shape((rows, width), BF),
            shape((8, width), F32),
            shape((hidden, width), BF),
        ],
        scratch_shapes=[pltpu.VMEM((hidden, width), BF), pltpu.SemaphoreType.DMA],
        compiler_params=params(),
        cost_estimate=cost(13),
        name="feed_down",
    )(place, act, unit, cot, own, vectors, *pieces)


def feed_back_kernel(place, grad, x, wu, wd, slope, act, keep, send, bias, out, held):
    step = pl.program_id(0)
    half = pl.num_programs(0) // 2
    chips, shards, _, sub, width = keep.shape

    @pl.when(step == 0)
    def _():
        out[...] = jnp.zeros_like(out)
        bias[...] = jnp.zeros_like(bias)

    total = None
    for at in range(0, x.shape[0], ROW_BLOCK):
        span = slice(at, at + ROW_BLOCK)
        act_grad = lax.dot_general(grad[span, :], wd[...], NT, preferred_element_type=F32)
        low = (act_grad * slope[span, :].astype(F32)).astype(BF)
        held[span, :] = low
        term = jnp.sum(low.astype(F32), axis=0, keepdims=True)
        total = term if total is None else total + term
    core, plane = place[0], place[1]
    owner = jnp.where(step < half, core ^ 1, core)
    row = lax.broadcasted_iota(jnp.int32, (bias.shape[0], sub), 0)
    for g in range(chips):
        early = plane ^ jnp.where(owner == 0, neighbour(0, g), neighbour(1, g))
        late = plane ^ jnp.where(owner == 0, neighbour(0, 2 + g), neighbour(1, 2 + g))
        target = owner * 4 + jnp.where(lax.rem(step, half) == 0, early, late)
        for r in range(shards):
            at = (g * shards + r) * sub
            lanes = slice(r * 128, r * 128 + sub)
            bias[:, lanes] = jnp.where(row == target, total[:, at : at + sub], bias[:, lanes])
    out[...] += jnp.dot(held[...], wu[...], preferred_element_type=F32)
    dims = (chips, shards, sub, width)
    up = lax.dot_general(held[...], x[...], TN, preferred_element_type=F32).astype(BF)
    down = lax.dot_general(act[...], grad[...], TN, preferred_element_type=F32).astype(BF)

    @pl.when(step < half)
    def _():
        send[:, :, 0] = up.reshape(dims)
        send[:, :, 1] = down.reshape(dims)

    @pl.when(step >= half)
    def _():
        keep[:, :, 0] = up.reshape(dims)
        keep[:, :, 1] = down.reshape(dims)


def feed_back(place, grad, x, wu, wd, slope, act, n_mp):
    rows, width = x.shape
    hidden = wu.shape[0]
    span = hidden // 4
    full = whole_spec((rows, width))
    weight = pl.BlockSpec((span, width), lambda j: ((j + 2) % 4, 0))
    wide = pl.BlockSpec((rows, span), lambda j: (0, (j + 2) % 4))
    dims = (4, n_mp, 2, hidden // 8 // n_mp, width)
    block = (2, *dims[1:])
    return pl.pallas_call(
        feed_back_kernel,
        grid=(4,),
        in_specs=[scalar_spec(), full, full, weight, weight, wide, wide],
        out_specs=[
            pl.BlockSpec(block, lambda j: (jnp.maximum(j - 2, 0), 0, 0, 0, 0)),
            pl.BlockSpec(block, lambda j: (jnp.minimum(j, 1), 0, 0, 0, 0)),
            fixed_spec((8, 128 * n_mp)),
            fixed_spec((rows, width)),
        ],
        out_shape=[
            shape(dims, BF),
            shape(dims, BF),
            shape((8, 128 * n_mp), F32),
            shape((rows, width), F32),
        ],
        scratch_shapes=[pltpu.VMEM((rows, span), BF)],
        compiler_params=params(),
        cost_estimate=cost(27),
        name="feed_back",
    )(place, grad, x, wu, wd, slope, act)


def middle_kernel(normed, second, unit, saved, ctx, wo, gain, *refs):
    first, context_grad, inner_sum, weight, sums, held, lows = refs[-7:]
    step = pl.program_id(0)
    grad = normed[...] + second[...]
    unit_val = unit[...]
    scaled = grad * gain[...]
    inner = (
        scaled
        - jnp.mean(scaled, axis=-1, keepdims=True)
        - unit_val * jnp.mean(scaled * unit_val, axis=-1, keepdims=True)
    )
    first_grad = saved[:, 127:128] * inner
    first[...] = first_grad
    low = first_grad.astype(BF)
    context_low = lax.dot_general(low, wo[0], NT, preferred_element_type=F32).astype(BF)
    context_grad[...] = context_low
    product = context_low.astype(F32) * ctx[...].astype(F32)
    high = product.astype(BF)
    rest = (product - high.astype(F32)).astype(BF)
    width = product.shape[1]
    head = lax.broadcasted_iota(jnp.int32, (width, 128), 0) // HEAD_DIM
    head = (head == lax.broadcasted_iota(jnp.int32, (width, 128), 1)).astype(BF)
    inner_sum[...] = jnp.dot(high, head, preferred_element_type=F32) + jnp.dot(
        rest, head, preferred_element_type=F32
    )
    at = pl.ds(pl.multiple_of(step * ROW_BLOCK, ROW_BLOCK), ROW_BLOCK)
    lows[at, :] = low
    held[at, :] = ctx[...]

    @pl.when(step == 0)
    def _():
        sums[...] = jnp.zeros_like(sums)

    sums[0:1, :] += jnp.sum(low.astype(F32), axis=0, keepdims=True)
    sums[1:2, :] += jnp.sum(grad * unit_val, axis=0, keepdims=True)
    sums[2:3, :] += jnp.sum(grad, axis=0, keepdims=True)

    @pl.when(step == pl.num_programs(0) - 1)
    def _():
        weight[...] = lax.dot_general(
            held[...], lows[...], TN, preferred_element_type=F32
        ).astype(BF)


def middle(normed, second, unit, saved, ctx, full, gain, *tokens):
    rows, width = normed.shape
    block = rows_spec(ROW_BLOCK, width)
    return pl.pallas_call(
        middle_kernel,
        grid=(rows // ROW_BLOCK,),
        in_specs=[
            block,
            block,
            block,
            rows_spec(ROW_BLOCK, 128),
            block,
            pl.BlockSpec((1, width, width), lambda i: (3, 0, 0), pipeline_mode=pl.Buffered(1)),
            whole_spec((1, width)),
        ]
        + [token_spec() for _ in tokens],
        out_specs=[block, block, rows_spec(ROW_BLOCK, 128), fixed_spec((width, width)), fixed_spec((8, width))],
        out_shape=[
            shape((rows, width), F32),
            shape((rows, width), BF),
            shape((rows, 128), F32),
            shape((width, width), BF),
            shape((8, width), F32),
        ],
        scratch_shapes=[pltpu.VMEM((rows, width), BF)] * 2,
        compiler_params=params(),
        cost_estimate=cost(8),
        name="middle",
    )(normed, second, unit, saved, ctx, full, gain, *tokens)


def head_weights_kernel(place, dq, dk, dv, x, wo, *refs):
    keep, send, held = refs[-3:]
    core = place[0]
    shards, heads = keep.shape[1], keep.shape[3]
    for kind in range(4):
        if kind < 3:
            held[...] = lax.dot_general(
                (dq, dk, dv)[kind][...], x[...], TN, preferred_element_type=F32
            ).astype(BF)
        source = held if kind < 3 else wo
        for side in range(2):

            @pl.when(core == side)
            def _():
                out = keep if side == kind // 2 else send
                for r in range(shards):
                    for h in range(heads):
                        for g in range(4):
                            at = (r * heads + h) * HEAD_DIM + g * GRAIN
                            out[g, r, kind % 2, h] = source[at : at + GRAIN, :]


def head_weights(place, dq, dk, dv, x, wo, n_mp, *tokens):
    rows, width = x.shape
    heads = width // HEAD_DIM // n_mp
    dims = (4, n_mp, 2, heads, GRAIN, width)
    keep, send = pl.pallas_call(
        head_weights_kernel,
        in_specs=[scalar_spec()] + [held_spec()] * 5 + [token_spec() for _ in tokens],
        out_specs=[held_spec()] * 2,
        out_shape=[shape(dims, BF)] * 2,
        scratch_shapes=[pltpu.VMEM((width, width), BF)],
        compiler_params=params(),
        cost_estimate=cost(8),
        name="head_weights",
    )(place, dq, dk, dv, x, wo, *tokens)
    dims = (4, n_mp, 2 * heads * GRAIN, width)
    return keep.reshape(dims), send.reshape(dims)


def input_kernel(dq, dk, dv, full, first, *refs):
    out = refs[-1]
    total = first[...]
    for kind, ref in enumerate((dq, dk, dv)):
        total = total + jnp.dot(ref[...], full[kind], preferred_element_type=F32)
    out[...] = total


def input_gradient(dq, dk, dv, full, first, *tokens):
    rows, width = dq.shape
    block = rows_spec(ROW_BLOCK, width)
    return pl.pallas_call(
        input_kernel,
        grid=(rows // ROW_BLOCK,),
        in_specs=[
            block,
            block,
            block,
            pl.BlockSpec((3, width, width), lambda i: (0, 0, 0), pipeline_mode=pl.Buffered(1)),
            block,
        ]
        + [token_spec() for _ in tokens],
        out_specs=block,
        out_shape=shape((rows, width), F32),
        compiler_params=params(),
        cost_estimate=cost(6),
        name="input_gradient",
    )(dq, dk, dv, full, first, *tokens)


def score_kernel(out_ref, segr_ref, len_ref, table_ref, pick_ref, *refs):
    score_ref = refs[-1]
    queries = pick_ref.shape[0]
    rows = out_ref.shape[0]
    label = lax.broadcasted_iota(jnp.int32, (queries, rows), 0)
    onehot = (label == segr_ref[...]).astype(F32)
    sums = jnp.dot(
        onehot, out_ref[...], precision=lax.Precision.HIGHEST, preferred_element_type=F32
    )
    means = sums / len_ref[...].astype(F32)
    every = lax.dot_general(
        means,
        table_ref[...].astype(F32),
        NT,
        precision=lax.Precision.HIGHEST,
        preferred_element_type=F32,
    )
    at = lax.broadcasted_iota(jnp.int32, every.shape, 1)
    column = lax.broadcasted_iota(jnp.int32, pick_ref.shape, 1)
    result = jnp.zeros(pick_ref.shape, F32)
    for p in range(pick_ref.shape[1]):
        chosen = jnp.sum(
            jnp.where(at == pick_ref[:, p : p + 1], every, 0.0), axis=1, keepdims=True
        )
        result = jnp.where(column == p, chosen, result)
    score_ref[...] = result


def score(layer_out, segr, lengths, table, picks, *tokens):
    return pl.pallas_call(
        score_kernel,
        in_specs=[held_spec()] * 5 + [token_spec() for _ in tokens],
        out_specs=held_spec(),
        out_shape=shape(picks.shape, F32),
        compiler_params=params(),
        cost_estimate=cost(8),
        name="score",
    )(layer_out, segr, lengths, table, picks, *tokens)


def per_device(
    n_dp,
    n_mp,
    hidden_in,
    cotangent,
    query_lengths,
    passage_index,
    passages,
    w_query,
    w_key,
    w_value,
    w_output,
    w_up,
    w_down,
    b_query,
    b_value,
    b_output,
    b_up,
    b_down,
    first_gain,
    first_shift,
    second_gain,
    second_shift,
):
    rows, width = hidden_in.shape
    heads = w_query.shape[1] // HEAD_DIM
    sub = w_up.shape[1] // 8
    at_dp = lax.axis_index("dp")
    core, plane = at_dp & 1, (at_dp >> 1) & 3
    shard = lax.axis_index("mp")
    place = jnp.stack([core, plane, shard]).astype(jnp.int32)
    own_heads = (w_query.T, w_key.T, w_value.T, w_output)

    cut = heads * HEAD_DIM
    heads_piece = piece_heads(place, *own_heads)
    bias_rows = jnp.stack(
        [jnp.pad(b_query, (0, width - cut)), jnp.pad(b_value, (0, width - cut)), b_up]
    )
    rest = jnp.pad(after(bias_rows, heads_piece), ((0, GRAIN - 3), (0, 0)))
    turned, up_piece, down_piece = piece_feed(place, w_up, w_down, rest, n_mp)
    heads_parts = [swap(after(heads_piece, rest), "mp", 1, n_mp)] + [
        swap(heads_piece, "mp", r, n_mp) for r in range(2, n_mp)
    ]
    up_got = exchange(up_piece, "mp")
    heads_shards = jnp.concatenate(heads_parts)
    heads_first = first_swap(heads_shards, n_dp)
    heads_second = second_swap(heads_shards, n_dp)
    heads_corner = second_swap(after(heads_first, heads_second), n_dp)
    heads_other = [core_swap(p, n_dp) for p in (heads_shards, heads_first, heads_second)]
    heads_corner, up_got = lax.optimization_barrier((heads_corner, up_got))
    heads_mine = [heads_shards, heads_first, heads_second, heads_corner]
    heads_other = heads_other + [core_swap(heads_corner, n_dp)]

    def others(got):
        return jnp.concatenate(
            [
                lax.dynamic_index_in_dim(got, shard ^ r, 0, keepdims=False)[:sub]
                for r in range(1, n_mp)
            ]
        )

    up_shards = others(after(up_got, *heads_mine, *heads_other))
    up_first = first_swap(up_shards, n_dp)
    up_second = second_swap(up_shards, n_dp)

    ranks = lax.broadcasted_iota(jnp.int32, (4, 4), 0)
    places4 = lax.broadcasted_iota(jnp.int32, (4, 4), 1)
    turned_ranks = jnp.where((ranks == 1) | (ranks == 2), ranks ^ 3, ranks)
    order_q = ((plane ^ ranks) == places4).astype(F32)
    order_v = ((plane ^ turned_ranks) == places4).astype(F32)
    owner = (core ^ jnp.arange(2, dtype=jnp.int32)).reshape(2, 1, 1, 1)
    is_owner = (owner == jnp.arange(2, dtype=jnp.int32).reshape(1, 1, 2, 1)).astype(F32)
    order_up = jnp.where(owner == 0, order_q[None, :, None], order_v[None, :, None])
    order_up = (order_up * is_owner).reshape(8, 8)
    exact = functools.partial(
        jnp.einsum, precision=lax.Precision.HIGHEST, preferred_element_type=F32
    )
    all_bias = up_got[:, sub : sub + 3].astype(F32)
    by_head = (n_mp, heads, 4, GRAIN)
    query_bias = exact("gk,zhki->zhgi", order_q, all_bias[:, 0, :cut].reshape(by_head))
    value_bias = exact("gk,zhki->zhgi", order_v, all_bias[:, 1, :cut].reshape(by_head))
    up_bias = exact("gk,zki->gzi", order_up, all_bias[:, 2].reshape(n_mp, 8, sub))
    query_bias, value_bias, up_bias = (
        b.reshape(1, -1) for b in (query_bias, value_bias, up_bias)
    )

    ends = jnp.cumsum(query_lengths, axis=-1, dtype=jnp.int32)
    places = lax.broadcasted_iota(jnp.int32, (rows, query_lengths.shape[1]), 0)
    seg = jnp.sum((places >= ends).astype(jnp.int32), axis=-1)
    segc, segr = seg.reshape(rows, 1), seg.reshape(1, rows)
    vectors = jnp.stack(
        [b_down, first_gain, first_shift, second_gain, second_shift, b_output, b_output, b_output]
    ).astype(F32)

    query, key, value, full = project(
        place, hidden_in, own_heads, query_bias, value_bias, heads_mine + heads_other
    )
    up_first, up_second, query = lax.optimization_barrier((up_first, up_second, query))
    down_got = exchange(after(down_piece, query), "mp")
    up_corner = second_swap(up_first, n_dp)
    up_mine = [up_shards, up_first, up_second]
    up_other = [core_swap(p, n_dp) for p in up_mine]
    held = attend(
        0, 2, query, key, value, segc, segr, hidden_in, full,
        vectors[5:6], vectors[1:2], vectors[2:3], (),
    )
    up_corner, down_got, up_other, *held = lax.optimization_barrier(
        (up_corner, down_got, up_other, *held)
    )
    up_pieces = up_mine + [up_corner] + up_other + [core_swap(up_corner, n_dp)]
    down_shards = others(down_got)
    down_first = first_swap(down_shards, n_dp)
    down_second = second_swap(down_shards, n_dp)
    context, saved, unit, low = attend(
        1, 2, query, key, value, segc, segr, hidden_in, full,
        vectors[5:6], vectors[1:2], vectors[2:3], held, down_shards,
    )
    down_first, down_second, low = lax.optimization_barrier((down_first, down_second, low))
    down_corner = second_swap(down_first, n_dp)
    down_mine = [down_shards, down_first, down_second]
    down_other = [core_swap(p, n_dp) for p in down_mine]
    act, slope, wu = feed_up(place, low, turned, up_bias, up_pieces, *down_mine[1:])
    down_corner, act = lax.optimization_barrier((down_corner, act))
    down_pieces = down_mine + [down_corner] + down_other + [core_swap(down_corner, n_dp)]
    layer_out, output, second_grad, down_grad, second_sums, wd = feed_down(
        place, act, unit, cotangent, w_down, vectors, down_pieces
    )

    feed_keep, feed_send, up_sums, normed = feed_back(
        place, down_grad, low, wu, wd, slope, act, n_mp
    )
    dims = (4, n_mp, 2 * sub, width)
    feed_keep = feed_keep.reshape(dims)
    got = core_swap(feed_send.reshape(dims), n_dp)
    first_grad, context_grad, inner, wo_grad, first_sums = middle(
        normed, second_grad, unit, saved, context, full, vectors[1:2]
    )
    got, context_grad = lax.optimization_barrier((got, context_grad))
    feed_stay, feed_go = chip_sum(feed_keep, got)
    got = first_swap(feed_go, n_dp)
    dq, dk, dv, head_sums = attend_back(
        place, query, key, value, context_grad, saved, inner, segc, segr, feed_go
    )
    got, head_sums = lax.optimization_barrier((got, head_sums))
    feed_own, feed_go = side_sum(feed_stay, got)
    got = second_swap(feed_go, n_dp)
    every = jnp.concatenate(
        [second_sums + first_sums + head_sums, up_sums], axis=1
    )
    vector_got = swap(every, "mp", 1, n_mp)
    heads_keep, heads_send = head_weights(
        place, dq, dk, dv, hidden_in, wo_grad, n_mp, every, feed_go
    )
    got, heads_keep = lax.optimization_barrier((got, heads_keep))
    feed_parts = add(feed_own, got)
    heads_got = core_swap(after(heads_send, feed_parts), n_dp)
    feed_got = exchange(feed_parts, "mp")
    heads_stay, heads_go = chip_sum(heads_keep, heads_got)
    heads_got = first_swap(heads_go, n_dp)
    every = every + after(vector_got, heads_go)
    vector_got = core_swap(every, n_dp)
    input_grad = input_gradient(dq, dk, dv, full, first_grad, heads_go, every)
    heads_got, vector_got, input_grad = lax.optimization_barrier(
        (heads_got, vector_got, input_grad)
    )
    heads_own, heads_go = side_sum(heads_stay, heads_got)
    heads_got = second_swap(heads_go, n_dp)
    every = every + after(vector_got, heads_go)
    bit = 2
    while bit < n_mp:
        vector_got = swap(every, "mp", bit, n_mp)
        bit *= 2
    heads_parts = add(heads_own, heads_got)
    feed_got, vector_got, heads_parts = lax.optimization_barrier(
        (feed_got, vector_got, heads_parts)
    )
    heads_got = exchange(heads_parts, "mp")
    every = every + after(vector_got, heads_parts)
    feed_got, every = lax.optimization_barrier((feed_got, every))
    feed_total = shard_sum(feed_got[0], [feed_got[r] for r in range(1, n_mp)], n_dp)
    feed_mine = [feed_total, first_swap(feed_total, n_dp), second_swap(feed_total, n_dp)]
    feed_mine.append(swap(feed_total, "dp", XBIT | YBIT, n_dp))
    vector_got = swap(every, "dp", XBIT, n_dp)
    scores = score(
        layer_out, segr, query_lengths.reshape(-1, 1), passages, passage_index, every
    )
    heads_got, vector_got, scores = lax.optimization_barrier((heads_got, vector_got, scores))
    every = every + vector_got
    vector_got = swap(every, "dp", YBIT, n_dp)
    heads_total = shard_sum(heads_got[0], [heads_got[r] for r in range(1, n_mp)], n_dp)
    heads_four = spread(heads_total, 4)
    heads_mine = plane_gather(heads_four, n_dp)
    feed_mine = lax.optimization_barrier((*feed_mine, heads_four))[:4]
    feed_other = [core_swap(p, n_dp) for p in feed_mine]
    every = every + after(vector_got, heads_four)
    bit = 8
    while bit < n_dp:
        every = every + swap(every, "dp", bit, n_dp)
        bit *= 2
    w_up_grad, w_down_grad = finish_feed(place, (*feed_mine, *feed_other), heads_four, every)
    heads_mine, w_up_grad = lax.optimization_barrier((heads_mine, w_up_grad))
    heads_other = core_swap(heads_mine, n_dp)
    query_t, key_t, value_t, w_output_grad = finish_heads(place, (heads_mine, heads_other))
    shared = every[:6, :width]
    query_sums, value_sums = (
        lax.dynamic_slice_in_dim(every[row, :width], shard * cut, cut) for row in (6, 7)
    )
    up_sums = lax.dynamic_slice_in_dim(every[:, width:], shard * 128, 128, axis=1)
    up_sums = up_sums[:, :sub].reshape(-1)
    return (
        output,
        scores,
        input_grad,
        query_t.T,
        key_t.T,
        value_t.T,
        w_output_grad,
        w_up_grad,
        w_down_grad,
        query_sums,
        value_sums,
        shared[0],
        up_sums,
        shared[3],
        shared[1],
        shared[2],
        shared[4],
        shared[5],
    )


def solution(mesh):
    both, split = P(("dp", "mp"), None), P(None, "mp")
    return jax.shard_map(
        functools.partial(per_device, mesh.shape["dp"], mesh.shape["mp"]),
        mesh=mesh,
        in_specs=(both, both, both, both, P())
        + (split, split, split, P("mp", None), split, P("mp", None))
        + (P("mp"), P("mp"), P(), P("mp"), P(), P(), P(), P(), P()),
        out_specs=(both, both, both)
        + (split, split, split, P("mp", None), split, P("mp", None))
        + (P("mp"), P("mp"), P(), P("mp"), P(), P(), P(), P(), P()),
        check_vma=False,
    )
```

```python
import functools

import jax
import jax.numpy as jnp
from jax import lax
from jax.experimental import pallas as pl
from jax.experimental.pallas import tpu as pltpu
from jax.sharding import PartitionSpec as P

HEAD_DIM = 64
SCALE = 0.125
EPSILON = 1e-12
MASKED = -1e30
BLOCK = 128
WINDOW = 384
GROUP = 4 * HEAD_DIM
ROW_BLOCK = 256
GRAIN = 16
MEBI = 1024 * 1024
NT = (((1,), (1,)), ((), ()))
TN = (((0,), (0,)), ((), ()))
BF = jnp.bfloat16
F32 = jnp.float32

CORE, XBIT, YBIT = 1, 2, 4


def params(mebi=60.5):
    return pltpu.CompilerParams(vmem_limit_bytes=int(mebi * MEBI))


def cost(us):
    return pl.CostEstimate(flops=int(us * 5e9), bytes_accessed=int(us * 15e6), transcendentals=0)


def shape(dims, dtype):
    return jax.ShapeDtypeStruct(dims, dtype)


def scalar_spec():
    return pl.BlockSpec(memory_space=pltpu.SMEM)


def held_spec():
    return pl.BlockSpec(memory_space=pltpu.VMEM)


def whole_spec(dims):
    return pl.BlockSpec(dims, lambda i: (0,) * len(dims), pipeline_mode=pl.Buffered(1))


def fixed_spec(dims):
    return pl.BlockSpec(dims, lambda i: (0,) * len(dims))


def rows_spec(rows, width):
    return pl.BlockSpec((rows, width), lambda i: (i, 0))


def token_spec():
    return pl.BlockSpec(memory_space=pl.ANY)


def swap(block, axis, bit, size):
    return lax.ppermute(block, axis, [(i, i ^ bit) for i in range(size)])


def after(value, *others):
    return lax.optimization_barrier((value, *others))[0]


def neighbour(core, g):
    if g in (0, 3):
        return g
    return g ^ (3 * core)


def piece_heads_kernel(place, wq, wk, wv, wo, piece, sems):
    core, plane = place[0], place[1]
    heads = piece.shape[0] // (2 * GRAIN)
    for side, pair in enumerate(((wq, wk), (wv, wo))):

        @pl.when(core == side)
        def _():
            copies = []
            for t, ref in enumerate(pair):
                for h in range(heads):
                    start = pl.multiple_of(h * HEAD_DIM + plane * GRAIN, GRAIN)
                    to = (t * heads + h) * GRAIN
                    copies.append(
                        pltpu.make_async_copy(
                            ref.at[pl.ds(start, GRAIN), :],
                            piece.at[to : to + GRAIN, :],
                            sems.at[t * heads + h],
                        )
                    )
            for copy in copies:
                copy.start()
            for copy in copies:
                copy.wait()


def piece_heads(place, *weights):
    local, width = weights[0].shape
    heads = local // HEAD_DIM
    return pl.pallas_call(
        piece_heads_kernel,
        in_specs=[scalar_spec()] + [token_spec()] * 4,
        out_specs=held_spec(),
        out_shape=shape((2 * heads * GRAIN, width), BF),
        scratch_shapes=[pltpu.SemaphoreType.DMA((2 * heads,))],
        compiler_params=params(),
        cost_estimate=cost(1),
        name="piece_heads",
    )(place, *weights)


def piece_feed_kernel(place, wu, wd, rest, turned, piece_up, piece_down):
    core, plane = place[0], place[1]
    sub = piece_down.shape[1]
    turned[...] = wu[...].astype(F32).T.astype(BF)
    start = pl.multiple_of((core * 4 + plane) * sub, GRAIN)
    for r in range(piece_up.shape[0]):
        piece_up[r, :sub, :] = turned[pl.ds(start, sub), :]
        piece_up[r, sub:, :] = rest[...]
        piece_down[r] = wd[pl.ds(start, sub), :]


def piece_feed(place, wu, wd, rest, n_mp):
    width, hidden = wu.shape
    sub = hidden // 8
    return pl.pallas_call(
        piece_feed_kernel,
        in_specs=[scalar_spec()] + [held_spec()] * 3,
        out_specs=[held_spec()] * 3,
        out_shape=[
            shape((hidden, width), BF),
            shape((n_mp, sub + GRAIN, width), BF),
            shape((n_mp, sub, width), BF),
        ],
        compiler_params=params(),
        cost_estimate=cost(3),
        name="piece_feed",
    )(place, wu, wd, rest)


def finish_feed_kernel(place, *refs):
    pieces, (up, down, held) = refs[:8], refs[-3:]
    core, plane = place[0], place[1]
    sub = pieces[0].shape[0] // 2
    for c in range(2):
        for g, ref in enumerate(pieces[4 * c : 4 * c + 4]):
            chip = plane ^ neighbour(core ^ c, g)
            start = pl.multiple_of(((core ^ c) * 4 + chip) * sub, GRAIN)
            held[pl.ds(start, sub), :] = ref[:sub, :].astype(F32)
            down[pl.ds(start, sub), :] = ref[sub:, :].astype(F32)
    up[...] = held[...].T


def finish_feed(place, pieces, *tokens):
    rows, width = pieces[0].shape
    return pl.pallas_call(
        finish_feed_kernel,
        in_specs=[scalar_spec()] + [held_spec()] * 8 + [token_spec() for _ in tokens],
        out_specs=[held_spec()] * 2,
        out_shape=[shape((width, 4 * rows), F32), shape((4 * rows, width), F32)],
        scratch_shapes=[pltpu.VMEM((4 * rows, width), F32)],
        compiler_params=params(),
        cost_estimate=cost(6),
        name="finish_feed",
    )(place, *pieces, *tokens)


def finish_heads_kernel(place, mine, other, *outs):
    core = place[0]
    heads = outs[0].shape[0] // HEAD_DIM
    for side in range(2):

        @pl.when(core == side)
        def _():
            for c, ref in enumerate((mine, other)):
                for t in range(2):
                    out = outs[2 * (side ^ c) + t]
                    for g in range(4):
                        for h in range(heads):
                            at = h * HEAD_DIM + g * GRAIN
                            row = (t * heads + h) * GRAIN
                            out[at : at + GRAIN, :] = ref[g, row : row + GRAIN, :].astype(F32)


def finish_heads(place, pieces):
    _, rows, width = pieces[0].shape
    local = rows // (2 * GRAIN) * HEAD_DIM
    return pl.pallas_call(
        finish_heads_kernel,
        in_specs=[scalar_spec()] + [held_spec()] * 2,
        out_specs=[held_spec()] * 4,
        out_shape=[shape((local, width), F32)] * 4,
        compiler_params=params(),
        cost_estimate=cost(2),
        name="finish_heads",
    )(place, *pieces)


def turn_swap(block, bits, n_dp):
    return lax.ppermute(block, "dp", [(i, i ^ bits[i & 1]) for i in range(n_dp)])


def first_swap(block, n_dp):
    return turn_swap(block, (XBIT, YBIT), n_dp)


def second_swap(block, n_dp):
    return turn_swap(block, (YBIT, XBIT), n_dp)


def core_swap(block, n_dp):
    return swap(block, "dp", CORE, n_dp)


def exchange(block, axis, groups=None):
    return lax.all_to_all(block, axis, 0, 0, axis_index_groups=groups, tiled=True)


def spread(block, n):
    return jnp.broadcast_to(block[None], (n, *block.shape))


def plane_groups(n_dp):
    return [[8 * e + 2 * g + c for g in range(4)] for e in range(n_dp // 8) for c in range(2)]


def add(*terms):
    total = terms[0].astype(F32)
    for term in terms[1:]:
        total = total + term.astype(F32)
    return total.astype(BF)


def chip_sum(keep, got):
    return add(keep[0::2], got[0::2]), add(keep[1::2], got[1::2])


def side_sum(stay, got):
    return add(stay[0], got[0]), add(stay[1], got[1])


def shard_sum(own, got, n_dp):
    total = own.astype(F32)
    for part in got:
        total = total + part.astype(F32)
    bit = 8
    while bit < n_dp:
        total = total + swap(total, "dp", bit, n_dp)
        bit *= 2
    return total.astype(BF)


def plane_gather(four, n_dp):
    return exchange(four, "dp", plane_groups(n_dp))


def project_kernel(place, x, wq, wk, wv, wo, bq, bv, *refs):
    pieces, (q, k, v, out, full, sems, sem) = refs[:8], refs[-7:]
    last = pltpu.make_async_copy(full, out, sem)
    core, plane, shard = place[0], place[1], place[2]
    heads = wq.shape[0] // HEAD_DIM
    shards = 1 + pieces[0].shape[0] // (2 * heads * GRAIN)

    @pl.when(pl.program_id(0) == 0)
    def _():
        copies = []
        base = pl.multiple_of(shard * heads * HEAD_DIM, HEAD_DIM)
        for kind, ref in enumerate((wq, wk, wv, wo)):
            for h in range(heads):
                for g in range(4):
                    source = plane ^ neighbour(kind // 2, g)
                    at = pl.multiple_of(h * HEAD_DIM + source * GRAIN, GRAIN)
                    to = pl.multiple_of(base + h * HEAD_DIM + g * GRAIN, GRAIN)
                    copies.append(
                        pltpu.make_async_copy(
                            ref.at[pl.ds(at, GRAIN), :],
                            full.at[kind, pl.ds(to, GRAIN), :],
                            sems.at[len(copies)],
                        )
                    )
        for copy in copies:
            copy.start()
        for c in range(2):
            for g, ref in enumerate(pieces[4 * c : 4 * c + 4]):
                for r in range(1, shards):
                    base = pl.multiple_of((shard ^ r) * heads * HEAD_DIM, HEAD_DIM)
                    for t in range(2):
                        for h in range(heads):
                            row = (((r - 1) * 2 + t) * heads + h) * GRAIN
                            to = pl.multiple_of(base + h * HEAD_DIM + g * GRAIN, GRAIN)
                            full[(core ^ c) * 2 + t, pl.ds(to, GRAIN), :] = ref[
                                row : row + GRAIN, :
                            ]
        for copy in copies:
            copy.wait()
        last.start()

    block = x[...]
    for kind, (into, bias) in enumerate(((q, bq), (k, None), (v, bv))):
        value = lax.dot_general(block, full[kind], NT, preferred_element_type=F32)
        if bias is not None:
            value = value + bias[...]
        into[...] = value.astype(BF)

    @pl.when(pl.program_id(0) == pl.num_programs(0) - 1)
    def _():
        last.wait()


def project(place, x, weights, bq, bv, pieces, *tokens):
    rows, width = x.shape
    block = rows_spec(ROW_BLOCK, width)
    return pl.pallas_call(
        project_kernel,
        grid=(rows // ROW_BLOCK,),
        in_specs=[scalar_spec(), block]
        + [token_spec()] * 4
        + [whole_spec(a.shape) for a in (bq, bv, *pieces)]
        + [token_spec() for _ in tokens],
        out_specs=[block, block, block, token_spec()],
        out_shape=[shape((rows, width), BF)] * 3 + [shape((4, width, width), BF)],
        scratch_shapes=[
            pltpu.VMEM((4, width, width), BF),
            pltpu.SemaphoreType.DMA((weights[0].shape[0] // GRAIN * 4,)),
            pltpu.SemaphoreType.DMA,
        ],
        compiler_params=params(),
        cost_estimate=cost(10),
        name="project",
    )(place, x, *weights, bq, bv, *pieces, *tokens)


def spread_heads(block):
    lane = lax.broadcasted_iota(jnp.int32, block.shape, 1) // HEAD_DIM
    return jnp.concatenate(
        [jnp.where(lane == h, block, jnp.zeros_like(block)) for h in range(4)], axis=0
    )


def gather_heads(stacked):
    rows = stacked.shape[0] // 4
    lane = lax.broadcasted_iota(jnp.int32, (rows, GROUP), 1) // HEAD_DIM
    out = stacked[:rows]
    for h in range(1, 4):
        out = jnp.where(lane == h, stacked[h * rows : (h + 1) * rows], out)
    return out


def window_start(step, rows):
    return pl.multiple_of(jnp.clip(step - 1, 0, (rows - WINDOW) // BLOCK) * BLOCK, BLOCK)


def attend_kernel(part, q, k, v, segc, segr, x, wo, bo, gain, shift, *refs):
    ctx, saved, unit, low = refs[-4:]
    start = window_start(part * pl.num_programs(0) + pl.program_id(0), k.shape[0])
    near = pl.ds(start, WINDOW)
    penalty = jnp.where(segc[...] == segr[:, near], 0.0, MASKED)
    lane = lax.broadcasted_iota(jnp.int32, (BLOCK, 128), 1)
    groups = q.shape[1] // GROUP

    def score_group(group):
        cols = slice(group * GROUP, (group + 1) * GROUP)
        return lax.dot_general(
            spread_heads(q[:, cols] * SCALE), k[near, cols], NT, preferred_element_type=F32
        )

    keep = jnp.zeros((BLOCK, 128), F32)
    ahead = score_group(0)
    for group in range(groups):
        cols = slice(group * GROUP, (group + 1) * GROUP)
        logits = ahead.reshape(4, BLOCK, WINDOW) + penalty[None]
        if group + 1 < groups:
            ahead = score_group(group + 1)
        peak = jnp.max(logits, axis=-1, keepdims=True)
        raised = jnp.exp(logits - peak)
        sums = jnp.sum(raised, axis=-1, keepdims=True)
        context = jnp.dot(
            raised.astype(BF).reshape(4 * BLOCK, WINDOW), v[near, cols], preferred_element_type=F32
        )
        context = (context.reshape(4, BLOCK, GROUP) * (1.0 / sums)).reshape(4 * BLOCK, GROUP)
        ctx[:, cols] = gather_heads(context).astype(BF)
        log_total = peak + jnp.log(sums)
        for h in range(4):
            keep = jnp.where(lane == group * 4 + h, log_total[h], keep)
    attended = jnp.dot(ctx[...], wo[0], preferred_element_type=F32) + bo[...]
    total = x[...].astype(F32) + attended
    centred = total - jnp.mean(total, axis=-1, keepdims=True)
    inv_std = lax.rsqrt(jnp.mean(centred * centred, axis=-1, keepdims=True) + EPSILON)
    unit_val = centred * inv_std
    unit[...] = unit_val
    low[...] = (unit_val * gain[...] + shift[...]).astype(BF)
    saved[...] = jnp.where(lane == 127, inv_std, keep)


def attend(part, parts, q, k, v, segc, segr, x, full, bo, gain, shift, held, *tokens):
    rows, width = q.shape
    steps = rows // BLOCK // parts

    def block(wide):
        return pl.BlockSpec((BLOCK, wide), lambda i: (part * steps + i, 0))

    return pl.pallas_call(
        functools.partial(attend_kernel, part),
        grid=(steps,),
        in_specs=[
            block(width),
            whole_spec((rows, width)),
            whole_spec((rows, width)),
            block(1),
            whole_spec((1, rows)),
            block(width),
            pl.BlockSpec((1, width, width), lambda i: (3, 0, 0), pipeline_mode=pl.Buffered(1)),
            whole_spec((1, width)),
            whole_spec((1, width)),
            whole_spec((1, width)),
        ]
        + [token_spec() for _ in (*held, *tokens)],
        out_specs=[block(width), block(128), block(width), block(width)],
        out_shape=[
            shape((rows, width), BF),
            shape((rows, 128), F32),
            shape((rows, width), F32),
            shape((rows, width), BF),
        ],
        input_output_aliases={10 + i: i for i in range(len(held))},
        compiler_params=params(),
        cost_estimate=cost(16 / parts),
        name="attend",
    )(q, k, v, segc, segr, x, full, bo, gain, shift, *held, *tokens)


def whole_order(rows, plane):
    width = rows.shape[1]
    rank = (lax.broadcasted_iota(jnp.int32, rows.shape, 1) // GRAIN) % 4
    row = lax.broadcasted_iota(jnp.int32, rows.shape, 0)

    def shifted(block, by):
        return pltpu.roll(block, by % width, 1)

    middle = jnp.where(rank == 1, shifted(rows, -GRAIN), shifted(rows, GRAIN))
    swapped = (row == 7) & ((rank == 1) | (rank == 2))
    rows = jnp.where(swapped, middle, rows)
    for bit in (1, 2):
        by = bit * GRAIN
        other = jnp.where((rank & bit) == 0, shifted(rows, -by), shifted(rows, by))
        rows = jnp.where((plane & bit) == 0, rows, other)
    return rows


def attend_back_kernel(place, q, k, v, do, saved, inner, segc, segr, *refs):
    dq, dk, dv, sums, dk_sum, dv_sum = refs[-6:]
    step = pl.program_id(0)

    @pl.when(step == 0)
    def _():
        dk_sum[...] = jnp.zeros_like(dk_sum)
        dv_sum[...] = jnp.zeros_like(dv_sum)
        sums[...] = jnp.zeros_like(sums)

    start = window_start(step, k.shape[0])
    near = pl.ds(start, WINDOW)
    penalty = jnp.where(segc[...] == segr[:, near], 0.0, MASKED)
    for group in range(q.shape[1] // GROUP):
        cols = slice(group * GROUP, (group + 1) * GROUP)
        q4 = spread_heads(q[:, cols] * SCALE)
        do4 = spread_heads(do[:, cols])
        k4 = k[near, cols]
        logits = lax.dot_general(q4, k4, NT, preferred_element_type=F32)
        logits = logits.reshape(4, BLOCK, WINDOW) + penalty[None]
        lse = jnp.stack([saved[:, group * 4 + h : group * 4 + h + 1] for h in range(4)])
        mean_grad = jnp.stack([inner[:, group * 4 + h : group * 4 + h + 1] for h in range(4)])
        probs = jnp.exp(logits - lse)
        weight_grad = lax.dot_general(
            do4, v[near, cols], NT, preferred_element_type=F32
        ).reshape(4, BLOCK, WINDOW)
        logit_grad = (probs * (weight_grad - mean_grad)).astype(BF).reshape(4 * BLOCK, WINDOW)
        probs_low = probs.astype(BF).reshape(4 * BLOCK, WINDOW)
        dq_low = (
            gather_heads(jnp.dot(logit_grad, k4, preferred_element_type=F32)) * SCALE
        ).astype(BF)
        dq[:, cols] = dq_low
        sums[6:7, cols] += jnp.sum(dq_low.astype(F32), axis=0, keepdims=True)
        dk_sum[near, cols] += lax.dot_general(logit_grad, q4, TN, preferred_element_type=F32)
        dv_sum[near, cols] += lax.dot_general(probs_low, do4, TN, preferred_element_type=F32)

    @pl.when(step == pl.num_programs(0) - 1)
    def _():
        dk[...] = dk_sum[...].astype(BF)
        dv_low = dv_sum[...].astype(BF)
        dv[...] = dv_low
        sums[7:8, :] = jnp.sum(dv_low.astype(F32), axis=0, keepdims=True)
        sums[...] = whole_order(sums[...], place[1])


def attend_back(place, q, k, v, do, saved, inner, segc, segr, *tokens):
    rows, width = q.shape
    block = rows_spec(BLOCK, width)
    full = whole_spec((rows, width))
    return pl.pallas_call(
        attend_back_kernel,
        grid=(rows // BLOCK,),
        in_specs=[
            scalar_spec(),
            block,
            full,
            full,
            block,
            rows_spec(BLOCK, 128),
            rows_spec(BLOCK, 128),
            rows_spec(BLOCK, 1),
            whole_spec((1, rows)),
        ]
        + [token_spec() for _ in tokens],
        out_specs=[block, fixed_spec((rows, width)), fixed_spec((rows, width)), fixed_spec((8, width))],
        out_shape=[shape((rows, width), BF)] * 3 + [shape((8, width), F32)],
        scratch_shapes=[pltpu.VMEM((rows, width), F32)] * 2,
        compiler_params=params(),
        cost_estimate=cost(22),
        name="attend_back",
    )(place, q, k, v, do, saved, inner, segc, segr, *tokens)


def assemble(place, own, pieces, into):
    core, plane, shard = place[0], place[1], place[2]
    sub = own.shape[0] // 8
    shards = 1 + pieces[0].shape[0] // sub

    def rows(c, g, r):
        return pl.ds(pl.multiple_of(((c * 4 + g) * shards + (shard ^ r)) * sub, GRAIN), sub)

    for c in range(2):
        for g, ref in enumerate(pieces[4 * c : 4 * c + 4]):
            at = pl.multiple_of(((core ^ c) * 4 + (plane ^ neighbour(core ^ c, g))) * sub, GRAIN)
            into[rows(c, g, 0), :] = own[pl.ds(at, sub), :]
            for r in range(1, shards):
                into[rows(c, g, r), :] = ref[(r - 1) * sub : r * sub, :]


def feed_up_kernel(place, x, own, bu, *refs):
    pieces, (act, slope, out, wu, sem) = refs[:8], refs[-5:]
    copy = pltpu.make_async_copy(wu, out, sem)

    @pl.when(pl.program_id(0) == 0)
    def _():
        assemble(place, own, pieces, wu)
        copy.start()

    block = x[...]
    for at in range(0, wu.shape[0], 256):
        span = slice(at, at + 256)
        pre = (
            lax.dot_general(block, wu[span, :], NT, preferred_element_type=F32) + bu[:, span]
        )
        below = 0.5 * (1.0 + lax.erf(pre * 0.7071067811865476))
        density = jnp.exp(-0.5 * pre * pre) * 0.3989422804014327
        act[:, span] = (pre * below).astype(BF)
        slope[:, span] = (below + pre * density).astype(BF)

    @pl.when(pl.program_id(0) == pl.num_programs(0) - 1)
    def _():
        copy.wait()


def feed_up(place, x, own, bu, pieces, *tokens):
    rows, width = x.shape
    hidden = bu.shape[1]
    wide = rows_spec(ROW_BLOCK, hidden)
    return pl.pallas_call(
        feed_up_kernel,
        grid=(rows // ROW_BLOCK,),
        in_specs=[scalar_spec(), rows_spec(ROW_BLOCK, width)]
        + [whole_spec(a.shape) for a in (own, bu, *pieces)]
        + [token_spec() for _ in tokens],
        out_specs=[wide, wide, token_spec()],
        out_shape=[shape((rows, hidden), BF)] * 2 + [shape((hidden, width), BF)],
        scratch_shapes=[pltpu.VMEM((hidden, width), BF), pltpu.SemaphoreType.DMA],
        compiler_params=params(),
        cost_estimate=cost(12),
        name="feed_up",
    )(place, x, own, bu, *pieces, *tokens)


def feed_down_kernel(place, act, unit, cot, own, vectors, *refs):
    pieces, outs = refs[:8], refs[-8:]
    layer, output, second, down_grad, sums, out, wd, sem = outs
    copy = pltpu.make_async_copy(wd, out, sem)

    @pl.when(pl.program_id(0) == 0)
    def _():
        sums[...] = jnp.zeros_like(sums)
        assemble(place, own, pieces, wd)
        copy.start()

    down = jnp.dot(act[...], wd[...], preferred_element_type=F32)
    b_down, first_gain, first_shift, second_gain, second_shift = (
        vectors[i : i + 1, :] for i in range(5)
    )
    total = unit[...] * first_gain + first_shift + down + b_down
    centred = total - jnp.mean(total, axis=-1, keepdims=True)
    inv_std = lax.rsqrt(jnp.mean(centred * centred, axis=-1, keepdims=True) + EPSILON)
    unit_val = centred * inv_std
    layer_out = unit_val * second_gain + second_shift
    layer[...] = layer_out
    output[...] = layer_out.astype(BF)
    grad = cot[...].astype(F32)
    scaled = grad * second_gain
    inner = (
        scaled
        - jnp.mean(scaled, axis=-1, keepdims=True)
        - unit_val * jnp.mean(scaled * unit_val, axis=-1, keepdims=True)
    )
    second_grad = inv_std * inner
    second[...] = second_grad
    grad_low = second_grad.astype(BF)
    down_grad[...] = grad_low
    sums[3:4, :] += jnp.sum(grad_low.astype(F32), axis=0, keepdims=True)
    sums[4:5, :] += jnp.sum(grad * unit_val, axis=0, keepdims=True)
    sums[5:6, :] += jnp.sum(grad, axis=0, keepdims=True)

    @pl.when(pl.program_id(0) == pl.num_programs(0) - 1)
    def _():
        copy.wait()


def feed_down(place, act, unit, cot, own, vectors, pieces):
    rows, hidden = act.shape
    width = unit.shape[1]
    block = rows_spec(ROW_BLOCK, width)
    return pl.pallas_call(
        feed_down_kernel,
        grid=(rows // ROW_BLOCK,),
        in_specs=[scalar_spec(), rows_spec(ROW_BLOCK, hidden), block, block]
        + [whole_spec(a.shape) for a in (own, vectors, *pieces)],
        out_specs=[block, block, block, block, fixed_spec((8, width)), token_spec()],
        out_shape=[
            shape((rows, width), F32),
            shape((rows, width), BF),
            shape((rows, width), F32),
            shape((rows, width), BF),
            shape((8, width), F32),
            shape((hidden, width), BF),
        ],
        scratch_shapes=[pltpu.VMEM((hidden, width), BF), pltpu.SemaphoreType.DMA],
        compiler_params=params(),
        cost_estimate=cost(13),
        name="feed_down",
    )(place, act, unit, cot, own, vectors, *pieces)


def feed_back_kernel(place, grad, x, wu, wd, slope, act, keep, send, bias, out, held):
    step = pl.program_id(0)
    half = pl.num_programs(0) // 2
    chips, shards, _, sub, width = keep.shape

    @pl.when(step == 0)
    def _():
        out[...] = jnp.zeros_like(out)
        bias[...] = jnp.zeros_like(bias)

    total = None
    for at in range(0, x.shape[0], ROW_BLOCK):
        span = slice(at, at + ROW_BLOCK)
        act_grad = lax.dot_general(grad[span, :], wd[...], NT, preferred_element_type=F32)
        low = (act_grad * slope[span, :].astype(F32)).astype(BF)
        held[span, :] = low
        term = jnp.sum(low.astype(F32), axis=0, keepdims=True)
        total = term if total is None else total + term
    core, plane = place[0], place[1]
    owner = jnp.where(step < half, core ^ 1, core)
    row = lax.broadcasted_iota(jnp.int32, (bias.shape[0], sub), 0)
    for g in range(chips):
        early = plane ^ jnp.where(owner == 0, neighbour(0, g), neighbour(1, g))
        late = plane ^ jnp.where(owner == 0, neighbour(0, 2 + g), neighbour(1, 2 + g))
        target = owner * 4 + jnp.where(lax.rem(step, half) == 0, early, late)
        for r in range(shards):
            at = (g * shards + r) * sub
            lanes = slice(r * 128, r * 128 + sub)
            bias[:, lanes] = jnp.where(row == target, total[:, at : at + sub], bias[:, lanes])
    out[...] += jnp.dot(held[...], wu[...], preferred_element_type=F32)
    dims = (chips, shards, sub, width)
    up = lax.dot_general(held[...], x[...], TN, preferred_element_type=F32).astype(BF)
    down = lax.dot_general(act[...], grad[...], TN, preferred_element_type=F32).astype(BF)

    @pl.when(step < half)
    def _():
        send[:, :, 0] = up.reshape(dims)
        send[:, :, 1] = down.reshape(dims)

    @pl.when(step >= half)
    def _():
        keep[:, :, 0] = up.reshape(dims)
        keep[:, :, 1] = down.reshape(dims)


def feed_back(place, grad, x, wu, wd, slope, act, n_mp):
    rows, width = x.shape
    hidden = wu.shape[0]
    span = hidden // 4
    full = whole_spec((rows, width))
    weight = pl.BlockSpec((span, width), lambda j: ((j + 2) % 4, 0))
    wide = pl.BlockSpec((rows, span), lambda j: (0, (j + 2) % 4))
    dims = (4, n_mp, 2, hidden // 8 // n_mp, width)
    block = (2, *dims[1:])
    return pl.pallas_call(
        feed_back_kernel,
        grid=(4,),
        in_specs=[scalar_spec(), full, full, weight, weight, wide, wide],
        out_specs=[
            pl.BlockSpec(block, lambda j: (jnp.maximum(j - 2, 0), 0, 0, 0, 0)),
            pl.BlockSpec(block, lambda j: (jnp.minimum(j, 1), 0, 0, 0, 0)),
            fixed_spec((8, 128 * n_mp)),
            fixed_spec((rows, width)),
        ],
        out_shape=[
            shape(dims, BF),
            shape(dims, BF),
            shape((8, 128 * n_mp), F32),
            shape((rows, width), F32),
        ],
        scratch_shapes=[pltpu.VMEM((rows, span), BF)],
        compiler_params=params(),
        cost_estimate=cost(27),
        name="feed_back",
    )(place, grad, x, wu, wd, slope, act)


def middle_kernel(normed, second, unit, saved, ctx, wo, gain, *refs):
    first, context_grad, inner_sum, weight, sums, held, lows = refs[-7:]
    step = pl.program_id(0)
    grad = normed[...] + second[...]
    unit_val = unit[...]
    scaled = grad * gain[...]
    inner = (
        scaled
        - jnp.mean(scaled, axis=-1, keepdims=True)
        - unit_val * jnp.mean(scaled * unit_val, axis=-1, keepdims=True)
    )
    first_grad = saved[:, 127:128] * inner
    first[...] = first_grad
    low = first_grad.astype(BF)
    context_low = lax.dot_general(low, wo[0], NT, preferred_element_type=F32).astype(BF)
    context_grad[...] = context_low
    product = context_low.astype(F32) * ctx[...].astype(F32)
    high = product.astype(BF)
    rest = (product - high.astype(F32)).astype(BF)
    width = product.shape[1]
    head = lax.broadcasted_iota(jnp.int32, (width, 128), 0) // HEAD_DIM
    head = (head == lax.broadcasted_iota(jnp.int32, (width, 128), 1)).astype(BF)
    inner_sum[...] = jnp.dot(high, head, preferred_element_type=F32) + jnp.dot(
        rest, head, preferred_element_type=F32
    )
    at = pl.ds(pl.multiple_of(step * ROW_BLOCK, ROW_BLOCK), ROW_BLOCK)
    lows[at, :] = low
    held[at, :] = ctx[...]

    @pl.when(step == 0)
    def _():
        sums[...] = jnp.zeros_like(sums)

    sums[0:1, :] += jnp.sum(low.astype(F32), axis=0, keepdims=True)
    sums[1:2, :] += jnp.sum(grad * unit_val, axis=0, keepdims=True)
    sums[2:3, :] += jnp.sum(grad, axis=0, keepdims=True)

    @pl.when(step == pl.num_programs(0) - 1)
    def _():
        weight[...] = lax.dot_general(
            held[...], lows[...], TN, preferred_element_type=F32
        ).astype(BF)


def middle(normed, second, unit, saved, ctx, full, gain, *tokens):
    rows, width = normed.shape
    block = rows_spec(ROW_BLOCK, width)
    return pl.pallas_call(
        middle_kernel,
        grid=(rows // ROW_BLOCK,),
        in_specs=[
            block,
            block,
            block,
            rows_spec(ROW_BLOCK, 128),
            block,
            pl.BlockSpec((1, width, width), lambda i: (3, 0, 0), pipeline_mode=pl.Buffered(1)),
            whole_spec((1, width)),
        ]
        + [token_spec() for _ in tokens],
        out_specs=[block, block, rows_spec(ROW_BLOCK, 128), fixed_spec((width, width)), fixed_spec((8, width))],
        out_shape=[
            shape((rows, width), F32),
            shape((rows, width), BF),
            shape((rows, 128), F32),
            shape((width, width), BF),
            shape((8, width), F32),
        ],
        scratch_shapes=[pltpu.VMEM((rows, width), BF)] * 2,
        compiler_params=params(),
        cost_estimate=cost(8),
        name="middle",
    )(normed, second, unit, saved, ctx, full, gain, *tokens)


def head_weights_kernel(place, dq, dk, dv, x, wo, *refs):
    keep, send, pairs, loaded, held, sems, out_sems = refs[-7:]
    core = place[0]
    shards, heads = keep.shape[1], keep.shape[3]
    width = x.shape[1]
    copies = [
        pltpu.make_async_copy(ref, loaded.at[n], sems.at[n])
        for n, ref in enumerate((dq, dk, dv, x))
    ] + [pltpu.make_async_copy(wo, loaded.at[4, :width, :], sems.at[4])]
    for n in (3, 0, 1, 2, 4):
        copies[n].start()
    copies[3].wait()

    def out_copy(pair, side):
        return pltpu.make_async_copy(
            pairs.at[pair], keep if side == pair else send, out_sems.at[pair]
        )

    for kind in range(4):
        if kind < 3:
            copies[kind].wait()
            held[...] = lax.dot_general(
                loaded[kind], loaded[3], TN, preferred_element_type=F32
            ).astype(BF)
        else:
            copies[4].wait()
        for r in range(shards):
            for h in range(heads):
                for g in range(4):
                    at = (r * heads + h) * HEAD_DIM + g * GRAIN
                    rows = slice(at, at + GRAIN)
                    value = held[rows, :] if kind < 3 else loaded[4, rows, :]
                    pairs[kind // 2, g, r, kind % 2, h] = value
        for side in range(2):
            if kind % 2 == 1:

                @pl.when(core == side)
                def _():
                    out_copy(kind // 2, side).start()

    for side in range(2):

        @pl.when(core == side)
        def _():
            for pair in range(2):
                out_copy(pair, side).wait()


def head_weights(place, dq, dk, dv, x, wo, n_mp, *tokens):
    rows, width = x.shape
    heads = width // HEAD_DIM // n_mp
    dims = (4, n_mp, 2, heads, GRAIN, width)
    keep, send = pl.pallas_call(
        head_weights_kernel,
        in_specs=[scalar_spec()] + [token_spec()] * 5 + [token_spec() for _ in tokens],
        out_specs=[token_spec()] * 2,
        out_shape=[shape(dims, BF)] * 2,
        scratch_shapes=[
            pltpu.VMEM((2, *dims), BF),
            pltpu.VMEM((5, rows, width), BF),
            pltpu.VMEM((width, width), BF),
            pltpu.SemaphoreType.DMA((5,)),
            pltpu.SemaphoreType.DMA((2,)),
        ],
        compiler_params=params(),
        cost_estimate=cost(9),
        name="head_weights",
    )(place, dq, dk, dv, x, wo, *tokens)
    dims = (4, n_mp, 2 * heads * GRAIN, width)
    return keep.reshape(dims), send.reshape(dims)


def input_kernel(dq, dk, dv, full, first, *refs):
    out = refs[-1]
    total = first[...]
    for kind, ref in enumerate((dq, dk, dv)):
        total = total + jnp.dot(ref[...], full[kind], preferred_element_type=F32)
    out[...] = total


def input_gradient(dq, dk, dv, full, first, *tokens):
    rows, width = dq.shape
    block = rows_spec(ROW_BLOCK, width)
    return pl.pallas_call(
        input_kernel,
        grid=(rows // ROW_BLOCK,),
        in_specs=[
            block,
            block,
            block,
            pl.BlockSpec((3, width, width), lambda i: (0, 0, 0), pipeline_mode=pl.Buffered(1)),
            block,
        ]
        + [token_spec() for _ in tokens],
        out_specs=block,
        out_shape=shape((rows, width), F32),
        compiler_params=params(),
        cost_estimate=cost(6),
        name="input_gradient",
    )(dq, dk, dv, full, first, *tokens)


def score_kernel(out_ref, segr_ref, len_ref, table_ref, pick_ref, *refs):
    score_ref = refs[-1]
    queries = pick_ref.shape[0]
    rows = out_ref.shape[0]
    label = lax.broadcasted_iota(jnp.int32, (queries, rows), 0)
    onehot = (label == segr_ref[...]).astype(F32)
    sums = jnp.dot(
        onehot, out_ref[...], precision=lax.Precision.HIGHEST, preferred_element_type=F32
    )
    means = sums / len_ref[...].astype(F32)
    every = lax.dot_general(
        means,
        table_ref[...].astype(F32),
        NT,
        precision=lax.Precision.HIGHEST,
        preferred_element_type=F32,
    )
    at = lax.broadcasted_iota(jnp.int32, every.shape, 1)
    column = lax.broadcasted_iota(jnp.int32, pick_ref.shape, 1)
    result = jnp.zeros(pick_ref.shape, F32)
    for p in range(pick_ref.shape[1]):
        chosen = jnp.sum(
            jnp.where(at == pick_ref[:, p : p + 1], every, 0.0), axis=1, keepdims=True
        )
        result = jnp.where(column == p, chosen, result)
    score_ref[...] = result


def score(layer_out, segr, lengths, table, picks, *tokens):
    return pl.pallas_call(
        score_kernel,
        in_specs=[held_spec()] * 5 + [token_spec() for _ in tokens],
        out_specs=held_spec(),
        out_shape=shape(picks.shape, F32),
        compiler_params=params(),
        cost_estimate=cost(8),
        name="score",
    )(layer_out, segr, lengths, table, picks, *tokens)


def per_device(
    n_dp,
    n_mp,
    hidden_in,
    cotangent,
    query_lengths,
    passage_index,
    passages,
    w_query,
    w_key,
    w_value,
    w_output,
    w_up,
    w_down,
    b_query,
    b_value,
    b_output,
    b_up,
    b_down,
    first_gain,
    first_shift,
    second_gain,
    second_shift,
):
    rows, width = hidden_in.shape
    heads = w_query.shape[1] // HEAD_DIM
    sub = w_up.shape[1] // 8
    at_dp = lax.axis_index("dp")
    core, plane = at_dp & 1, (at_dp >> 1) & 3
    shard = lax.axis_index("mp")
    place = jnp.stack([core, plane, shard]).astype(jnp.int32)
    own_heads = (w_query.T, w_key.T, w_value.T, w_output)

    cut = heads * HEAD_DIM
    heads_piece = piece_heads(place, *own_heads)
    bias_rows = jnp.stack(
        [jnp.pad(b_query, (0, width - cut)), jnp.pad(b_value, (0, width - cut)), b_up]
    )
    rest = jnp.pad(after(bias_rows, heads_piece), ((0, GRAIN - 3), (0, 0)))
    turned, up_piece, down_piece = piece_feed(place, w_up, w_down, rest, n_mp)
    heads_parts = [swap(after(heads_piece, rest), "mp", 1, n_mp)] + [
        swap(heads_piece, "mp", r, n_mp) for r in range(2, n_mp)
    ]
    up_got = exchange(up_piece, "mp")
    heads_shards = jnp.concatenate(heads_parts)
    heads_first = first_swap(heads_shards, n_dp)
    heads_second = second_swap(heads_shards, n_dp)
    heads_corner = second_swap(after(heads_first, heads_second), n_dp)
    heads_other = [core_swap(p, n_dp) for p in (heads_shards, heads_first, heads_second)]
    heads_corner, up_got = lax.optimization_barrier((heads_corner, up_got))
    heads_mine = [heads_shards, heads_first, heads_second, heads_corner]
    heads_other = heads_other + [core_swap(heads_corner, n_dp)]

    def others(got):
        return jnp.concatenate(
            [
                lax.dynamic_index_in_dim(got, shard ^ r, 0, keepdims=False)[:sub]
                for r in range(1, n_mp)
            ]
        )

    up_shards = others(after(up_got, *heads_mine, *heads_other))
    up_first = first_swap(up_shards, n_dp)
    up_second = second_swap(up_shards, n_dp)

    ranks = lax.broadcasted_iota(jnp.int32, (4, 4), 0)
    places4 = lax.broadcasted_iota(jnp.int32, (4, 4), 1)
    turned_ranks = jnp.where((ranks == 1) | (ranks == 2), ranks ^ 3, ranks)
    order_q = ((plane ^ ranks) == places4).astype(F32)
    order_v = ((plane ^ turned_ranks) == places4).astype(F32)
    owner = (core ^ jnp.arange(2, dtype=jnp.int32)).reshape(2, 1, 1, 1)
    is_owner = (owner == jnp.arange(2, dtype=jnp.int32).reshape(1, 1, 2, 1)).astype(F32)
    order_up = jnp.where(owner == 0, order_q[None, :, None], order_v[None, :, None])
    order_up = (order_up * is_owner).reshape(8, 8)
    exact = functools.partial(
        jnp.einsum, precision=lax.Precision.HIGHEST, preferred_element_type=F32
    )
    all_bias = up_got[:, sub : sub + 3].astype(F32)
    by_head = (n_mp, heads, 4, GRAIN)
    query_bias = exact("gk,zhki->zhgi", order_q, all_bias[:, 0, :cut].reshape(by_head))
    value_bias = exact("gk,zhki->zhgi", order_v, all_bias[:, 1, :cut].reshape(by_head))
    up_bias = exact("gk,zki->gzi", order_up, all_bias[:, 2].reshape(n_mp, 8, sub))
    query_bias, value_bias, up_bias = (
        b.reshape(1, -1) for b in (query_bias, value_bias, up_bias)
    )

    ends = jnp.cumsum(query_lengths, axis=-1, dtype=jnp.int32)
    places = lax.broadcasted_iota(jnp.int32, (rows, query_lengths.shape[1]), 0)
    seg = jnp.sum((places >= ends).astype(jnp.int32), axis=-1)
    segc, segr = seg.reshape(rows, 1), seg.reshape(1, rows)
    vectors = jnp.stack(
        [b_down, first_gain, first_shift, second_gain, second_shift, b_output, b_output, b_output]
    ).astype(F32)

    query, key, value, full = project(
        place, hidden_in, own_heads, query_bias, value_bias, heads_mine + heads_other
    )
    up_first, up_second, query = lax.optimization_barrier((up_first, up_second, query))
    down_got = exchange(after(down_piece, query), "mp")
    up_corner = second_swap(up_first, n_dp)
    up_mine = [up_shards, up_first, up_second]
    up_other = [core_swap(p, n_dp) for p in up_mine]
    held = attend(
        0, 2, query, key, value, segc, segr, hidden_in, full,
        vectors[5:6], vectors[1:2], vectors[2:3], (),
    )
    up_corner, down_got, up_other, *held = lax.optimization_barrier(
        (up_corner, down_got, up_other, *held)
    )
    up_pieces = up_mine + [up_corner] + up_other + [core_swap(up_corner, n_dp)]
    down_shards = others(down_got)
    down_first = first_swap(down_shards, n_dp)
    down_second = second_swap(down_shards, n_dp)
    context, saved, unit, low = attend(
        1, 2, query, key, value, segc, segr, hidden_in, full,
        vectors[5:6], vectors[1:2], vectors[2:3], held, down_shards,
    )
    down_first, down_second, low = lax.optimization_barrier((down_first, down_second, low))
    down_corner = second_swap(down_first, n_dp)
    down_mine = [down_shards, down_first, down_second]
    down_other = [core_swap(p, n_dp) for p in down_mine]
    act, slope, wu = feed_up(place, low, turned, up_bias, up_pieces, *down_mine[1:])
    down_corner, act = lax.optimization_barrier((down_corner, act))
    down_pieces = down_mine + [down_corner] + down_other + [core_swap(down_corner, n_dp)]
    layer_out, output, second_grad, down_grad, second_sums, wd = feed_down(
        place, act, unit, cotangent, w_down, vectors, down_pieces
    )

    feed_keep, feed_send, up_sums, normed = feed_back(
        place, down_grad, low, wu, wd, slope, act, n_mp
    )
    dims = (4, n_mp, 2 * sub, width)
    feed_keep = feed_keep.reshape(dims)
    got = core_swap(feed_send.reshape(dims), n_dp)
    first_grad, context_grad, inner, wo_grad, first_sums = middle(
        normed, second_grad, unit, saved, context, full, vectors[1:2]
    )
    got, context_grad = lax.optimization_barrier((got, context_grad))
    feed_stay, feed_go = chip_sum(feed_keep, got)
    got = first_swap(feed_go, n_dp)
    dq, dk, dv, head_sums = attend_back(
        place, query, key, value, context_grad, saved, inner, segc, segr, feed_go
    )
    got, head_sums = lax.optimization_barrier((got, head_sums))
    feed_own, feed_go = side_sum(feed_stay, got)
    got = second_swap(feed_go, n_dp)
    every = jnp.concatenate(
        [second_sums + first_sums + head_sums, up_sums], axis=1
    )
    vector_got = swap(every, "mp", 1, n_mp)
    heads_keep, heads_send = head_weights(
        place, dq, dk, dv, hidden_in, wo_grad, n_mp, every, feed_go
    )
    got, heads_keep = lax.optimization_barrier((got, heads_keep))
    feed_parts = add(feed_own, got)
    heads_got = core_swap(after(heads_send, got), n_dp)
    feed_got = exchange(feed_parts, "mp")
    heads_stay, heads_go = chip_sum(heads_keep, heads_got)
    heads_got = first_swap(heads_go, n_dp)
    every = every + after(vector_got, heads_go)
    vector_got = core_swap(every, n_dp)
    input_grad = input_gradient(dq, dk, dv, full, first_grad, heads_go, every)
    heads_got, vector_got, input_grad = lax.optimization_barrier(
        (heads_got, vector_got, input_grad)
    )
    heads_own, heads_go = side_sum(heads_stay, heads_got)
    heads_got = second_swap(heads_go, n_dp)
    every = every + after(vector_got, heads_go)
    bit = 2
    while bit < n_mp:
        vector_got = swap(every, "mp", bit, n_mp)
        bit *= 2
    heads_parts = add(heads_own, heads_got)
    feed_got, vector_got, heads_parts = lax.optimization_barrier(
        (feed_got, vector_got, heads_parts)
    )
    heads_got = exchange(heads_parts, "mp")
    every = every + after(vector_got, heads_parts)
    feed_got, every = lax.optimization_barrier((feed_got, every))
    feed_total = shard_sum(feed_got[0], [feed_got[r] for r in range(1, n_mp)], n_dp)
    feed_mine = [feed_total, first_swap(feed_total, n_dp), second_swap(feed_total, n_dp)]
    feed_mine.append(swap(feed_total, "dp", XBIT | YBIT, n_dp))
    vector_got = swap(every, "dp", XBIT, n_dp)
    scores = score(
        layer_out, segr, query_lengths.reshape(-1, 1), passages, passage_index, every
    )
    heads_got, vector_got, scores = lax.optimization_barrier((heads_got, vector_got, scores))
    every = every + vector_got
    vector_got = swap(every, "dp", YBIT, n_dp)
    heads_total = shard_sum(heads_got[0], [heads_got[r] for r in range(1, n_mp)], n_dp)
    heads_four = spread(heads_total, 4)
    heads_mine = plane_gather(heads_four, n_dp)
    feed_mine = lax.optimization_barrier((*feed_mine, heads_four))[:4]
    feed_other = [core_swap(p, n_dp) for p in feed_mine]
    every = every + after(vector_got, heads_four)
    bit = 8
    while bit < n_dp:
        every = every + swap(every, "dp", bit, n_dp)
        bit *= 2
    w_up_grad, w_down_grad = finish_feed(place, (*feed_mine, *feed_other), heads_four, every)
    heads_mine, w_up_grad = lax.optimization_barrier((heads_mine, w_up_grad))
    heads_other = core_swap(heads_mine, n_dp)
    query_t, key_t, value_t, w_output_grad = finish_heads(place, (heads_mine, heads_other))
    shared = every[:6, :width]
    query_sums, value_sums = (
        lax.dynamic_slice_in_dim(every[row, :width], shard * cut, cut) for row in (6, 7)
    )
    up_sums = lax.dynamic_slice_in_dim(every[:, width:], shard * 128, 128, axis=1)
    up_sums = up_sums[:, :sub].reshape(-1)
    return (
        output,
        scores,
        input_grad,
        query_t.T,
        key_t.T,
        value_t.T,
        w_output_grad,
        w_up_grad,
        w_down_grad,
        query_sums,
        value_sums,
        shared[0],
        up_sums,
        shared[3],
        shared[1],
        shared[2],
        shared[4],
        shared[5],
    )


def solution(mesh):
    both, split = P(("dp", "mp"), None), P(None, "mp")
    return jax.shard_map(
        functools.partial(per_device, mesh.shape["dp"], mesh.shape["mp"]),
        mesh=mesh,
        in_specs=(both, both, both, both, P())
        + (split, split, split, P("mp", None), split, P("mp", None))
        + (P("mp"), P("mp"), P(), P("mp"), P(), P(), P(), P(), P()),
        out_specs=(both, both, both)
        + (split, split, split, P("mp", None), split, P("mp", None))
        + (P("mp"), P("mp"), P(), P("mp"), P(), P(), P(), P(), P()),
        check_vma=False,
    )
```

```python
import functools

import jax
import jax.numpy as jnp
from jax import lax
from jax.experimental import pallas as pl
from jax.experimental.pallas import tpu as pltpu
from jax.sharding import PartitionSpec as P

HEAD_DIM = 64
SCALE = 0.125
EPSILON = 1e-12
MASKED = -1e30
BLOCK = 128
WINDOW = 384
GROUP = 4 * HEAD_DIM
ROW_BLOCK = 256
MIDDLE_BLOCK = 512
GRAIN = 16
MEBI = 1024 * 1024
NT = (((1,), (1,)), ((), ()))
TN = (((0,), (0,)), ((), ()))
BF = jnp.bfloat16
F32 = jnp.float32

CORE, XBIT, YBIT = 1, 2, 4


def params(mebi=60.5):
    return pltpu.CompilerParams(vmem_limit_bytes=int(mebi * MEBI))


def cost(us):
    return pl.CostEstimate(flops=int(us * 5e9), bytes_accessed=int(us * 15e6), transcendentals=0)


def shape(dims, dtype):
    return jax.ShapeDtypeStruct(dims, dtype)


def scalar_spec():
    return pl.BlockSpec(memory_space=pltpu.SMEM)


def held_spec():
    return pl.BlockSpec(memory_space=pltpu.VMEM)


def whole_spec(dims):
    return pl.BlockSpec(dims, lambda i: (0,) * len(dims), pipeline_mode=pl.Buffered(1))


def fixed_spec(dims):
    return pl.BlockSpec(dims, lambda i: (0,) * len(dims))


def rows_spec(rows, width):
    return pl.BlockSpec((rows, width), lambda i: (i, 0))


def token_spec():
    return pl.BlockSpec(memory_space=pl.ANY)


def swap(block, axis, bit, size):
    return lax.ppermute(block, axis, [(i, i ^ bit) for i in range(size)])


def after(value, *others):
    return lax.optimization_barrier((value, *others))[0]


def neighbour(core, g):
    if g in (0, 3):
        return g
    return g ^ (3 * core)


def piece_heads_kernel(place, wq, wk, wv, wo, piece, sems):
    core, plane = place[0], place[1]
    heads = piece.shape[0] // (2 * GRAIN)
    for side, pair in enumerate(((wq, wk), (wv, wo))):

        @pl.when(core == side)
        def _():
            copies = []
            for t, ref in enumerate(pair):
                for h in range(heads):
                    start = pl.multiple_of(h * HEAD_DIM + plane * GRAIN, GRAIN)
                    to = (t * heads + h) * GRAIN
                    copies.append(
                        pltpu.make_async_copy(
                            ref.at[pl.ds(start, GRAIN), :],
                            piece.at[to : to + GRAIN, :],
                            sems.at[t * heads + h],
                        )
                    )
            for copy in copies:
                copy.start()
            for copy in copies:
                copy.wait()


def piece_heads(place, *weights):
    local, width = weights[0].shape
    heads = local // HEAD_DIM
    return pl.pallas_call(
        piece_heads_kernel,
        in_specs=[scalar_spec()] + [token_spec()] * 4,
        out_specs=held_spec(),
        out_shape=shape((2 * heads * GRAIN, width), BF),
        scratch_shapes=[pltpu.SemaphoreType.DMA((2 * heads,))],
        compiler_params=params(),
        cost_estimate=cost(1),
        name="piece_heads",
    )(place, *weights)


def piece_feed_kernel(place, wu, wd, rest, turned, piece_up, piece_down):
    core, plane = place[0], place[1]
    sub = piece_down.shape[1]
    turned[...] = wu[...].astype(F32).T.astype(BF)
    start = pl.multiple_of((core * 4 + plane) * sub, GRAIN)
    for r in range(piece_up.shape[0]):
        piece_up[r, :sub, :] = turned[pl.ds(start, sub), :]
        piece_up[r, sub:, :] = rest[...]
        piece_down[r] = wd[pl.ds(start, sub), :]


def piece_feed(place, wu, wd, rest, n_mp):
    width, hidden = wu.shape
    sub = hidden // 8
    return pl.pallas_call(
        piece_feed_kernel,
        in_specs=[scalar_spec()] + [held_spec()] * 3,
        out_specs=[held_spec()] * 3,
        out_shape=[
            shape((hidden, width), BF),
            shape((n_mp, sub + GRAIN, width), BF),
            shape((n_mp, sub, width), BF),
        ],
        compiler_params=params(),
        cost_estimate=cost(3),
        name="piece_feed",
    )(place, wu, wd, rest)


def finish_feed_kernel(place, *refs):
    pieces, (up, down, held) = refs[:8], refs[-3:]
    core, plane = place[0], place[1]
    sub = pieces[0].shape[0] // 2
    for c in range(2):
        for g, ref in enumerate(pieces[4 * c : 4 * c + 4]):
            chip = plane ^ neighbour(core ^ c, g)
            start = pl.multiple_of(((core ^ c) * 4 + chip) * sub, GRAIN)
            held[pl.ds(start, sub), :] = ref[:sub, :].astype(F32)
            down[pl.ds(start, sub), :] = ref[sub:, :].astype(F32)
    up[...] = held[...].T


def finish_feed(place, pieces, *tokens):
    rows, width = pieces[0].shape
    return pl.pallas_call(
        finish_feed_kernel,
        in_specs=[scalar_spec()] + [held_spec()] * 8 + [token_spec() for _ in tokens],
        out_specs=[held_spec()] * 2,
        out_shape=[shape((width, 4 * rows), F32), shape((4 * rows, width), F32)],
        scratch_shapes=[pltpu.VMEM((4 * rows, width), F32)],
        compiler_params=params(),
        cost_estimate=cost(6),
        name="finish_feed",
    )(place, *pieces, *tokens)


def finish_heads_kernel(place, mine, other, *outs):
    core = place[0]
    heads = outs[0].shape[0] // HEAD_DIM
    for side in range(2):

        @pl.when(core == side)
        def _():
            for c, ref in enumerate((mine, other)):
                for t in range(2):
                    out = outs[2 * (side ^ c) + t]
                    for g in range(4):
                        for h in range(heads):
                            at = h * HEAD_DIM + g * GRAIN
                            row = (t * heads + h) * GRAIN
                            out[at : at + GRAIN, :] = ref[g, row : row + GRAIN, :].astype(F32)


def finish_heads(place, pieces):
    _, rows, width = pieces[0].shape
    local = rows // (2 * GRAIN) * HEAD_DIM
    return pl.pallas_call(
        finish_heads_kernel,
        in_specs=[scalar_spec()] + [held_spec()] * 2,
        out_specs=[held_spec()] * 4,
        out_shape=[shape((local, width), F32)] * 4,
        compiler_params=params(),
        cost_estimate=cost(2),
        name="finish_heads",
    )(place, *pieces)


def turn_swap(block, bits, n_dp):
    return lax.ppermute(block, "dp", [(i, i ^ bits[i & 1]) for i in range(n_dp)])


def first_swap(block, n_dp):
    return turn_swap(block, (XBIT, YBIT), n_dp)


def second_swap(block, n_dp):
    return turn_swap(block, (YBIT, XBIT), n_dp)


def core_swap(block, n_dp):
    return swap(block, "dp", CORE, n_dp)


def exchange(block, axis, groups=None):
    return lax.all_to_all(block, axis, 0, 0, axis_index_groups=groups, tiled=True)


def spread(block, n):
    return jnp.broadcast_to(block[None], (n, *block.shape))


def plane_groups(n_dp):
    return [[8 * e + 2 * g + c for g in range(4)] for e in range(n_dp // 8) for c in range(2)]


def add(*terms):
    total = terms[0].astype(F32)
    for term in terms[1:]:
        total = total + term.astype(F32)
    return total.astype(BF)


def chip_sum(keep, got):
    return add(keep[0::2], got[0::2]), add(keep[1::2], got[1::2])


def side_sum(stay, got):
    return add(stay[0], got[0]), add(stay[1], got[1])


def shard_sum(own, got, n_dp):
    total = own.astype(F32)
    for part in got:
        total = total + part.astype(F32)
    bit = 8
    while bit < n_dp:
        total = total + swap(total, "dp", bit, n_dp)
        bit *= 2
    return total.astype(BF)


def plane_gather(four, n_dp):
    return exchange(four, "dp", plane_groups(n_dp))


def project_kernel(place, x, wq, wk, wv, wo, bq, bv, *refs):
    pieces, (q, k, v, out, full, sems, sem) = refs[:8], refs[-7:]
    last = pltpu.make_async_copy(full, out, sem)
    core, plane, shard = place[0], place[1], place[2]
    heads = wq.shape[0] // HEAD_DIM
    shards = 1 + pieces[0].shape[0] // (2 * heads * GRAIN)

    @pl.when(pl.program_id(0) == 0)
    def _():
        copies = []
        base = pl.multiple_of(shard * heads * HEAD_DIM, HEAD_DIM)
        for kind, ref in enumerate((wq, wk, wv, wo)):
            for h in range(heads):
                for g in range(4):
                    source = plane ^ neighbour(kind // 2, g)
                    at = pl.multiple_of(h * HEAD_DIM + source * GRAIN, GRAIN)
                    to = pl.multiple_of(base + h * HEAD_DIM + g * GRAIN, GRAIN)
                    copies.append(
                        pltpu.make_async_copy(
                            ref.at[pl.ds(at, GRAIN), :],
                            full.at[kind, pl.ds(to, GRAIN), :],
                            sems.at[len(copies)],
                        )
                    )
        for copy in copies:
            copy.start()
        for c in range(2):
            for g, ref in enumerate(pieces[4 * c : 4 * c + 4]):
                for r in range(1, shards):
                    base = pl.multiple_of((shard ^ r) * heads * HEAD_DIM, HEAD_DIM)
                    for t in range(2):
                        for h in range(heads):
                            row = (((r - 1) * 2 + t) * heads + h) * GRAIN
                            to = pl.multiple_of(base + h * HEAD_DIM + g * GRAIN, GRAIN)
                            full[(core ^ c) * 2 + t, pl.ds(to, GRAIN), :] = ref[
                                row : row + GRAIN, :
                            ]
        for copy in copies:
            copy.wait()
        last.start()

    block = x[...]
    for kind, (into, bias) in enumerate(((q, bq), (k, None), (v, bv))):
        value = lax.dot_general(block, full[kind], NT, preferred_element_type=F32)
        if bias is not None:
            value = value + bias[...]
        into[...] = value.astype(BF)

    @pl.when(pl.program_id(0) == pl.num_programs(0) - 1)
    def _():
        last.wait()


def project(place, x, weights, bq, bv, pieces, *tokens):
    rows, width = x.shape
    block = rows_spec(ROW_BLOCK, width)
    return pl.pallas_call(
        project_kernel,
        grid=(rows // ROW_BLOCK,),
        in_specs=[scalar_spec(), block]
        + [token_spec()] * 4
        + [whole_spec(a.shape) for a in (bq, bv, *pieces)]
        + [token_spec() for _ in tokens],
        out_specs=[block, block, block, token_spec()],
        out_shape=[shape((rows, width), BF)] * 3 + [shape((4, width, width), BF)],
        scratch_shapes=[
            pltpu.VMEM((4, width, width), BF),
            pltpu.SemaphoreType.DMA((weights[0].shape[0] // GRAIN * 4,)),
            pltpu.SemaphoreType.DMA,
        ],
        compiler_params=params(),
        cost_estimate=cost(10),
        name="project",
    )(place, x, *weights, bq, bv, *pieces, *tokens)


def spread_heads(block):
    lane = lax.broadcasted_iota(jnp.int32, block.shape, 1) // HEAD_DIM
    return jnp.concatenate(
        [jnp.where(lane == h, block, jnp.zeros_like(block)) for h in range(4)], axis=0
    )


def gather_heads(stacked):
    rows = stacked.shape[0] // 4
    lane = lax.broadcasted_iota(jnp.int32, (rows, GROUP), 1) // HEAD_DIM
    out = stacked[:rows]
    for h in range(1, 4):
        out = jnp.where(lane == h, stacked[h * rows : (h + 1) * rows], out)
    return out


def window_start(step, rows):
    return pl.multiple_of(jnp.clip(step - 1, 0, (rows - WINDOW) // BLOCK) * BLOCK, BLOCK)


def attend_kernel(part, q, k, v, segc, segr, x, wo, bo, gain, shift, *refs):
    ctx, saved, unit, low = refs[-4:]
    start = window_start(part * pl.num_programs(0) + pl.program_id(0), k.shape[0])
    near = pl.ds(start, WINDOW)
    penalty = jnp.where(segc[...] == segr[:, near], 0.0, MASKED)
    lane = lax.broadcasted_iota(jnp.int32, (BLOCK, 128), 1)
    groups = q.shape[1] // GROUP

    def score_group(group):
        cols = slice(group * GROUP, (group + 1) * GROUP)
        return lax.dot_general(
            spread_heads(q[:, cols] * SCALE), k[near, cols], NT, preferred_element_type=F32
        )

    keep = jnp.zeros((BLOCK, 128), F32)
    ahead = score_group(0)
    for group in range(groups):
        cols = slice(group * GROUP, (group + 1) * GROUP)
        logits = ahead.reshape(4, BLOCK, WINDOW) + penalty[None]
        if group + 1 < groups:
            ahead = score_group(group + 1)
        peak = jnp.max(logits, axis=-1, keepdims=True)
        raised = jnp.exp(logits - peak)
        sums = jnp.sum(raised, axis=-1, keepdims=True)
        context = jnp.dot(
            raised.astype(BF).reshape(4 * BLOCK, WINDOW), v[near, cols], preferred_element_type=F32
        )
        context = (context.reshape(4, BLOCK, GROUP) * (1.0 / sums)).reshape(4 * BLOCK, GROUP)
        ctx[:, cols] = gather_heads(context).astype(BF)
        log_total = peak + jnp.log(sums)
        for h in range(4):
            keep = jnp.where(lane == group * 4 + h, log_total[h], keep)
    attended = jnp.dot(ctx[...], wo[0], preferred_element_type=F32) + bo[...]
    total = x[...].astype(F32) + attended
    centred = total - jnp.mean(total, axis=-1, keepdims=True)
    inv_std = lax.rsqrt(jnp.mean(centred * centred, axis=-1, keepdims=True) + EPSILON)
    unit_val = centred * inv_std
    unit[...] = unit_val
    low[...] = (unit_val * gain[...] + shift[...]).astype(BF)
    saved[...] = jnp.where(lane == 127, inv_std, keep)


def attend(part, parts, q, k, v, segc, segr, x, full, bo, gain, shift, held, *tokens):
    rows, width = q.shape
    steps = rows // BLOCK // parts

    def block(wide):
        return pl.BlockSpec((BLOCK, wide), lambda i: (part * steps + i, 0))

    return pl.pallas_call(
        functools.partial(attend_kernel, part),
        grid=(steps,),
        in_specs=[
            block(width),
            whole_spec((rows, width)),
            whole_spec((rows, width)),
            block(1),
            whole_spec((1, rows)),
            block(width),
            pl.BlockSpec((1, width, width), lambda i: (3, 0, 0), pipeline_mode=pl.Buffered(1)),
            whole_spec((1, width)),
            whole_spec((1, width)),
            whole_spec((1, width)),
        ]
        + [token_spec() for _ in (*held, *tokens)],
        out_specs=[block(width), block(128), block(width), block(width)],
        out_shape=[
            shape((rows, width), BF),
            shape((rows, 128), F32),
            shape((rows, width), F32),
            shape((rows, width), BF),
        ],
        input_output_aliases={10 + i: i for i in range(len(held))},
        compiler_params=params(),
        cost_estimate=cost(16 / parts),
        name="attend",
    )(q, k, v, segc, segr, x, full, bo, gain, shift, *held, *tokens)


def whole_order(rows, plane):
    width = rows.shape[1]
    rank = (lax.broadcasted_iota(jnp.int32, rows.shape, 1) // GRAIN) % 4
    row = lax.broadcasted_iota(jnp.int32, rows.shape, 0)

    def shifted(block, by):
        return pltpu.roll(block, by % width, 1)

    middle = jnp.where(rank == 1, shifted(rows, -GRAIN), shifted(rows, GRAIN))
    swapped = (row == 7) & ((rank == 1) | (rank == 2))
    rows = jnp.where(swapped, middle, rows)
    for bit in (1, 2):
        by = bit * GRAIN
        other = jnp.where((rank & bit) == 0, shifted(rows, -by), shifted(rows, by))
        rows = jnp.where((plane & bit) == 0, rows, other)
    return rows


def attend_back_kernel(place, q, k, v, do, saved, inner, segc, segr, *refs):
    dq, dk, dv, sums, dk_sum, dv_sum = refs[-6:]
    step = pl.program_id(0)

    @pl.when(step == 0)
    def _():
        dk_sum[...] = jnp.zeros_like(dk_sum)
        dv_sum[...] = jnp.zeros_like(dv_sum)
        sums[...] = jnp.zeros_like(sums)

    start = window_start(step, k.shape[0])
    near = pl.ds(start, WINDOW)
    penalty = jnp.where(segc[...] == segr[:, near], 0.0, MASKED)
    for group in range(q.shape[1] // GROUP):
        cols = slice(group * GROUP, (group + 1) * GROUP)
        q4 = spread_heads(q[:, cols] * SCALE)
        do4 = spread_heads(do[:, cols])
        k4 = k[near, cols]
        logits = lax.dot_general(q4, k4, NT, preferred_element_type=F32)
        logits = logits.reshape(4, BLOCK, WINDOW) + penalty[None]
        lse = jnp.stack([saved[:, group * 4 + h : group * 4 + h + 1] for h in range(4)])
        mean_grad = jnp.stack([inner[:, group * 4 + h : group * 4 + h + 1] for h in range(4)])
        probs = jnp.exp(logits - lse)
        weight_grad = lax.dot_general(
            do4, v[near, cols], NT, preferred_element_type=F32
        ).reshape(4, BLOCK, WINDOW)
        logit_grad = (probs * (weight_grad - mean_grad)).astype(BF).reshape(4 * BLOCK, WINDOW)
        probs_low = probs.astype(BF).reshape(4 * BLOCK, WINDOW)
        dq_low = (
            gather_heads(jnp.dot(logit_grad, k4, preferred_element_type=F32)) * SCALE
        ).astype(BF)
        dq[:, cols] = dq_low
        sums[6:7, cols] += jnp.sum(dq_low.astype(F32), axis=0, keepdims=True)
        dk_sum[near, cols] += lax.dot_general(logit_grad, q4, TN, preferred_element_type=F32)
        dv_sum[near, cols] += lax.dot_general(probs_low, do4, TN, preferred_element_type=F32)

    @pl.when(step == pl.num_programs(0) - 1)
    def _():
        dk[...] = dk_sum[...].astype(BF)
        dv_low = dv_sum[...].astype(BF)
        dv[...] = dv_low
        sums[7:8, :] = jnp.sum(dv_low.astype(F32), axis=0, keepdims=True)
        sums[...] = whole_order(sums[...], place[1])


def attend_back(place, q, k, v, do, saved, inner, segc, segr, *tokens):
    rows, width = q.shape
    block = rows_spec(BLOCK, width)
    full = whole_spec((rows, width))
    return pl.pallas_call(
        attend_back_kernel,
        grid=(rows // BLOCK,),
        in_specs=[
            scalar_spec(),
            block,
            full,
            full,
            block,
            rows_spec(BLOCK, 128),
            rows_spec(BLOCK, 128),
            rows_spec(BLOCK, 1),
            whole_spec((1, rows)),
        ]
        + [token_spec() for _ in tokens],
        out_specs=[block, fixed_spec((rows, width)), fixed_spec((rows, width)), fixed_spec((8, width))],
        out_shape=[shape((rows, width), BF)] * 3 + [shape((8, width), F32)],
        scratch_shapes=[pltpu.VMEM((rows, width), F32)] * 2,
        compiler_params=params(),
        cost_estimate=cost(22),
        name="attend_back",
    )(place, q, k, v, do, saved, inner, segc, segr, *tokens)


def assemble(place, own, pieces, into):
    core, plane, shard = place[0], place[1], place[2]
    sub = own.shape[0] // 8
    shards = 1 + pieces[0].shape[0] // sub

    def rows(c, g, r):
        return pl.ds(pl.multiple_of(((c * 4 + g) * shards + (shard ^ r)) * sub, GRAIN), sub)

    for c in range(2):
        for g, ref in enumerate(pieces[4 * c : 4 * c + 4]):
            at = pl.multiple_of(((core ^ c) * 4 + (plane ^ neighbour(core ^ c, g))) * sub, GRAIN)
            into[rows(c, g, 0), :] = own[pl.ds(at, sub), :]
            for r in range(1, shards):
                into[rows(c, g, r), :] = ref[(r - 1) * sub : r * sub, :]


def feed_up_kernel(place, x, own, bu, *refs):
    pieces, (act, slope, out, wu, sem) = refs[:8], refs[-5:]
    copy = pltpu.make_async_copy(wu, out, sem)

    @pl.when(pl.program_id(0) == 0)
    def _():
        assemble(place, own, pieces, wu)
        copy.start()

    block = x[...]
    for at in range(0, wu.shape[0], 256):
        span = slice(at, at + 256)
        pre = (
            lax.dot_general(block, wu[span, :], NT, preferred_element_type=F32) + bu[:, span]
        )
        below = 0.5 * (1.0 + lax.erf(pre * 0.7071067811865476))
        density = jnp.exp(-0.5 * pre * pre) * 0.3989422804014327
        act[:, span] = (pre * below).astype(BF)
        slope[:, span] = (below + pre * density).astype(BF)

    @pl.when(pl.program_id(0) == pl.num_programs(0) - 1)
    def _():
        copy.wait()


def feed_up(place, x, own, bu, pieces, *tokens):
    rows, width = x.shape
    hidden = bu.shape[1]
    wide = rows_spec(ROW_BLOCK, hidden)
    return pl.pallas_call(
        feed_up_kernel,
        grid=(rows // ROW_BLOCK,),
        in_specs=[scalar_spec(), rows_spec(ROW_BLOCK, width)]
        + [whole_spec(a.shape) for a in (own, bu, *pieces)]
        + [token_spec() for _ in tokens],
        out_specs=[wide, wide, token_spec()],
        out_shape=[shape((rows, hidden), BF)] * 2 + [shape((hidden, width), BF)],
        scratch_shapes=[pltpu.VMEM((hidden, width), BF), pltpu.SemaphoreType.DMA],
        compiler_params=params(),
        cost_estimate=cost(12),
        name="feed_up",
    )(place, x, own, bu, *pieces, *tokens)


def feed_down_kernel(place, act, unit, cot, own, vectors, *refs):
    pieces, outs = refs[:8], refs[-8:]
    layer, output, second, down_grad, sums, out, wd, sem = outs
    copy = pltpu.make_async_copy(wd, out, sem)

    @pl.when(pl.program_id(0) == 0)
    def _():
        sums[...] = jnp.zeros_like(sums)
        assemble(place, own, pieces, wd)
        copy.start()

    down = jnp.dot(act[...], wd[...], preferred_element_type=F32)
    b_down, first_gain, first_shift, second_gain, second_shift = (
        vectors[i : i + 1, :] for i in range(5)
    )
    total = unit[...] * first_gain + first_shift + down + b_down
    centred = total - jnp.mean(total, axis=-1, keepdims=True)
    inv_std = lax.rsqrt(jnp.mean(centred * centred, axis=-1, keepdims=True) + EPSILON)
    unit_val = centred * inv_std
    layer_out = unit_val * second_gain + second_shift
    layer[...] = layer_out
    output[...] = layer_out.astype(BF)
    grad = cot[...].astype(F32)
    scaled = grad * second_gain
    inner = (
        scaled
        - jnp.mean(scaled, axis=-1, keepdims=True)
        - unit_val * jnp.mean(scaled * unit_val, axis=-1, keepdims=True)
    )
    second_grad = inv_std * inner
    second[...] = second_grad
    grad_low = second_grad.astype(BF)
    down_grad[...] = grad_low
    sums[3:4, :] += jnp.sum(grad_low.astype(F32), axis=0, keepdims=True)
    sums[4:5, :] += jnp.sum(grad * unit_val, axis=0, keepdims=True)
    sums[5:6, :] += jnp.sum(grad, axis=0, keepdims=True)

    @pl.when(pl.program_id(0) == pl.num_programs(0) - 1)
    def _():
        copy.wait()


def feed_down(place, act, unit, cot, own, vectors, pieces):
    rows, hidden = act.shape
    width = unit.shape[1]
    block = rows_spec(ROW_BLOCK, width)
    return pl.pallas_call(
        feed_down_kernel,
        grid=(rows // ROW_BLOCK,),
        in_specs=[scalar_spec(), rows_spec(ROW_BLOCK, hidden), block, block]
        + [whole_spec(a.shape) for a in (own, vectors, *pieces)],
        out_specs=[block, block, block, block, fixed_spec((8, width)), token_spec()],
        out_shape=[
            shape((rows, width), F32),
            shape((rows, width), BF),
            shape((rows, width), F32),
            shape((rows, width), BF),
            shape((8, width), F32),
            shape((hidden, width), BF),
        ],
        scratch_shapes=[pltpu.VMEM((hidden, width), BF), pltpu.SemaphoreType.DMA],
        compiler_params=params(),
        cost_estimate=cost(13),
        name="feed_down",
    )(place, act, unit, cot, own, vectors, *pieces)


def feed_back_kernel(place, grad, x, wu, wd, slope, act, keep, send, bias, out, held):
    step = pl.program_id(0)
    half = pl.num_programs(0) // 2
    chips, shards, _, sub, width = keep.shape

    @pl.when(step == 0)
    def _():
        out[...] = jnp.zeros_like(out)
        bias[...] = jnp.zeros_like(bias)

    total = None
    for at in range(0, x.shape[0], ROW_BLOCK):
        span = slice(at, at + ROW_BLOCK)
        act_grad = lax.dot_general(grad[span, :], wd[...], NT, preferred_element_type=F32)
        low = (act_grad * slope[span, :].astype(F32)).astype(BF)
        held[span, :] = low
        term = jnp.sum(low.astype(F32), axis=0, keepdims=True)
        total = term if total is None else total + term
    core, plane = place[0], place[1]
    owner = jnp.where(step < half, core ^ 1, core)
    row = lax.broadcasted_iota(jnp.int32, (bias.shape[0], sub), 0)
    for g in range(chips):
        early = plane ^ jnp.where(owner == 0, neighbour(0, g), neighbour(1, g))
        late = plane ^ jnp.where(owner == 0, neighbour(0, 2 + g), neighbour(1, 2 + g))
        target = owner * 4 + jnp.where(lax.rem(step, half) == 0, early, late)
        for r in range(shards):
            at = (g * shards + r) * sub
            lanes = slice(r * 128, r * 128 + sub)
            bias[:, lanes] = jnp.where(row == target, total[:, at : at + sub], bias[:, lanes])
    out[...] += jnp.dot(held[...], wu[...], preferred_element_type=F32)
    dims = (chips, shards, sub, width)
    up = lax.dot_general(held[...], x[...], TN, preferred_element_type=F32).astype(BF)
    down = lax.dot_general(act[...], grad[...], TN, preferred_element_type=F32).astype(BF)

    @pl.when(step < half)
    def _():
        send[:, :, 0] = up.reshape(dims)
        send[:, :, 1] = down.reshape(dims)

    @pl.when(step >= half)
    def _():
        keep[:, :, 0] = up.reshape(dims)
        keep[:, :, 1] = down.reshape(dims)


def feed_back(place, grad, x, wu, wd, slope, act, n_mp):
    rows, width = x.shape
    hidden = wu.shape[0]
    span = hidden // 4
    full = whole_spec((rows, width))
    weight = pl.BlockSpec((span, width), lambda j: ((j + 2) % 4, 0))
    wide = pl.BlockSpec((rows, span), lambda j: (0, (j + 2) % 4))
    dims = (4, n_mp, 2, hidden // 8 // n_mp, width)
    block = (2, *dims[1:])
    return pl.pallas_call(
        feed_back_kernel,
        grid=(4,),
        in_specs=[scalar_spec(), full, full, weight, weight, wide, wide],
        out_specs=[
            pl.BlockSpec(block, lambda j: (jnp.maximum(j - 2, 0), 0, 0, 0, 0)),
            pl.BlockSpec(block, lambda j: (jnp.minimum(j, 1), 0, 0, 0, 0)),
            fixed_spec((8, 128 * n_mp)),
            fixed_spec((rows, width)),
        ],
        out_shape=[
            shape(dims, BF),
            shape(dims, BF),
            shape((8, 128 * n_mp), F32),
            shape((rows, width), F32),
        ],
        scratch_shapes=[pltpu.VMEM((rows, span), BF)],
        compiler_params=params(),
        cost_estimate=cost(27),
        name="feed_back",
    )(place, grad, x, wu, wd, slope, act)


def middle_kernel(normed, second, unit, saved, ctx, wo, gain, *refs):
    first, context_grad, inner_sum, weight, sums, held, lows = refs[-7:]
    step = pl.program_id(0)
    grad = normed[...] + second[...]
    unit_val = unit[...]
    scaled = grad * gain[...]
    inner = (
        scaled
        - jnp.mean(scaled, axis=-1, keepdims=True)
        - unit_val * jnp.mean(scaled * unit_val, axis=-1, keepdims=True)
    )
    first_grad = saved[:, 127:128] * inner
    first[...] = first_grad
    low = first_grad.astype(BF)
    context_low = lax.dot_general(low, wo[0], NT, preferred_element_type=F32).astype(BF)
    context_grad[...] = context_low
    product = context_low.astype(F32) * ctx[...].astype(F32)
    high = product.astype(BF)
    rest = (product - high.astype(F32)).astype(BF)
    width = product.shape[1]
    head = lax.broadcasted_iota(jnp.int32, (width, 128), 0) // HEAD_DIM
    head = (head == lax.broadcasted_iota(jnp.int32, (width, 128), 1)).astype(BF)
    inner_sum[...] = jnp.dot(high, head, preferred_element_type=F32) + jnp.dot(
        rest, head, preferred_element_type=F32
    )
    at = pl.ds(pl.multiple_of(step * MIDDLE_BLOCK, MIDDLE_BLOCK), MIDDLE_BLOCK)
    lows[at, :] = low
    held[at, :] = ctx[...]

    @pl.when(step == 0)
    def _():
        sums[...] = jnp.zeros_like(sums)

    sums[0:1, :] += jnp.sum(low.astype(F32), axis=0, keepdims=True)
    sums[1:2, :] += jnp.sum(grad * unit_val, axis=0, keepdims=True)
    sums[2:3, :] += jnp.sum(grad, axis=0, keepdims=True)

    @pl.when(step == pl.num_programs(0) - 1)
    def _():
        weight[...] = lax.dot_general(
            held[...], lows[...], TN, preferred_element_type=F32
        ).astype(BF)


def middle(normed, second, unit, saved, ctx, full, gain, *tokens):
    rows, width = normed.shape
    block = rows_spec(MIDDLE_BLOCK, width)
    return pl.pallas_call(
        middle_kernel,
        grid=(rows // MIDDLE_BLOCK,),
        in_specs=[
            block,
            block,
            block,
            rows_spec(MIDDLE_BLOCK, 128),
            block,
            pl.BlockSpec((1, width, width), lambda i: (3, 0, 0), pipeline_mode=pl.Buffered(1)),
            whole_spec((1, width)),
        ]
        + [token_spec() for _ in tokens],
        out_specs=[block, block, rows_spec(MIDDLE_BLOCK, 128), fixed_spec((width, width)), fixed_spec((8, width))],
        out_shape=[
            shape((rows, width), F32),
            shape((rows, width), BF),
            shape((rows, 128), F32),
            shape((width, width), BF),
            shape((8, width), F32),
        ],
        scratch_shapes=[pltpu.VMEM((rows, width), BF)] * 2,
        compiler_params=params(),
        cost_estimate=cost(8),
        name="middle",
    )(normed, second, unit, saved, ctx, full, gain, *tokens)


def head_weights_kernel(place, dq, dk, dv, x, wo, *refs):
    keep, send, pairs, loaded, held, sems, out_sems = refs[-7:]
    core = place[0]
    shards, heads = keep.shape[1], keep.shape[3]
    width = x.shape[1]
    copies = [
        pltpu.make_async_copy(ref, loaded.at[n], sems.at[n])
        for n, ref in enumerate((dq, dk, dv, x))
    ] + [pltpu.make_async_copy(wo, loaded.at[4, :width, :], sems.at[4])]
    for n in (3, 0, 1, 2, 4):
        copies[n].start()
    copies[3].wait()

    def out_copy(pair, side):
        return pltpu.make_async_copy(
            pairs.at[pair], keep if side == pair else send, out_sems.at[pair]
        )

    for kind in range(4):
        if kind < 3:
            copies[kind].wait()
            held[...] = lax.dot_general(
                loaded[kind], loaded[3], TN, preferred_element_type=F32
            ).astype(BF)
        else:
            copies[4].wait()
        for r in range(shards):
            for h in range(heads):
                for g in range(4):
                    at = (r * heads + h) * HEAD_DIM + g * GRAIN
                    rows = slice(at, at + GRAIN)
                    value = held[rows, :] if kind < 3 else loaded[4, rows, :]
                    pairs[kind // 2, g, r, kind % 2, h] = value
        for side in range(2):
            if kind % 2 == 1:

                @pl.when(core == side)
                def _():
                    out_copy(kind // 2, side).start()

    for side in range(2):

        @pl.when(core == side)
        def _():
            for pair in range(2):
                out_copy(pair, side).wait()


def head_weights(place, dq, dk, dv, x, wo, n_mp, *tokens):
    rows, width = x.shape
    heads = width // HEAD_DIM // n_mp
    dims = (4, n_mp, 2, heads, GRAIN, width)
    keep, send = pl.pallas_call(
        head_weights_kernel,
        in_specs=[scalar_spec()] + [token_spec()] * 5 + [token_spec() for _ in tokens],
        out_specs=[token_spec()] * 2,
        out_shape=[shape(dims, BF)] * 2,
        scratch_shapes=[
            pltpu.VMEM((2, *dims), BF),
            pltpu.VMEM((5, rows, width), BF),
            pltpu.VMEM((width, width), BF),
            pltpu.SemaphoreType.DMA((5,)),
            pltpu.SemaphoreType.DMA((2,)),
        ],
        compiler_params=params(),
        cost_estimate=cost(9),
        name="head_weights",
    )(place, dq, dk, dv, x, wo, *tokens)
    dims = (4, n_mp, 2 * heads * GRAIN, width)
    return keep.reshape(dims), send.reshape(dims)


def input_kernel(dq, dk, dv, full, first, *refs):
    out = refs[-1]
    total = first[...]
    for kind, ref in enumerate((dq, dk, dv)):
        total = total + jnp.dot(ref[...], full[kind], preferred_element_type=F32)
    out[...] = total


def input_gradient(dq, dk, dv, full, first, *tokens):
    rows, width = dq.shape
    block = rows_spec(ROW_BLOCK, width)
    return pl.pallas_call(
        input_kernel,
        grid=(rows // ROW_BLOCK,),
        in_specs=[
            block,
            block,
            block,
            pl.BlockSpec((3, width, width), lambda i: (0, 0, 0), pipeline_mode=pl.Buffered(1)),
            block,
        ]
        + [token_spec() for _ in tokens],
        out_specs=block,
        out_shape=shape((rows, width), F32),
        compiler_params=params(),
        cost_estimate=cost(6),
        name="input_gradient",
    )(dq, dk, dv, full, first, *tokens)


def score_kernel(out_ref, segr_ref, len_ref, table_ref, pick_ref, *refs):
    score_ref = refs[-1]
    queries = pick_ref.shape[0]
    rows = out_ref.shape[0]
    label = lax.broadcasted_iota(jnp.int32, (queries, rows), 0)
    onehot = (label == segr_ref[...]).astype(F32)
    sums = jnp.dot(
        onehot, out_ref[...], precision=lax.Precision.HIGHEST, preferred_element_type=F32
    )
    means = sums / len_ref[...].astype(F32)
    every = lax.dot_general(
        means,
        table_ref[...].astype(F32),
        NT,
        precision=lax.Precision.HIGHEST,
        preferred_element_type=F32,
    )
    at = lax.broadcasted_iota(jnp.int32, every.shape, 1)
    column = lax.broadcasted_iota(jnp.int32, pick_ref.shape, 1)
    result = jnp.zeros(pick_ref.shape, F32)
    for p in range(pick_ref.shape[1]):
        chosen = jnp.sum(
            jnp.where(at == pick_ref[:, p : p + 1], every, 0.0), axis=1, keepdims=True
        )
        result = jnp.where(column == p, chosen, result)
    score_ref[...] = result


def score(layer_out, segr, lengths, table, picks, *tokens):
    return pl.pallas_call(
        score_kernel,
        in_specs=[held_spec()] * 5 + [token_spec() for _ in tokens],
        out_specs=held_spec(),
        out_shape=shape(picks.shape, F32),
        compiler_params=params(),
        cost_estimate=cost(8),
        name="score",
    )(layer_out, segr, lengths, table, picks, *tokens)


def per_device(
    n_dp,
    n_mp,
    hidden_in,
    cotangent,
    query_lengths,
    passage_index,
    passages,
    w_query,
    w_key,
    w_value,
    w_output,
    w_up,
    w_down,
    b_query,
    b_value,
    b_output,
    b_up,
    b_down,
    first_gain,
    first_shift,
    second_gain,
    second_shift,
):
    rows, width = hidden_in.shape
    heads = w_query.shape[1] // HEAD_DIM
    sub = w_up.shape[1] // 8
    at_dp = lax.axis_index("dp")
    core, plane = at_dp & 1, (at_dp >> 1) & 3
    shard = lax.axis_index("mp")
    place = jnp.stack([core, plane, shard]).astype(jnp.int32)
    own_heads = (w_query.T, w_key.T, w_value.T, w_output)

    cut = heads * HEAD_DIM
    heads_piece = piece_heads(place, *own_heads)
    bias_rows = jnp.stack(
        [jnp.pad(b_query, (0, width - cut)), jnp.pad(b_value, (0, width - cut)), b_up]
    )
    rest = jnp.pad(after(bias_rows, heads_piece), ((0, GRAIN - 3), (0, 0)))
    turned, up_piece, down_piece = piece_feed(place, w_up, w_down, rest, n_mp)
    heads_parts = [swap(after(heads_piece, rest), "mp", 1, n_mp)] + [
        swap(heads_piece, "mp", r, n_mp) for r in range(2, n_mp)
    ]
    up_got = exchange(up_piece, "mp")
    heads_shards = jnp.concatenate(heads_parts)
    heads_first = first_swap(heads_shards, n_dp)
    heads_second = second_swap(heads_shards, n_dp)
    heads_corner = second_swap(after(heads_first, heads_second), n_dp)
    heads_other = [core_swap(p, n_dp) for p in (heads_shards, heads_first, heads_second)]
    heads_corner, up_got = lax.optimization_barrier((heads_corner, up_got))
    heads_mine = [heads_shards, heads_first, heads_second, heads_corner]
    heads_other = heads_other + [core_swap(heads_corner, n_dp)]

    def others(got):
        return jnp.concatenate(
            [
                lax.dynamic_index_in_dim(got, shard ^ r, 0, keepdims=False)[:sub]
                for r in range(1, n_mp)
            ]
        )

    up_shards = others(after(up_got, *heads_mine, *heads_other))
    up_first = first_swap(up_shards, n_dp)
    up_second = second_swap(up_shards, n_dp)

    ranks = lax.broadcasted_iota(jnp.int32, (4, 4), 0)
    places4 = lax.broadcasted_iota(jnp.int32, (4, 4), 1)
    turned_ranks = jnp.where((ranks == 1) | (ranks == 2), ranks ^ 3, ranks)
    order_q = ((plane ^ ranks) == places4).astype(F32)
    order_v = ((plane ^ turned_ranks) == places4).astype(F32)
    owner = (core ^ jnp.arange(2, dtype=jnp.int32)).reshape(2, 1, 1, 1)
    is_owner = (owner == jnp.arange(2, dtype=jnp.int32).reshape(1, 1, 2, 1)).astype(F32)
    order_up = jnp.where(owner == 0, order_q[None, :, None], order_v[None, :, None])
    order_up = (order_up * is_owner).reshape(8, 8)
    exact = functools.partial(
        jnp.einsum, precision=lax.Precision.HIGHEST, preferred_element_type=F32
    )
    all_bias = up_got[:, sub : sub + 3].astype(F32)
    by_head = (n_mp, heads, 4, GRAIN)
    query_bias = exact("gk,zhki->zhgi", order_q, all_bias[:, 0, :cut].reshape(by_head))
    value_bias = exact("gk,zhki->zhgi", order_v, all_bias[:, 1, :cut].reshape(by_head))
    up_bias = exact("gk,zki->gzi", order_up, all_bias[:, 2].reshape(n_mp, 8, sub))
    query_bias, value_bias, up_bias = (
        b.reshape(1, -1) for b in (query_bias, value_bias, up_bias)
    )

    ends = jnp.cumsum(query_lengths, axis=-1, dtype=jnp.int32)
    places = lax.broadcasted_iota(jnp.int32, (rows, query_lengths.shape[1]), 0)
    seg = jnp.sum((places >= ends).astype(jnp.int32), axis=-1)
    segc, segr = seg.reshape(rows, 1), seg.reshape(1, rows)
    vectors = jnp.stack(
        [b_down, first_gain, first_shift, second_gain, second_shift, b_output, b_output, b_output]
    ).astype(F32)

    query, key, value, full = project(
        place, hidden_in, own_heads, query_bias, value_bias, heads_mine + heads_other
    )
    up_first, up_second, query = lax.optimization_barrier((up_first, up_second, query))
    down_got = exchange(after(down_piece, query), "mp")
    up_corner = second_swap(up_first, n_dp)
    up_mine = [up_shards, up_first, up_second]
    up_other = [core_swap(p, n_dp) for p in up_mine]
    held = attend(
        0, 2, query, key, value, segc, segr, hidden_in, full,
        vectors[5:6], vectors[1:2], vectors[2:3], (),
    )
    up_corner, down_got, up_other, *held = lax.optimization_barrier(
        (up_corner, down_got, up_other, *held)
    )
    up_pieces = up_mine + [up_corner] + up_other + [core_swap(up_corner, n_dp)]
    down_shards = others(down_got)
    down_first = first_swap(down_shards, n_dp)
    down_second = second_swap(down_shards, n_dp)
    context, saved, unit, low = attend(
        1, 2, query, key, value, segc, segr, hidden_in, full,
        vectors[5:6], vectors[1:2], vectors[2:3], held, down_shards,
    )
    down_first, down_second, low = lax.optimization_barrier((down_first, down_second, low))
    down_corner = second_swap(down_first, n_dp)
    down_mine = [down_shards, down_first, down_second]
    down_other = [core_swap(p, n_dp) for p in down_mine]
    act, slope, wu = feed_up(place, low, turned, up_bias, up_pieces, *down_mine[1:])
    down_corner, act = lax.optimization_barrier((down_corner, act))
    down_pieces = down_mine + [down_corner] + down_other + [core_swap(down_corner, n_dp)]
    layer_out, output, second_grad, down_grad, second_sums, wd = feed_down(
        place, act, unit, cotangent, w_down, vectors, down_pieces
    )

    feed_keep, feed_send, up_sums, normed = feed_back(
        place, down_grad, low, wu, wd, slope, act, n_mp
    )
    dims = (4, n_mp, 2 * sub, width)
    feed_keep = feed_keep.reshape(dims)
    got = core_swap(feed_send.reshape(dims), n_dp)
    first_grad, context_grad, inner, wo_grad, first_sums = middle(
        normed, second_grad, unit, saved, context, full, vectors[1:2]
    )
    got, context_grad = lax.optimization_barrier((got, context_grad))
    feed_stay, feed_go = chip_sum(feed_keep, got)
    got = first_swap(feed_go, n_dp)
    dq, dk, dv, head_sums = attend_back(
        place, query, key, value, context_grad, saved, inner, segc, segr, feed_go
    )
    got, head_sums = lax.optimization_barrier((got, head_sums))
    feed_own, feed_go = side_sum(feed_stay, got)
    got = second_swap(feed_go, n_dp)
    every = jnp.concatenate(
        [second_sums + first_sums + head_sums, up_sums], axis=1
    )
    vector_got = swap(every, "mp", 1, n_mp)
    heads_keep, heads_send = head_weights(
        place, dq, dk, dv, hidden_in, wo_grad, n_mp, every, feed_go
    )
    got, heads_keep = lax.optimization_barrier((got, heads_keep))
    feed_parts = add(feed_own, got)
    heads_got = core_swap(after(heads_send, got), n_dp)
    feed_got = exchange(feed_parts, "mp")
    heads_stay, heads_go = chip_sum(heads_keep, heads_got)
    heads_got = first_swap(heads_go, n_dp)
    every = every + after(vector_got, heads_go)
    vector_got = core_swap(every, n_dp)
    input_grad = input_gradient(dq, dk, dv, full, first_grad, heads_go, every)
    heads_got, vector_got, input_grad = lax.optimization_barrier(
        (heads_got, vector_got, input_grad)
    )
    heads_own, heads_go = side_sum(heads_stay, heads_got)
    heads_got = second_swap(heads_go, n_dp)
    every = every + after(vector_got, heads_go)
    bit = 2
    while bit < n_mp:
        vector_got = swap(every, "mp", bit, n_mp)
        bit *= 2
    heads_parts = add(heads_own, heads_got)
    feed_got, vector_got, heads_parts = lax.optimization_barrier(
        (feed_got, vector_got, heads_parts)
    )
    heads_got = exchange(heads_parts, "mp")
    every = every + after(vector_got, heads_parts)
    feed_got, every = lax.optimization_barrier((feed_got, every))
    feed_total = shard_sum(feed_got[0], [feed_got[r] for r in range(1, n_mp)], n_dp)
    feed_mine = [feed_total, first_swap(feed_total, n_dp), second_swap(feed_total, n_dp)]
    feed_mine.append(swap(feed_total, "dp", XBIT | YBIT, n_dp))
    vector_got = swap(every, "dp", XBIT, n_dp)
    scores = score(
        layer_out, segr, query_lengths.reshape(-1, 1), passages, passage_index, every
    )
    heads_got, vector_got, scores = lax.optimization_barrier((heads_got, vector_got, scores))
    every = every + vector_got
    vector_got = swap(every, "dp", YBIT, n_dp)
    heads_total = shard_sum(heads_got[0], [heads_got[r] for r in range(1, n_mp)], n_dp)
    heads_four = spread(heads_total, 4)
    heads_mine = plane_gather(heads_four, n_dp)
    feed_mine = lax.optimization_barrier((*feed_mine, heads_four))[:4]
    feed_other = [core_swap(p, n_dp) for p in feed_mine]
    every = every + after(vector_got, heads_four)
    bit = 8
    while bit < n_dp:
        every = every + swap(every, "dp", bit, n_dp)
        bit *= 2
    w_up_grad, w_down_grad = finish_feed(place, (*feed_mine, *feed_other), heads_four, every)
    heads_mine, w_up_grad = lax.optimization_barrier((heads_mine, w_up_grad))
    heads_other = core_swap(heads_mine, n_dp)
    query_t, key_t, value_t, w_output_grad = finish_heads(place, (heads_mine, heads_other))
    shared = every[:6, :width]
    query_sums, value_sums = (
        lax.dynamic_slice_in_dim(every[row, :width], shard * cut, cut) for row in (6, 7)
    )
    up_sums = lax.dynamic_slice_in_dim(every[:, width:], shard * 128, 128, axis=1)
    up_sums = up_sums[:, :sub].reshape(-1)
    return (
        output,
        scores,
        input_grad,
        query_t.T,
        key_t.T,
        value_t.T,
        w_output_grad,
        w_up_grad,
        w_down_grad,
        query_sums,
        value_sums,
        shared[0],
        up_sums,
        shared[3],
        shared[1],
        shared[2],
        shared[4],
        shared[5],
    )


def solution(mesh):
    both, split = P(("dp", "mp"), None), P(None, "mp")
    return jax.shard_map(
        functools.partial(per_device, mesh.shape["dp"], mesh.shape["mp"]),
        mesh=mesh,
        in_specs=(both, both, both, both, P())
        + (split, split, split, P("mp", None), split, P("mp", None))
        + (P("mp"), P("mp"), P(), P("mp"), P(), P(), P(), P(), P()),
        out_specs=(both, both, both)
        + (split, split, split, P("mp", None), split, P("mp", None))
        + (P("mp"), P("mp"), P(), P("mp"), P(), P(), P(), P(), P()),
        check_vma=False,
    )
```
